128 devices in a mesh: obj: 4 (over y), pat: 32 (over z, x, core).
Axes of the slice: x: 4, y: 4, z: 4, core: 2. Of those that a mesh axis runs over, the one named last changes fastest.
Arguments:
- obj: bfloat16 [2, 768, 4096], P(None, 'pat', 'obj'), may hold values from -6 to 6
- probe: float32 [2, 512, 512], replicated, may hold values from -6 to 6
- amps: float32 [384, 512, 512], P(('obj', 'pat')), may hold values from 0.2 to 3
- rows: int32 [384], P(('obj', 'pat')), may hold values from 0 to 256
- cols: int32 [384], P(('obj', 'pat')), may hold values from 0 to 768
Outputs:
- obj_step: float32 [2, 768, 4096], P(None, 'pat', 'obj')
- probe_grad: float32 [2, 512, 512], replicated
The draws below stay inside these ranges and needn't reach their ends.
All inputs are finite; a program needn't handle non-finite values.
Results may differ from the reference program's by a relative error of at most 0.0041.
Values may be sent and summed in bfloat16 or wider, within the bound.
A program may use at most 192 MiB of HBM per device.

```python
import math
import jax
import jax.numpy as jnp
from jax import lax

PX = 512
H = 768
TW = 1024
HALO = 256
PPD = 3
W = 4096
NPAT = 384
N_PAT = 32


def place_ends(drawn, own_key, least, top_value):
    longest = drawn.shape.index(max(drawn.shape))
    spots = []
    for shift in (0, 1):
        where = [jax.random.randint(jax.random.fold_in(own_key, axis), (), 0, length) for axis, length in enumerate(drawn.shape)]
        where[longest] = (where[longest] + shift) % drawn.shape[longest]
        spots.append(tuple(where))
    return drawn.at[spots[0]].set(least).at[spots[1]].set(top_value)


def steps_of(own_key, dims, cuts, low, top_value):
    level = 1.0
    for axis_at, blocks in cuts:
        draws = jax.random.uniform(jax.random.fold_in(jax.random.fold_in(own_key, 6), axis_at), (blocks,), jnp.float32, low / len(cuts), top_value / len(cuts))
        level = level * jnp.repeat(jnp.exp(draws), dims[axis_at] // blocks).reshape((-1,) + (1,) * (len(dims) - 1 - axis_at))
    return level


def normal_values(rng, dims, scale, bound, pieces=(), kind=jnp.bfloat16):
    array = scale * jax.random.normal(rng, dims, jnp.float32)
    if pieces:
        array = array * steps_of(rng, dims, pieces, -0.22, 0.18)
    return jnp.clip(array, -bound, bound).astype(kind)


def setup_inputs(seed: int = 0) -> dict:
    seeds = jax.random.split(jax.random.key(seed), 6)
    obj = normal_values(seeds[0], (2, H, W), 1.0, 6.0, ((1, 32), (2, 4)))
    probe = normal_values(seeds[1], (2, PX, PX), 1.0, 6.0, (), jnp.float32)
    amps = jnp.clip(jnp.exp(math.log(3.0) - 2.7080502 * jax.random.uniform(seeds[2], (NPAT, PX, PX), jnp.float32) ** steps_of(seeds[2], (NPAT, PX, PX), ((0, 128),), -0.2, 0.2)), 0.2, 3.0)
    rows = place_ends(jax.random.randint(seeds[3], (NPAT,), 0, H - PX + 1), jax.random.fold_in(seeds[3], 1), 0, H - PX).astype(jnp.int32)
    cols = place_ends(jax.random.randint(seeds[4], (NPAT,), 0, TW - PX + HALO + 1), jax.random.fold_in(seeds[4], 1), 0, TW - PX + HALO).astype(jnp.int32)
    return dict(obj=obj, probe=probe, amps=amps, rows=rows, cols=cols)


def dft_table(order):
    index = jnp.arange(order, dtype=jnp.int32)
    phase = index[:, None] * index[None, :] % order
    angle = phase.astype(jnp.float32) * (2.0 * math.pi / order)
    scale = 1.0 / math.sqrt(order)
    return ((jnp.cos(angle) * scale).astype(jnp.bfloat16), (-jnp.sin(angle) * scale).astype(jnp.bfloat16))

def matmul(left, right):
    return jnp.dot(left, right, preferred_element_type=jnp.float32)

def complex_dot(left_re, left_im, right_re, right_im):
    real = matmul(left_re, right_re) - matmul(left_im, right_im)
    imag = matmul(left_re, right_im) + matmul(left_im, right_re)
    return (real, imag)

def project(patch_re, patch_im, probe_re, probe_im, amp, tab_re, tab_im):
    exit_re = (probe_re * patch_re - probe_im * patch_im).astype(jnp.bfloat16)
    exit_im = (probe_re * patch_im + probe_im * patch_re).astype(jnp.bfloat16)
    half_re, half_im = complex_dot(tab_re, tab_im, exit_re, exit_im)
    half_re = half_re.astype(jnp.bfloat16)
    half_im = half_im.astype(jnp.bfloat16)
    wave_re, wave_im = complex_dot(half_re, half_im, tab_re, tab_im)
    ratio = amp / jnp.sqrt(wave_re * wave_re + wave_im * wave_im + 1.0)
    diff_re = (wave_re * ratio - wave_re).astype(jnp.bfloat16)
    diff_im = (wave_im * ratio - wave_im).astype(jnp.bfloat16)
    conj_im = -tab_im
    back_re, back_im = complex_dot(tab_re, conj_im, diff_re, diff_im)
    back_re = back_re.astype(jnp.bfloat16)
    back_im = back_im.astype(jnp.bfloat16)
    delta_re, delta_im = complex_dot(back_re, back_im, tab_re, conj_im)
    gobj_re = probe_re * delta_re + probe_im * delta_im
    gobj_im = probe_re * delta_im - probe_im * delta_re
    gprobe_re = patch_re * delta_re + patch_im * delta_im
    gprobe_im = patch_re * delta_im - patch_im * delta_re
    return (gobj_re, gobj_im, gprobe_re, gprobe_im)

def reference(obj, probe, amps, rows, cols):
    width = obj.shape[2]
    group = PPD * N_PAT
    padded = jnp.pad(obj, ((0, 0), (0, 0), (0, HALO)))
    tab_re, tab_im = dft_table(PX)
    probe_re, probe_im = (probe[0], probe[1])
    light_patch = probe_re * probe_re + probe_im * probe_im
    index = jnp.arange(NPAT, dtype=jnp.int32)
    starts = (index // group * TW + cols).astype(jnp.int32)
    zero = jnp.zeros((), jnp.int32)

    def step(carry, item):
        grad, light, acc_re, acc_im = carry
        amp, row, start = item
        patch = lax.dynamic_slice(padded, (zero, row, start), (2, PX, PX)).astype(jnp.float32)
        gobj_re, gobj_im, gprobe_re, gprobe_im = project(patch[0], patch[1], probe_re, probe_im, amp, tab_re, tab_im)
        current = lax.dynamic_slice(grad, (zero, row, start), (2, PX, PX))
        grad = lax.dynamic_update_slice(grad, current + jnp.stack([gobj_re, gobj_im]), (zero, row, start))
        lit = lax.dynamic_slice(light, (row, start), (PX, PX))
        light = lax.dynamic_update_slice(light, lit + light_patch, (row, start))
        return ((grad, light, acc_re + gprobe_re, acc_im + gprobe_im), None)
    init = (jnp.zeros((2, H, width + HALO), jnp.float32), jnp.zeros((H, width + HALO), jnp.float32), jnp.zeros((PX, PX), jnp.float32), jnp.zeros((PX, PX), jnp.float32))
    carry, _ = lax.scan(step, init, (amps, rows.astype(jnp.int32), starts))
    grad = carry[0][:, :, :width]
    light = carry[1][:, :width]
    obj_step = grad / (light + 1.0)
    probe_grad = jnp.stack([carry[2], carry[3]]) * (1.0 / math.sqrt(NPAT))
    return (obj_step, probe_grad)
```

```python
import functools
import math

import jax
import jax.numpy as jnp
import ml_dtypes
import numpy as np
from jax import lax
from jax.experimental import pallas as pl
from jax.experimental.pallas import tpu as pltpu
from jax.sharding import PartitionSpec as P

PX = 512
HALO = 256
H = 768
TW = 1024
WIDE = TW + HALO
OWN = 24
BF = jnp.bfloat16
F32 = jnp.float32
MESH = pl.DeviceIdType.MESH
DIMS = ("xa", "za", "xb", "zb")
MB = 1 << 20


def bits_of(pat):
    x, z = (pat // 2) % 4, pat // 8
    return {
        "core": pat % 2,
        "xa": (x // 2 + x) % 2,
        "xb": x // 2,
        "za": (z // 2 + z) % 2,
        "zb": z // 2,
    }


def partner_of(pat, dim):
    core, x, z = pat % 2, (pat // 2) % 4, pat // 8
    if dim == "core":
        core = 1 - core
    elif dim == "xa":
        x = x + 1 - 2 * (x % 2)
    elif dim == "xb":
        x = 3 - x
    elif dim == "za":
        z = z + 1 - 2 * (z % 2)
    else:
        z = 3 - z
    return (z * 4 + x) * 2 + core


def order(part):
    return [DIMS[(part + k) % 4] for k in range(4)]


def gather_place(pat, part):
    bits = bits_of(pat)
    return bits["core"] * 16 + sum(bits[d] * 2**k for k, d in enumerate(order(part)))


def scatter_place(pat, part):
    bits = bits_of(pat)
    return bits["core"] * 16 + sum(bits[d] * 2 ** (3 - k) for k, d in enumerate(order(part)))


def greet(peers):
    barrier = pltpu.get_barrier_semaphore()
    for peer in peers:
        pl.semaphore_signal(barrier, inc=1, device_id=peer, device_id_type=MESH)
    pl.semaphore_wait(barrier, len(peers))


class Doubling:
    def __init__(self, buf, part, me, sems):
        self.buf, self.part, self.sems = buf, part, sems
        self.y, self.pat = me
        self.place = gather_place(self.pat, part)
        self.pending = []

    def copy(self, src, dst, kind, slot, dim):
        send, recv = self.sems
        peer = (self.y, partner_of(self.pat, dim))
        made = pltpu.make_async_remote_copy(
            src_ref=src, dst_ref=dst,
            send_sem=send.at[kind, self.part, slot], recv_sem=recv.at[kind, self.part, slot],
            device_id=peer, device_id_type=MESH,
        )
        made.start()
        return made

    def base(self, step):
        return self.place - self.place % 2**step

    def first(self, src):
        mine = self.buf.at[self.part, pl.ds(self.place, 1)]
        self.ici = self.copy(src, mine, 0, 0, order(self.part)[0])
        self.pending.append(self.copy(src, mine, 1, 0, "core"))

    def step(self, s):
        self.ici.wait_recv()
        self.pending_send(self.ici)
        size = 2**s
        held = self.base(s)
        bit = (held // size) % 2
        came = held + size - 2 * size * bit
        if s < 3:
            full = self.buf.at[self.part, pl.ds(self.base(s + 1), 2 * size)]
            nxt = self.copy(full, full, 0, s + 1, order(self.part)[s + 1])
        got = self.buf.at[self.part, pl.ds(came, size)]
        self.pending.append(self.copy(got, got, 1, s + 1, "core"))
        if s < 3:
            self.ici = nxt

    def pending_send(self, made):
        self.sent = getattr(self, "sent", [])
        self.sent.append(made)

    def finish(self):
        for made in self.sent:
            made.wait_send()
        for made in self.pending:
            made.wait()


def gather_kernel(obj_ref, main_ref, halo_ref, edge, masked, msend, mrecv, hsend, hrecv, esem, lsem):
    y, pat = lax.axis_index("obj"), lax.axis_index("pat")
    rows = lax.axis_size("obj")
    left, right = (y + rows - 1) % rows, (y + 1) % rows
    greet([(left, pat), (right, pat)] + [(y, partner_of(pat, d)) for d in DIMS + ("core",)])
    send_edge = pltpu.make_async_remote_copy(
        src_ref=obj_ref.at[:, :, pl.ds(0, HALO)], dst_ref=edge,
        send_sem=esem.at[0], recv_sem=esem.at[1], device_id=(left, pat), device_id_type=MESH,
    )
    send_edge.start()
    mains = [Doubling(main_ref, p, (y, pat), (msend, mrecv)) for p in range(4)]
    halos = [Doubling(halo_ref, p, (y, pat), (hsend, hrecv)) for p in range(3)]
    own = []
    for p, part in enumerate(mains):
        part.first(obj_ref.at[:, :, pl.ds(p * 256, 256)])
    for p, part in enumerate(mains):
        own.append(pltpu.make_async_copy(
            obj_ref.at[:, :, pl.ds(p * 256, 256)], main_ref.at[p, pl.ds(part.place, 1)], lsem.at[p]))
        own[-1].start()
    send_edge.wait_recv()
    masked[...] = jnp.where(y == rows - 1, jnp.zeros_like(masked), edge[...])
    for p, part in enumerate(halos):
        part.first(masked.at[:, pl.ds(p * 16, 16)])
    for p, part in enumerate(halos):
        own.append(pltpu.make_async_copy(
            masked.at[:, pl.ds(p * 16, 16)], halo_ref.at[p, pl.ds(part.place, 1)], lsem.at[4 + p]))
        own[-1].start()
    for made in own:
        made.wait()
    for s in range(4):
        for part in mains:
            part.step(s)
        for part in halos:
            part.step(s)
    for part in mains + halos:
        part.finish()
    send_edge.wait_send()


def gather(obj):
    anywhere = pl.BlockSpec(memory_space=pl.ANY)
    dma = pltpu.SemaphoreType.DMA
    return pl.pallas_call(
        gather_kernel,
        out_shape=[
            jax.ShapeDtypeStruct((4, 32, 48, 256), BF),
            jax.ShapeDtypeStruct((3, 32, 16, 256), BF),
        ],
        in_specs=[pl.BlockSpec(memory_space=pltpu.VMEM)],
        out_specs=[anywhere, anywhere],
        scratch_shapes=[
            pltpu.VMEM((1, 48, HALO), BF),
            pltpu.VMEM((1, 48, HALO), BF),
            dma((2, 4, 5)), dma((2, 4, 5)), dma((2, 3, 5)), dma((2, 3, 5)), dma((2,)), dma((7,)),
        ],
        compiler_params=pltpu.CompilerParams(collective_id=0, has_side_effects=True),
        cost_estimate=pl.CostEstimate(flops=0, bytes_accessed=60 * MB, transcendentals=0),
        name="gather",
    )(obj.reshape(1, 48, TW))


def tables():
    index = np.arange(PX)
    angle = (index[:, None] * index[None, :] % PX) * (2.0 * np.pi / PX)
    real = (np.cos(angle) / np.sqrt(PX)).astype(ml_dtypes.bfloat16)
    imag = (-np.sin(angle) / np.sqrt(PX)).astype(ml_dtypes.bfloat16)
    fwd = np.block([[real, -imag], [imag, real]])
    inv = np.block([[real, imag], [-imag, real]])
    return fwd, inv


def dot(a, b):
    return jnp.dot(a, b, preferred_element_type=F32)


CH = 64


def window(value, rm, cm, rows):
    value = pltpu.roll(value, (640 - cm) % 640, 1)[:, :PX]
    return pltpu.roll(value, (rows + 8 - rm) % (rows + 8), 0)[:rows]


def work_kernel(rows_ref, cols_ref, main_ref, halo_ref, probe_ref, amps_ref, fwd_ref, inv_ref, out_ref,
                tile, grad, pacc, patch, stack, flat):
    slot = pl.program_id(0)

    @pl.when(slot == 0)
    def _():
        for o in range(32):
            for p in range(4):
                block = main_ref[p, gather_place(o, p)].astype(F32)
                cs = slice(p * 256, (p + 1) * 256)
                tile[0, o * OWN:(o + 1) * OWN, cs] = block[:OWN]
                tile[1, o * OWN:(o + 1) * OWN, cs] = block[OWN:]
            part = [halo_ref[p, gather_place(o, p)].astype(F32) for p in range(3)]
            cs = slice(TW, WIDE)
            tile[0, o * OWN:o * OWN + 16, cs] = part[0]
            tile[0, o * OWN + 16:o * OWN + 24, cs] = part[1][:8]
            tile[1, o * OWN:o * OWN + 8, cs] = part[1][8:]
            tile[1, o * OWN + 8:o * OWN + 24, cs] = part[2]
        tile[:, :, WIDE:] = jnp.zeros((2, H + 8, 128), F32)
        tile[:, H:, :WIDE] = jnp.zeros((2, 8, WIDE), F32)

        @pl.loop(0, H + 8, step=8)
        def _(r):
            grad[:, pl.ds(pl.multiple_of(r, 8), 8), :] = jnp.zeros((2, 8, WIDE + 128), F32)

    row, col = rows_ref[slot], cols_ref[slot]
    r0, c0 = pl.multiple_of(row // 8 * 8, 8), pl.multiple_of(col // 128 * 128, 128)
    rm, cm = row % 8, col % 128

    @pl.loop(0, PX, step=CH)
    def _(r):
        r = pl.multiple_of(r, CH)
        re, im = (window(tile[k, pl.ds(r0 + r, CH + 8), pl.ds(c0, 640)], rm, cm, CH) for k in range(2))
        patch[0, pl.ds(r, CH)] = re
        patch[1, pl.ds(r, CH)] = im
        pr, pi = probe_ref[0, pl.ds(r, CH)], probe_ref[1, pl.ds(r, CH)]
        stack[pl.ds(r, CH)] = (pr * re - pi * im).astype(BF)
        stack[pl.ds(PX + r, CH)] = (pr * im + pi * re).astype(BF)

    for h in range(2):
        flat[:, h * PX:(h + 1) * PX] = dot(fwd_ref[h * PX:(h + 1) * PX], stack[...]).astype(BF)

    @pl.loop(0, PX, step=256)
    def _(r):
        r = pl.multiple_of(r, 256)
        wave = dot(flat[pl.ds(r, 256)], inv_ref[...])
        re, im = wave[:, :PX], wave[:, PX:]
        ratio = amps_ref[0, pl.ds(r, 256)] * lax.rsqrt(re * re + im * im + 1.0)
        stack[pl.ds(r, 256)] = (re * ratio - re).astype(BF)
        stack[pl.ds(PX + r, 256)] = (im * ratio - im).astype(BF)

    for h in range(2):
        flat[:, h * PX:(h + 1) * PX] = dot(inv_ref[h * PX:(h + 1) * PX], stack[...]).astype(BF)

    @pl.loop(0, PX, step=256)
    def _(r):
        r = pl.multiple_of(r, 256)
        delta = dot(flat[pl.ds(r, 256)], fwd_ref[...])
        for k in range(0, 256, CH):
            dr, di = delta[k:k + CH, :PX], delta[k:k + CH, PX:]
            here = pl.ds(r + k, CH)
            pr, pi = probe_ref[0, here], probe_ref[1, here]
            qr, qi = patch[0, here], patch[1, here]
            mine = (qr * dr + qi * di, qr * di - qi * dr)
            for layer in range(2):
                pacc[layer, here] = jnp.where(slot == 0, 0.0, pacc[layer, here]) + mine[layer]
            terms = (pr * dr + pi * di, pr * di - pi * dr)
            for layer in range(2):
                wide = jnp.pad(terms[layer], ((0, 8), (0, 128)))
                wide = pltpu.roll(pltpu.roll(wide, rm, 0), cm, 1)
                grad[layer, pl.ds(r0 + r + k, CH + 8), pl.ds(c0, 640)] += wide

    @pl.when(slot == pl.num_programs(0) - 1)
    def _():
        for o in range(32):
            at = o * OWN
            parts = (
                grad[0, at:at + 16, :WIDE],
                jnp.concatenate([grad[0, at + 16:at + 24, :WIDE], grad[1, at:at + 8, :WIDE]], axis=0),
                grad[1, at + 8:at + 24, :WIDE],
                jnp.concatenate([pacc[0, o * 16:(o + 1) * 16], pacc[1, o * 16:(o + 1) * 16],
                                 jnp.zeros((16, HALO), F32)], axis=1),
            )
            for p in range(4):
                out_ref[p, scatter_place(o, p)] = parts[p].astype(BF)


def work(rows, cols, main, halo, probe, amps):
    fwd, inv = tables()
    whole = lambda *shape: pl.BlockSpec(shape, lambda i, r, c: (0,) * len(shape))
    return pl.pallas_call(
        work_kernel,
        out_shape=jax.ShapeDtypeStruct((4, 32, 16, WIDE), BF),
        grid_spec=pltpu.PrefetchScalarGridSpec(
            num_scalar_prefetch=2,
            grid=(3,),
            in_specs=[
                whole(4, 32, 48, 256), whole(3, 32, 16, 256), whole(2, PX, PX),
                pl.BlockSpec((1, PX, PX), lambda i, r, c: (i, 0, 0)),
                whole(2 * PX, 2 * PX), whole(2 * PX, 2 * PX),
            ],
            out_specs=whole(4, 32, 16, WIDE),
            scratch_shapes=[
                pltpu.VMEM((2, H + 8, WIDE + 128), F32),
                pltpu.VMEM((2, H + 8, WIDE + 128), F32),
                pltpu.VMEM((2, PX, PX), F32),
                pltpu.VMEM((2, PX, PX), F32),
                pltpu.VMEM((2 * PX, PX), BF),
                pltpu.VMEM((PX, 2 * PX), BF),
            ],
        ),
        compiler_params=pltpu.CompilerParams(vmem_limit_bytes=60 * MB),
        name="work",
    )(rows, cols, main, halo, probe, amps, jnp.asarray(fwd), jnp.asarray(inv))


def light_kernel(n, own_rows, own_cols, left_rows, left_cols, first_ref, probe_ref, out_ref, lit, acc):
    first = first_ref[0]
    keep = first_ref[1].astype(F32)
    lit[...] = jnp.zeros_like(lit)

    @pl.loop(0, PX, step=CH)
    def _(r):
        pr = probe_ref[0, pl.ds(pl.multiple_of(r, CH), CH)]
        pi = probe_ref[1, pl.ds(pl.multiple_of(r, CH), CH)]
        lit[pl.ds(pl.multiple_of(r + OWN, 8), CH), :PX] = pr * pr + pi * pi

    acc[...] = jnp.zeros_like(acc)
    group = 4
    for which, (rows, cols) in enumerate(((own_rows, own_cols), (left_rows, left_cols))):
        @pl.loop(0, n, step=group)
        def _(i):
            spots = []
            for k in range(group):
                row, col = rows[i + k], cols[i + k]
                start = jnp.clip(first - row + OWN, 0, PX + OWN)
                c0 = pl.multiple_of(col // 128 * 128, 128)
                value = lit[pl.ds(pl.multiple_of(start // 8 * 8, 8), OWN + 8), :]
                value = pltpu.roll(value, (OWN + 8 - start % 8) % (OWN + 8), 0)[:OWN]
                spots.append((c0, pltpu.roll(value, col % 128, 1)))
            for c0, value in spots:
                acc[which, :, pl.ds(c0, 640)] += value

    out_ref[:, :HALO] = acc[0, :, :HALO] + keep * acc[1, :, TW:WIDE]
    out_ref[:, HALO:] = acc[0, :, HALO:TW]


def light_sum(own_rows, own_cols, left_rows, left_cols, first, probe):
    n = own_rows.shape[0]
    smem = pl.BlockSpec(memory_space=pltpu.SMEM)
    return pl.pallas_call(
        functools.partial(light_kernel, n),
        out_shape=jax.ShapeDtypeStruct((OWN, TW), F32),
        in_specs=[smem] * 5 + [pl.BlockSpec(memory_space=pltpu.VMEM)],
        out_specs=pl.BlockSpec(memory_space=pltpu.VMEM),
        scratch_shapes=[
            pltpu.VMEM((PX + 2 * OWN + 8, 640), F32),
            pltpu.VMEM((2, OWN, WIDE + 128), F32),
        ],
        compiler_params=pltpu.CompilerParams(vmem_limit_bytes=16 * MB),
        name="light_sum",
    )(own_rows, own_cols, left_rows, left_cols, first, probe)


def reduce_kernel(g_ref, obj_out, probe_out, own, came0, acc0, acc1, acc2, acc3,
                  s0, s1, s2, s3, r0, r1, r2, r3, fin, spill, spilled, ypro, pbuf,
                  csend, crecv, lsem, rsend, rrecv, ysend, yrecv, psend, precv):
    y, pat = lax.axis_index("obj"), lax.axis_index("pat")
    rows = lax.axis_size("obj")
    core = pat % 2
    others = [((y + k) % rows, pat) for k in (1, 2, 3)]
    greet(others + [(y, partner_of(pat, d)) for d in DIMS + ("core",)])
    sibling = (y, partner_of(pat, "core"))
    bits = bits_of(pat)
    tops = [bits[order(p)[0]] for p in range(4)]
    swaps, locals_ = {}, {}
    for half in range(2):
        for p in range(4):
            at = (1 - tops[p]) * 8 if half == 0 else tops[p] * 8
            swaps[p, half] = pltpu.make_async_remote_copy(
                src_ref=g_ref.at[p, pl.ds((1 - core) * 16 + at, 8)], dst_ref=came0.at[p, half],
                send_sem=csend.at[p, half], recv_sem=crecv.at[p, half],
                device_id=sibling, device_id_type=MESH)
            swaps[p, half].start()
            locals_[p, half] = pltpu.make_async_copy(
                g_ref.at[p, pl.ds(core * 16 + at, 8)], own.at[p, half], lsem.at[p, half])
            locals_[p, half].start()
    accs, sends, recvs = (acc0, acc1, acc2, acc3), (s0, s1, s2, s3), (r0, r1, r2, r3)
    made = {}

    def start(p, s):
        made[p, s] = pltpu.make_async_remote_copy(
            src_ref=sends[s].at[p], dst_ref=recvs[s].at[p],
            send_sem=rsend.at[p, s], recv_sem=rrecv.at[p, s],
            device_id=(y, partner_of(pat, order(p)[s])), device_id_type=MESH)
        made[p, s].start()

    for half in range(2):
        for p in range(4):
            swaps[p, half].wait_recv()
            locals_[p, half].wait()

            @pl.loop(0, 8)
            def _(j):
                total = own[p, half, j].astype(F32) + came0[p, half, j].astype(F32)
                if half == 0:
                    s0[p, j] = total.astype(BF)
                else:
                    acc0[p, j] = total

            if half == 0:
                start(p, 0)
    for s in range(1, 4):
        size = 8 >> s
        for p in range(4):
            made[p, s - 1].wait_recv()
            bit = bits[order(p)[s]]

            @pl.loop(0, size)
            def _(j):
                at = (1 - bit) * size + j
                sends[s][p, j] = (accs[s - 1][p, at] + recvs[s - 1][p, at].astype(F32)).astype(BF)

            start(p, s)

            @pl.loop(0, size)
            def _(j):
                at = bit * size + j
                accs[s][p, j] = accs[s - 1][p, at] + recvs[s - 1][p, at].astype(F32)

    for p in (3, 0, 1, 2):
        made[p, 3].wait_recv()
        fin[p] = acc3[p, 0] + r3[p, 0].astype(F32)
        if p == 3:
            ypro[pl.ds(y, 1)] = fin[3, :, :TW].reshape(1, 16, TW)
            mine = ypro.at[pl.ds(y, 1)]
            across = []
            for k, other in enumerate(others):
                across.append(pltpu.make_async_remote_copy(
                    src_ref=mine, dst_ref=mine, send_sem=ysend.at[k], recv_sem=yrecv.at[k],
                    device_id=other, device_id_type=MESH))
                across[-1].start()
    spill[...] = fin[0:3, :, TW:]
    over = pltpu.make_async_remote_copy(
        src_ref=spill, dst_ref=spilled, send_sem=ysend.at[3], recv_sem=yrecv.at[3],
        device_id=others[0], device_id_type=MESH)
    over.start()
    for made_y in across:
        made_y.wait_recv()
    probe = (ypro[0] + ypro[1] + ypro[2] + ypro[3]).astype(BF)
    gathers = [Doubling(pbuf, p, (y, pat), (psend, precv)) for p in range(4)]
    for p, part in enumerate(gathers):
        pbuf[p, pl.ds(part.place, 1)] = probe[:, p * 256:(p + 1) * 256].reshape(1, 16, 256)
        part.first(pbuf.at[p, pl.ds(part.place, 1)])
    over.wait_recv()
    for p in range(3):
        extra = jnp.where(y == 0, 0.0, spilled[p])
        obj_out[p * 16:(p + 1) * 16, :HALO] = fin[p, :, :HALO] + extra
        obj_out[p * 16:(p + 1) * 16, HALO:] = fin[p, :, HALO:TW]
    for s in range(4):
        for part in gathers:
            part.step(s)
    for part in gathers:
        part.finish()
    for o in range(32):
        for p in range(4):
            probe_out[p // 2, o * 16:(o + 1) * 16, (p % 2) * 256:(p % 2 + 1) * 256] = pbuf[p, gather_place(o, p)]
    for half in range(2):
        for p in range(4):
            swaps[p, half].wait_send()
    for s in range(4):
        for p in range(4):
            made[p, s].wait_send()
    for made_y in across:
        made_y.wait_send()
    over.wait_send()


def reduce_all(g):
    dma = pltpu.SemaphoreType.DMA
    vmem = pltpu.VMEM
    return pl.pallas_call(
        reduce_kernel,
        out_shape=[jax.ShapeDtypeStruct((48, TW), F32), jax.ShapeDtypeStruct((2, PX, PX), BF)],
        in_specs=[pl.BlockSpec(memory_space=pl.ANY)],
        out_specs=[pl.BlockSpec(memory_space=pltpu.VMEM)] * 2,
        scratch_shapes=[
            vmem((4, 2, 8, 16, WIDE), BF), vmem((4, 2, 8, 16, WIDE), BF),
            *[vmem((4, 8 >> s, 16, WIDE), F32) for s in range(4)],
            *[vmem((4, 8 >> s, 16, WIDE), BF) for s in range(4)],
            *[vmem((4, 8 >> s, 16, WIDE), BF) for s in range(4)],
            vmem((4, 16, WIDE), F32),
            vmem((3, 16, HALO), F32), vmem((3, 16, HALO), F32),
            vmem((4, 16, TW), F32), vmem((4, 32, 16, 256), BF),
            dma((4, 2)), dma((4, 2)), dma((4, 2)), dma((4, 4)), dma((4, 4)), dma((4,)), dma((4,)),
            dma((2, 4, 5)), dma((2, 4, 5)),
        ],
        compiler_params=pltpu.CompilerParams(
            collective_id=1, has_side_effects=True, vmem_limit_bytes=32 * MB),
        cost_estimate=pl.CostEstimate(flops=0, bytes_accessed=60 * MB, transcendentals=0),
        name="reduce_all",
    )(g)


def local(obj, probe, amps, rows, cols):
    total = rows.shape[0] * lax.axis_size("obj") * lax.axis_size("pat")
    y, pat = lax.axis_index("obj"), lax.axis_index("pat")
    n = rows.shape[0] * lax.axis_size("pat")
    spots = lax.all_gather(jnp.stack([rows, cols]), ("obj", "pat"), axis=1, tiled=True)
    main, halo = gather(obj)
    g = work(rows, cols, main, halo, probe, amps)
    mine = lax.dynamic_slice(spots, (0, y * n), (2, n))
    left = lax.dynamic_slice(spots, (0, jnp.maximum(y - 1, 0) * n), (2, n))
    first = jnp.stack([pat * OWN, (y > 0).astype(jnp.int32)])
    light = light_sum(mine[0], mine[1], left[0], left[1], first, probe)
    own, probe_sum = reduce_all(g)
    obj_step = own.reshape(2, OWN, TW) / (light + 1.0)
    probe_grad = probe_sum.astype(F32) * (1.0 / math.sqrt(total))
    return (obj_step, probe_grad)


def solution(mesh):
    placed = (
        P(None, "pat", "obj"),
        P(),
        P(("obj", "pat"), None, None),
        P(("obj", "pat")),
        P(("obj", "pat")),
    )
    return jax.shard_map(
        local, mesh=mesh, in_specs=placed, out_specs=(P(None, "pat", "obj"), P()), check_vma=False
    )
```

```python
import functools
import math

import jax
import jax.numpy as jnp
import ml_dtypes
import numpy as np
from jax import lax
from jax.experimental import pallas as pl
from jax.experimental.pallas import tpu as pltpu
from jax.sharding import PartitionSpec as P

PX = 512
HALO = 256
H = 768
TW = 1024
WIDE = TW + HALO
OWN = 24
BF = jnp.bfloat16
F32 = jnp.float32
MESH = pl.DeviceIdType.MESH
DIMS = ("xa", "za", "xb", "zb")
MB = 1 << 20


def bits_of(pat):
    x, z = (pat // 2) % 4, pat // 8
    return {
        "core": pat % 2,
        "xa": (x // 2 + x) % 2,
        "xb": x // 2,
        "za": (z // 2 + z) % 2,
        "zb": z // 2,
    }


def partner_of(pat, dim):
    core, x, z = pat % 2, (pat // 2) % 4, pat // 8
    if dim == "core":
        core = 1 - core
    elif dim == "xa":
        x = x + 1 - 2 * (x % 2)
    elif dim == "xb":
        x = 3 - x
    elif dim == "za":
        z = z + 1 - 2 * (z % 2)
    else:
        z = 3 - z
    return (z * 4 + x) * 2 + core


def order(part):
    return [DIMS[(part + k) % 4] for k in range(4)]


def gather_place(pat, part):
    bits = bits_of(pat)
    return bits["core"] * 16 + sum(bits[d] * 2**k for k, d in enumerate(order(part)))


def scatter_place(pat, part):
    bits = bits_of(pat)
    return bits["core"] * 16 + sum(bits[d] * 2 ** (3 - k) for k, d in enumerate(order(part)))


def greet(peers):
    barrier = pltpu.get_barrier_semaphore()
    for peer in peers:
        pl.semaphore_signal(barrier, inc=1, device_id=peer, device_id_type=MESH)
    pl.semaphore_wait(barrier, len(peers))


class Doubling:
    def __init__(self, buf, part, me, sems):
        self.buf, self.part, self.sems = buf, part, sems
        self.y, self.pat = me
        self.place = gather_place(self.pat, part)
        self.pending = []

    def copy(self, src, dst, kind, slot, dim):
        send, recv = self.sems
        peer = (self.y, partner_of(self.pat, dim))
        made = pltpu.make_async_remote_copy(
            src_ref=src, dst_ref=dst,
            send_sem=send.at[kind, self.part, slot], recv_sem=recv.at[kind, self.part, slot],
            device_id=peer, device_id_type=MESH,
        )
        made.start()
        return made

    def base(self, step):
        return self.place - self.place % 2**step

    def first(self, src):
        mine = self.buf.at[self.part, pl.ds(self.place, 1)]
        self.ici = self.copy(src, mine, 0, 0, order(self.part)[0])
        self.pending.append(self.copy(src, mine, 1, 0, "core"))

    def step(self, s):
        self.ici.wait_recv()
        self.pending_send(self.ici)
        size = 2**s
        held = self.base(s)
        bit = (held // size) % 2
        came = held + size - 2 * size * bit
        if s < 3:
            full = self.buf.at[self.part, pl.ds(self.base(s + 1), 2 * size)]
            nxt = self.copy(full, full, 0, s + 1, order(self.part)[s + 1])
        got = self.buf.at[self.part, pl.ds(came, size)]
        self.pending.append(self.copy(got, got, 1, s + 1, "core"))
        if s < 3:
            self.ici = nxt

    def pending_send(self, made):
        self.sent = getattr(self, "sent", [])
        self.sent.append(made)

    def finish(self):
        for made in self.sent:
            made.wait_send()
        for made in self.pending:
            made.wait()


def gather_kernel(obj_ref, pos_ref, split_ref, main_ref, halo_ref, spots_ref, mine, edge, masked, pos_in, pos_all,
                  msend, mrecv, hsend, hrecv, psend, precv, esem, lsem):
    y, pat = lax.axis_index("obj"), lax.axis_index("pat")
    rows = lax.axis_size("obj")
    left, right = (y + rows - 1) % rows, (y + 1) % rows
    greet([(left, pat), (right, pat)] + [(y, partner_of(pat, d)) for d in DIMS + ("core",)])
    send_pos = pltpu.make_async_remote_copy(
        src_ref=pos_ref, dst_ref=pos_in,
        send_sem=esem.at[2], recv_sem=esem.at[3], device_id=(right, pat), device_id_type=MESH,
    )
    send_pos.start()
    mains = [Doubling(main_ref, p, (y, pat), (msend, mrecv)) for p in range(4)]
    halos = [Doubling(halo_ref, p, (y, pat), (hsend, hrecv)) for p in range(3)]
    spots = Doubling(spots_ref, 0, (y, pat), (psend, precv))
    own = []
    for p, part in enumerate(mains):
        here = pl.ds(p * 256, 256)
        mine[0, :, here] = dot(obj_ref[0, :, here], split_ref[...]).astype(BF)
        if p == 0:
            send_edge = pltpu.make_async_remote_copy(
                src_ref=mine.at[:, :, here], dst_ref=edge,
                send_sem=esem.at[0], recv_sem=esem.at[1], device_id=(left, pat), device_id_type=MESH,
            )
            send_edge.start()
        part.first(mine.at[:, :, here])
    for p, part in enumerate(mains):
        own.append(pltpu.make_async_copy(
            mine.at[:, :, pl.ds(p * 256, 256)], main_ref.at[p, pl.ds(part.place, 1)], lsem.at[p]))
        own[-1].start()
    send_edge.wait_recv()
    masked[...] = jnp.where(y == rows - 1, jnp.zeros_like(masked), edge[...])
    for p, part in enumerate(halos):
        part.first(masked.at[:, pl.ds(p * 16, 16)])
    for p, part in enumerate(halos):
        own.append(pltpu.make_async_copy(
            masked.at[:, pl.ds(p * 16, 16)], halo_ref.at[p, pl.ds(part.place, 1)], lsem.at[4 + p]))
        own[-1].start()
    send_pos.wait_recv()
    line = lax.broadcasted_iota(jnp.int32, (1, 8, 128), 1)
    pos_all[...] = jnp.where(line < 2, pos_ref[...], pltpu.roll(pos_in[...], 2, 1))
    spots.first(pos_all)
    own.append(pltpu.make_async_copy(pos_all, spots_ref.at[0, pl.ds(spots.place, 1)], lsem.at[7]))
    own[-1].start()
    for made in own:
        made.wait()
    for s in range(4):
        for part in mains + halos + [spots]:
            part.step(s)
    for part in mains + halos + [spots]:
        part.finish()
    send_edge.wait_send()
    send_pos.wait_send()


def gather(obj, pos, split):
    anywhere = pl.BlockSpec(memory_space=pl.ANY)
    dma = pltpu.SemaphoreType.DMA
    return pl.pallas_call(
        gather_kernel,
        out_shape=[
            jax.ShapeDtypeStruct((4, 32, 48, 256), BF),
            jax.ShapeDtypeStruct((3, 32, 16, 256), BF),
            jax.ShapeDtypeStruct((1, 32, 8, 128), jnp.int32),
        ],
        in_specs=[pl.BlockSpec(memory_space=pltpu.VMEM)] * 3,
        out_specs=[anywhere] * 3,
        scratch_shapes=[
            pltpu.VMEM((1, 48, TW), BF),
            pltpu.VMEM((1, 48, HALO), BF),
            pltpu.VMEM((1, 48, HALO), BF),
            pltpu.VMEM((1, 8, 128), jnp.int32),
            pltpu.VMEM((1, 8, 128), jnp.int32),
            dma((2, 4, 5)), dma((2, 4, 5)), dma((2, 3, 5)), dma((2, 3, 5)), dma((2, 1, 5)), dma((2, 1, 5)),
            dma((4,)), dma((8,)),
        ],
        compiler_params=pltpu.CompilerParams(collective_id=0, has_side_effects=True),
        cost_estimate=pl.CostEstimate(flops=0, bytes_accessed=60 * MB, transcendentals=0),
        name="gather",
    )(obj.reshape(1, 48, TW), pos, split)


def tables():
    index = np.arange(PX)
    angle = (index[:, None] * index[None, :] % PX) * (2.0 * np.pi / PX)
    real = (np.cos(angle) / np.sqrt(PX)).astype(ml_dtypes.bfloat16)
    imag = (-np.sin(angle) / np.sqrt(PX)).astype(ml_dtypes.bfloat16)
    low = np.arange(256)
    sorted_low = np.concatenate([low[::2], low[1::2]])
    even, odd = index[::2], index[1::2]

    def left(re, im, rows, cols):
        pick = np.ix_(rows, cols)
        return np.block([[re[pick], -im[pick]], [im[pick], re[pick]]])

    def right(re, im, rows, cols):
        pick = np.ix_(rows, cols)
        return np.block([[re[pick], im[pick]], [-im[pick], re[pick]]])

    return np.stack([
        left(real, imag, sorted_low, even), left(real, imag, sorted_low, odd),
        right(real, imag, even, low), right(real, imag, odd, low),
        left(real, -imag, sorted_low, even), left(real, -imag, sorted_low, odd),
        right(real, -imag, low, even), right(real, -imag, low, odd),
    ])


def splitter():
    k = np.arange(256)
    return (np.arange(256)[:, None] == 2 * (k % 128) + k // 128).astype(ml_dtypes.bfloat16)


def dot(a, b):
    return jnp.dot(a, b, preferred_element_type=F32)


def moved(x, pick):
    high = x.astype(BF)
    rest = x - high.astype(F32)
    mid = rest.astype(BF)
    low = (rest - mid.astype(F32)).astype(BF)
    return dot(high, pick) + dot(mid, pick) + dot(low, pick)


SLABS = 6
ROWS = H + 8


def work_kernel(rows_ref, cols_ref, main_ref, halo_ref, probe_ref, amps_ref, tab_ref, split_ref, out_ref,
                main, halo, tile, grad, plain, probe, amps, tab, split, pacc, patch, stack, flat, out, sems):
    loads = {}

    def load(name, src, dst, slot):
        loads[name] = pltpu.make_async_copy(src, dst, sems.at[slot])
        loads[name].start()

    load("probe", probe_ref, plain, 0)
    load("split", split_ref, split, 1)
    load("main", main_ref, main, 2)
    load("halo", halo_ref, halo, 3)
    load("tab", tab_ref, tab, 4)
    for i in range(3):
        for j in range(4):
            load(("amps", i, j), amps_ref.at[i, :, pl.ds(j * 128, 128)], amps.at[i, j, pl.ds(0, PX)], 5 + i * 4 + j)

    @pl.loop(0, ROWS, step=8)
    def _(r):
        grad[:, :, :, pl.ds(pl.multiple_of(r, 8), 8), :] = jnp.zeros((2, 2, SLABS, 8, 128), F32)

    @pl.loop(0, PX, step=64)
    def _(r):
        pacc[:, :, :, pl.ds(pl.multiple_of(r, 64), 64), :] = jnp.zeros((2, 2, 2, 64, 128), F32)

    loads["probe"].wait()
    loads["split"].wait()
    for layer in range(2):
        @pl.loop(0, PX, step=256)
        def _(r):
            here = pl.ds(pl.multiple_of(r, 256), 256)
            for j in range(2):
                parted = moved(plain[layer, here, j * 256:(j + 1) * 256], split[...])
                for q in range(2):
                    probe[layer, q, j, here] = parted[:, q * 128:(q + 1) * 128]

    loads["main"].wait()
    loads["halo"].wait()

    @pl.loop(0, 32)
    def _(o):
        at = pl.multiple_of(o * OWN, 8)
        for p in range(4):
            block = main[p, gather_place(o, p)].astype(F32)
            for layer in range(2):
                for q in range(2):
                    tile[layer, q, p, pl.ds(at, OWN)] = block[layer * OWN:(layer + 1) * OWN, q * 128:(q + 1) * 128]
        part = [halo[p, gather_place(o, p)].astype(F32) for p in range(3)]
        for q in range(2):
            cs = slice(q * 128, (q + 1) * 128)
            tile[0, q, 4, pl.ds(at, 16)] = part[0][:, cs]
            tile[0, q, 4, pl.ds(at + 16, 8)] = part[1][:8, cs]
            tile[1, q, 4, pl.ds(at, 8)] = part[1][8:, cs]
            tile[1, q, 4, pl.ds(at + 8, 16)] = part[2][:, cs]

    loads["tab"].wait()
    for i in range(3):
        for j in range(4):
            loads["amps", i, j].wait()
    lane = lax.broadcasted_iota(jnp.int32, (32, 128), 1)

    @pl.loop(0, 3)
    def _(slot):
        row, col = rows_ref[slot], cols_ref[slot]
        places = []
        for q in range(2):
            start = (col + q) // 2
            places.append(((col + q) % 2, start // 128, start % 128))

        for t in range(2):
            @pl.loop(0, 8)
            def _(i):
                i32 = pl.multiple_of(i * 32, 32)
                here = pl.ds(t + i * 64, 32, stride=2)
                there = pl.ds(row + t + i * 64, 32, stride=2)
                for q, (plane, b, m) in enumerate(places):
                    got = []
                    for layer in range(2):
                        turned = [pltpu.roll(tile[layer, plane, b + j, there, :], (128 - m) % 128, 1) for j in range(3)]
                        got.append([jnp.where(lane < 128 - m, turned[j], turned[j + 1]) for j in range(2)])
                    for j in range(2):
                        re, im = got[0][j], got[1][j]
                        pr, pi = probe[0, q, j, here, :], probe[1, q, j, here, :]
                        patch[0, t, q, j, pl.ds(i32, 32)] = re
                        patch[1, t, q, j, pl.ds(i32, 32)] = im
                        cs = slice(j * 128, (j + 1) * 128)
                        stack[t, q, pl.ds(i32, 32), cs] = (pr * re - pi * im).astype(BF)
                        stack[t, q, pl.ds(256 + i32, 32), cs] = (pr * im + pi * re).astype(BF)

        def spread(to, which, total, other):
            for part in range(2):
                for upper, value in ((0, total), (1, other)):
                    for t in range(2):
                        at = part * 256 + t * 128
                        to[which, t * 256 + upper * 128:t * 256 + (upper + 1) * 128, part * 256:(part + 1) * 256] = (
                            value[at:at + 128].astype(BF))

        @pl.loop(0, 2)
        def _(q):
            even, odd = dot(tab[0], stack[0, q]), dot(tab[1], stack[1, q])
            spread(flat, q, even + odd, even - odd)

        @pl.loop(0, 2)
        def _(t):
            here = pl.ds(pl.multiple_of(t * 256, 256), 256)
            even, odd = dot(flat[0, here], tab[2]), dot(flat[1, here], tab[3])
            for upper, wave in ((0, even + odd), (1, even - odd)):
                for j in range(2):
                    re, im = wave[:, j * 128:(j + 1) * 128], wave[:, 256 + j * 128:256 + (j + 1) * 128]
                    amp = amps[slot, 2 * upper + j, pl.ds(t, 256, stride=2), :]
                    ratio = amp * lax.rsqrt(re * re + im * im + 1.0)
                    cs = slice(j * 128, (j + 1) * 128)
                    stack[t, upper, 0:256, cs] = (re * ratio - re).astype(BF)
                    stack[t, upper, 256:512, cs] = (im * ratio - im).astype(BF)

        halves = []
        for upper in range(2):
            even, odd = dot(tab[4], stack[0, upper]), dot(tab[5], stack[1, upper])
            halves.append((even + odd, even - odd))
        spread(flat, 0, halves[0][0] + halves[1][0], halves[0][1] + halves[1][1])
        spread(flat, 1, halves[0][0] - halves[1][0], halves[0][1] - halves[1][1])

        @pl.loop(0, 2)
        def _(t):
            here = pl.ds(pl.multiple_of(t * 256, 256), 256)
            deltas = dot(flat[0, here], tab[6]), dot(flat[1, here], tab[7])
            for i in range(8):
                at = pl.ds(t + i * 64, 32, stride=2)
                there = pl.ds(row + t + i * 64, 32, stride=2)
                rs = slice(i * 32, (i + 1) * 32)
                for q, (plane, b, m) in enumerate(places):
                    turned = [[], []]
                    for j in range(2):
                        dr = deltas[q][rs, j * 128:(j + 1) * 128]
                        di = deltas[q][rs, 256 + j * 128:256 + (j + 1) * 128]
                        pr, pi = probe[0, q, j, at, :], probe[1, q, j, at, :]
                        qr, qi = patch[0, t, q, j, rs], patch[1, t, q, j, rs]
                        pacc[0, q, j, at, :] += qr * dr + qi * di
                        pacc[1, q, j, at, :] += qr * di - qi * dr
                        turned[0].append(pltpu.roll(pr * dr + pi * di, m, 1))
                        turned[1].append(pltpu.roll(pr * di - pi * dr, m, 1))
                    for layer in range(2):
                        one, two = turned[layer]
                        grad[layer, plane, b, there, :] += jnp.where(lane >= m, one, 0.0)
                        grad[layer, plane, b + 1, there, :] += jnp.where(lane >= m, two, one)
                        grad[layer, plane, b + 2, there, :] += jnp.where(lane < m, two, 0.0)

    stores = []
    for core in range(2):
        @pl.loop(0, 16)
        def _(pair):
            o = 2 * pair + core
            at = pl.multiple_of(o * OWN, 8)
            spot = [scatter_place(o, p) for p in range(4)]
            for c in range(5):
                for q in range(2):
                    cs = slice(c * 256 + q * 128, c * 256 + (q + 1) * 128)
                    low = grad[0, q, c, pl.ds(at, OWN)]
                    high = grad[1, q, c, pl.ds(at, OWN)]
                    out[0, spot[0], :, cs] = low[:16].astype(BF)
                    out[1, spot[1], :, cs] = jnp.concatenate([low[16:], high[:8]], axis=0).astype(BF)
                    out[2, spot[2], :, cs] = high[8:].astype(BF)
            rs = pl.ds(pl.multiple_of(o * 16, 16), 16)
            for layer in range(2):
                for j in range(2):
                    for q in range(2):
                        c = layer * 512 + j * 256 + q * 128
                        out[3, spot[3], :, c:c + 128] = pacc[layer, q, j, rs].astype(BF)
            out[3, spot[3], :, TW:] = jnp.zeros((16, HALO), BF)

        half = pl.ds(core * 16, 16)
        stores.append(pltpu.make_async_copy(out.at[:, half], out_ref.at[:, half], sems.at[17 + core]))
        stores[-1].start()
    for made in stores:
        made.wait()


def work(rows, cols, main, halo, probe, amps, split):
    smem = pl.BlockSpec(memory_space=pltpu.SMEM)
    anywhere = pl.BlockSpec(memory_space=pl.ANY)
    vmem = pltpu.VMEM
    return pl.pallas_call(
        work_kernel,
        out_shape=jax.ShapeDtypeStruct((4, 32, 16, WIDE), BF),
        in_specs=[smem] * 2 + [anywhere] * 6,
        out_specs=anywhere,
        scratch_shapes=[
            vmem((4, 32, 48, 256), BF), vmem((3, 32, 16, 256), BF),
            vmem((2, 2, SLABS, ROWS, 128), F32), vmem((2, 2, SLABS, ROWS, 128), F32),
            vmem((2, PX, PX), F32), vmem((2, 2, 2, PX + 8, 128), F32), vmem((3, 4, PX + 8, 128), F32),
            vmem((8, PX, PX), BF), vmem((256, 256), BF),
            vmem((2, 2, 2, PX + 8, 128), F32), vmem((2, 2, 2, 2, 256, 128), F32),
            vmem((2, 2, PX, 256), BF), vmem((2, PX, PX), BF),
            vmem((4, 32, 16, WIDE), BF),
            pltpu.SemaphoreType.DMA((19,)),
        ],
        compiler_params=pltpu.CompilerParams(vmem_limit_bytes=62 * MB),
        name="work",
    )(rows, cols, main, halo, probe, amps, jnp.asarray(tables()), split)


def light_kernel(spots, first_ref, probe_ref, out_ref, lit, acc):
    first = first_ref[0]
    keep = first_ref[1].astype(F32)
    for j in range(4):
        lit[j, 0:OWN] = jnp.zeros((OWN, 128), F32)
        lit[j, PX + OWN:] = jnp.zeros((OWN + 8, 128), F32)

        @pl.loop(0, PX, step=64)
        def _(r):
            here = pl.ds(pl.multiple_of(r, 64), 64)
            cs = slice(j * 128, (j + 1) * 128)
            pr, pi = probe_ref[0, here, cs], probe_ref[1, here, cs]
            lit[j, pl.ds(pl.multiple_of(r + OWN, 8), 64)] = pr * pr + pi * pi

    acc[...] = jnp.zeros_like(acc)
    lane = lax.broadcasted_iota(jnp.int32, (8, 128), 1)

    @pl.loop(0, 32)
    def _(o):
        for which in range(2):
            for k in range(3):
                row, col = spots[o * 12 + which * 6 + k], spots[o * 12 + which * 6 + 3 + k]
                start = jnp.clip(first - row + OWN, 0, PX + OWN)
                b, m = col // 128, col % 128
                keeps = lane >= m
                for t in range(3):
                    last = 0.0
                    for j in range(5):
                        here = pltpu.roll(lit[j, pl.ds(start + t, 8, stride=3), :], m, 1) if j < 4 else 0.0
                        acc[which, t, b + j] += jnp.where(keeps, here, last)
                        last = here

    for j in range(8):
        for t in range(3):
            value = acc[0, t, j]
            if j < 2:
                value = value + keep * acc[1, t, 8 + j]
            out_ref[j, pl.ds(t, 8, stride=3), :] = value


def light_sum(spots, first, probe):
    smem = pl.BlockSpec(memory_space=pltpu.SMEM)
    return pl.pallas_call(
        light_kernel,
        out_shape=jax.ShapeDtypeStruct((8, OWN, 128), F32),
        in_specs=[smem] * 2 + [pl.BlockSpec(memory_space=pltpu.VMEM)],
        out_specs=pl.BlockSpec(memory_space=pltpu.VMEM),
        scratch_shapes=[
            pltpu.VMEM((4, PX + 2 * OWN + 8, 128), F32),
            pltpu.VMEM((2, 3, 11, 8, 128), F32),
        ],
        compiler_params=pltpu.CompilerParams(vmem_limit_bytes=16 * MB),
        name="light_sum",
    )(spots, first, probe)


def reduce_kernel(g_ref, join_ref, obj_out, probe_out, own, came0, acc0, acc1, acc2, acc3,
                  s0, s1, s2, s3, r0, r1, r2, r3, fin, spill, spilled, ypro, pbuf,
                  csend, crecv, lsem, rsend, rrecv, ysend, yrecv, psend, precv):
    y, pat = lax.axis_index("obj"), lax.axis_index("pat")
    rows = lax.axis_size("obj")
    core = pat % 2
    others = [((y + k) % rows, pat) for k in (1, 2, 3)]
    greet(others + [(y, partner_of(pat, d)) for d in DIMS + ("core",)])
    sibling = (y, partner_of(pat, "core"))
    bits = bits_of(pat)
    tops = [bits[order(p)[0]] for p in range(4)]
    swaps, locals_ = {}, {}
    for half in range(2):
        for p in range(4):
            at = (1 - tops[p]) * 8 if half == 0 else tops[p] * 8
            swaps[p, half] = pltpu.make_async_remote_copy(
                src_ref=g_ref.at[p, pl.ds((1 - core) * 16 + at, 8)], dst_ref=came0.at[p, half],
                send_sem=csend.at[p, half], recv_sem=crecv.at[p, half],
                device_id=sibling, device_id_type=MESH)
            swaps[p, half].start()
            locals_[p, half] = pltpu.make_async_copy(
                g_ref.at[p, pl.ds(core * 16 + at, 8)], own.at[p, half], lsem.at[p, half])
            locals_[p, half].start()
    accs, sends, recvs = (acc0, acc1, acc2, acc3), (s0, s1, s2, s3), (r0, r1, r2, r3)
    made = {}

    def start(p, s):
        made[p, s] = pltpu.make_async_remote_copy(
            src_ref=sends[s].at[p], dst_ref=recvs[s].at[p],
            send_sem=rsend.at[p, s], recv_sem=rrecv.at[p, s],
            device_id=(y, partner_of(pat, order(p)[s])), device_id_type=MESH)
        made[p, s].start()

    for half in range(2):
        for p in range(4):
            swaps[p, half].wait_recv()
            locals_[p, half].wait()

            @pl.loop(0, 8)
            def _(j):
                total = own[p, half, j].astype(F32) + came0[p, half, j].astype(F32)
                if half == 0:
                    s0[p, j] = total.astype(BF)
                else:
                    acc0[p, j] = total

            if half == 0:
                start(p, 0)
    for s in range(1, 4):
        size = 8 >> s
        for p in range(4):
            made[p, s - 1].wait_recv()
            bit = bits[order(p)[s]]

            @pl.loop(0, size)
            def _(j):
                at = (1 - bit) * size + j
                sends[s][p, j] = (accs[s - 1][p, at] + recvs[s - 1][p, at].astype(F32)).astype(BF)

            start(p, s)

            @pl.loop(0, size)
            def _(j):
                at = bit * size + j
                accs[s][p, j] = accs[s - 1][p, at] + recvs[s - 1][p, at].astype(F32)

    for p in (3, 0, 1, 2):
        made[p, 3].wait_recv()
        fin[p] = acc3[p, 0] + r3[p, 0].astype(F32)
        if p == 3:
            ypro[pl.ds(y, 1)] = fin[3, :, :TW].reshape(1, 16, TW)
            mine = ypro.at[pl.ds(y, 1)]
            across = []
            for k, other in enumerate(others):
                across.append(pltpu.make_async_remote_copy(
                    src_ref=mine, dst_ref=mine, send_sem=ysend.at[k], recv_sem=yrecv.at[k],
                    device_id=other, device_id_type=MESH))
                across[-1].start()
    spill[...] = fin[0:3, :, TW:]
    over = pltpu.make_async_remote_copy(
        src_ref=spill, dst_ref=spilled, send_sem=ysend.at[3], recv_sem=yrecv.at[3],
        device_id=others[0], device_id_type=MESH)
    over.start()
    for made_y in across:
        made_y.wait_recv()
    probe = (ypro[0] + ypro[1] + ypro[2] + ypro[3]).astype(BF)
    probe = [dot(probe[:, p * 256:(p + 1) * 256], join_ref[...]).astype(BF) for p in range(4)]
    gathers = [Doubling(pbuf, p, (y, pat), (psend, precv)) for p in range(4)]
    for p, part in enumerate(gathers):
        pbuf[p, pl.ds(part.place, 1)] = probe[p].reshape(1, 16, 256)
        part.first(pbuf.at[p, pl.ds(part.place, 1)])
    over.wait_recv()
    for p in range(3):
        extra = jnp.where(y == 0, 0.0, spilled[p])
        for c in range(4):
            cs = slice(c * 256, (c + 1) * 256)
            own_sum = fin[p, :, cs] + extra if c == 0 else fin[p, :, cs]
            obj_out[p * 16:(p + 1) * 16, cs] = moved(own_sum, join_ref[...])
    for s in range(4):
        for part in gathers:
            part.step(s)
    for part in gathers:
        part.finish()
    for o in range(32):
        for p in range(4):
            probe_out[p // 2, o * 16:(o + 1) * 16, (p % 2) * 256:(p % 2 + 1) * 256] = pbuf[p, gather_place(o, p)]
    for half in range(2):
        for p in range(4):
            swaps[p, half].wait_send()
    for s in range(4):
        for p in range(4):
            made[p, s].wait_send()
    for made_y in across:
        made_y.wait_send()
    over.wait_send()


def reduce_all(g, join):
    dma = pltpu.SemaphoreType.DMA
    vmem = pltpu.VMEM
    return pl.pallas_call(
        reduce_kernel,
        out_shape=[jax.ShapeDtypeStruct((48, TW), F32), jax.ShapeDtypeStruct((2, PX, PX), BF)],
        in_specs=[pl.BlockSpec(memory_space=pl.ANY), pl.BlockSpec(memory_space=pltpu.VMEM)],
        out_specs=[pl.BlockSpec(memory_space=pltpu.VMEM)] * 2,
        scratch_shapes=[
            vmem((4, 2, 8, 16, WIDE), BF), vmem((4, 2, 8, 16, WIDE), BF),
            *[vmem((4, 8 >> s, 16, WIDE), F32) for s in range(4)],
            *[vmem((4, 8 >> s, 16, WIDE), BF) for s in range(4)],
            *[vmem((4, 8 >> s, 16, WIDE), BF) for s in range(4)],
            vmem((4, 16, WIDE), F32),
            vmem((3, 16, HALO), F32), vmem((3, 16, HALO), F32),
            vmem((4, 16, TW), F32), vmem((4, 32, 16, 256), BF),
            dma((4, 2)), dma((4, 2)), dma((4, 2)), dma((4, 4)), dma((4, 4)), dma((4,)), dma((4,)),
            dma((2, 4, 5)), dma((2, 4, 5)),
        ],
        compiler_params=pltpu.CompilerParams(
            collective_id=1, has_side_effects=True, vmem_limit_bytes=32 * MB),
        cost_estimate=pl.CostEstimate(flops=0, bytes_accessed=60 * MB, transcendentals=0),
        name="reduce_all",
    )(g, join)


def local(obj, probe, amps, rows, cols):
    total = rows.shape[0] * lax.axis_size("obj") * lax.axis_size("pat")
    y, pat = lax.axis_index("obj"), lax.axis_index("pat")
    pos = jnp.pad(jnp.stack([rows, cols]), ((0, 6), (0, 125)))[None]
    split = splitter()
    main, halo, spots = gather(obj, pos, jnp.asarray(split))
    g = work(rows, cols, main, halo, probe, amps, jnp.asarray(split))
    first = jnp.stack([pat * OWN, (y > 0).astype(jnp.int32)])
    light = light_sum(spots[0, :, :4, :3].reshape(-1), first, probe)
    light = light.transpose(1, 0, 2).reshape(1, OWN, TW)
    own, probe_sum = reduce_all(g, jnp.asarray(split.T))
    obj_step = own.reshape(2, OWN, TW) / (light + 1.0)
    probe_grad = probe_sum.astype(F32) * (1.0 / math.sqrt(total))
    return (obj_step, probe_grad)


def solution(mesh):
    placed = (
        P(None, "pat", "obj"),
        P(),
        P(("obj", "pat"), None, None),
        P(("obj", "pat")),
        P(("obj", "pat")),
    )
    return jax.shard_map(
        local, mesh=mesh, in_specs=placed, out_specs=(P(None, "pat", "obj"), P()), check_vma=False
    )
```

```python
import functools
import math

import jax
import jax.numpy as jnp
import ml_dtypes
import numpy as np
from jax import lax
from jax.experimental import pallas as pl
from jax.experimental.pallas import tpu as pltpu
from jax.sharding import PartitionSpec as P

PX = 512
HALO = 256
H = 768
TW = 1024
WIDE = TW + HALO
OWN = 24
BF = jnp.bfloat16
F32 = jnp.float32
MESH = pl.DeviceIdType.MESH
DIMS = ("xa", "za", "xb", "zb")
MB = 1 << 20


def bits_of(pat):
    x, z = (pat // 2) % 4, pat // 8
    return {
        "core": pat % 2,
        "xa": (x // 2 + x) % 2,
        "xb": x // 2,
        "za": (z // 2 + z) % 2,
        "zb": z // 2,
    }


def partner_of(pat, dim):
    core, x, z = pat % 2, (pat // 2) % 4, pat // 8
    if dim == "core":
        core = 1 - core
    elif dim == "xa":
        x = x + 1 - 2 * (x % 2)
    elif dim == "xb":
        x = 3 - x
    elif dim == "za":
        z = z + 1 - 2 * (z % 2)
    else:
        z = 3 - z
    return (z * 4 + x) * 2 + core


def order(part):
    return [DIMS[(part + k) % 4] for k in range(4)]


def gather_place(pat, part):
    bits = bits_of(pat)
    return bits["core"] * 16 + sum(bits[d] * 2**k for k, d in enumerate(order(part)))


def scatter_place(pat, part):
    bits = bits_of(pat)
    return bits["core"] * 16 + sum(bits[d] * 2 ** (3 - k) for k, d in enumerate(order(part)))


def ring_place(pat, layer):
    core, x, z = pat % 2, (pat // 2) % 4, pat // 8
    return core * 16 + (x * 4 + z if layer == 0 else z * 4 + x)


def along(pat, axis, k):
    core, x, z = pat % 2, (pat // 2) % 4, pat // 8
    if axis == "x":
        x = (x + k) % 4
    else:
        z = (z + k) % 4
    return (z * 4 + x) * 2 + core


def greet(peers):
    barrier = pltpu.get_barrier_semaphore()
    for peer in peers:
        pl.semaphore_signal(barrier, inc=1, device_id=peer, device_id_type=MESH)
    pl.semaphore_wait(barrier, len(peers))


class Doubling:
    def __init__(self, buf, part, me, sems):
        self.buf, self.part, self.sems = buf, part, sems
        self.y, self.pat = me
        self.place = gather_place(self.pat, part)
        self.pending = []

    def copy(self, src, dst, kind, slot, dim):
        send, recv = self.sems
        peer = (self.y, partner_of(self.pat, dim))
        made = pltpu.make_async_remote_copy(
            src_ref=src, dst_ref=dst,
            send_sem=send.at[kind, self.part, slot], recv_sem=recv.at[kind, self.part, slot],
            device_id=peer, device_id_type=MESH,
        )
        made.start()
        return made

    def base(self, step):
        return self.place - self.place % 2**step

    def first(self, src):
        mine = self.buf.at[self.part, pl.ds(self.place, 1)]
        self.ici = self.copy(src, mine, 0, 0, order(self.part)[0])
        self.pending.append(self.copy(src, mine, 1, 0, "core"))

    def step(self, s):
        self.ici.wait_recv()
        self.pending_send(self.ici)
        size = 2**s
        held = self.base(s)
        bit = (held // size) % 2
        came = held + size - 2 * size * bit
        if s < 3:
            full = self.buf.at[self.part, pl.ds(self.base(s + 1), 2 * size)]
            nxt = self.copy(full, full, 0, s + 1, order(self.part)[s + 1])
        got = self.buf.at[self.part, pl.ds(came, size)]
        self.pending.append(self.copy(got, got, 1, s + 1, "core"))
        if s < 3:
            self.ici = nxt

    def pending_send(self, made):
        self.sent = getattr(self, "sent", [])
        self.sent.append(made)

    def finish(self):
        for made in self.sent:
            made.wait_send()
        for made in self.pending:
            made.wait()


def gather_kernel(obj_ref, pos_ref, split_ref, main_ref, halo_ref, spots_ref, mine, edge, masked, pos_in, pos_all,
                  msend, mrecv, hsend, hrecv, psend, precv, esem, lsem):
    y, pat = lax.axis_index("obj"), lax.axis_index("pat")
    rows = lax.axis_size("obj")
    left, right = (y + rows - 1) % rows, (y + 1) % rows
    greet([(left, pat), (right, pat)] + [(y, partner_of(pat, d)) for d in DIMS + ("core",)])
    send_pos = pltpu.make_async_remote_copy(
        src_ref=pos_ref, dst_ref=pos_in,
        send_sem=esem.at[2], recv_sem=esem.at[3], device_id=(right, pat), device_id_type=MESH,
    )
    send_pos.start()
    mains = [Doubling(main_ref, p, (y, pat), (msend, mrecv)) for p in range(4)]
    halos = [Doubling(halo_ref, p, (y, pat), (hsend, hrecv)) for p in range(3)]
    spots = Doubling(spots_ref, 0, (y, pat), (psend, precv))
    own = []
    for p, part in enumerate(mains):
        here = pl.ds(p * 256, 256)
        mine[0, :, here] = dot(obj_ref[0, :, here], split_ref[...]).astype(BF)
        if p == 0:
            send_edge = pltpu.make_async_remote_copy(
                src_ref=mine.at[:, :, here], dst_ref=edge,
                send_sem=esem.at[0], recv_sem=esem.at[1], device_id=(left, pat), device_id_type=MESH,
            )
            send_edge.start()
        part.first(mine.at[:, :, here])
    for p, part in enumerate(mains):
        own.append(pltpu.make_async_copy(
            mine.at[:, :, pl.ds(p * 256, 256)], main_ref.at[p, pl.ds(part.place, 1)], lsem.at[p]))
        own[-1].start()
    send_edge.wait_recv()
    masked[...] = jnp.where(y == rows - 1, jnp.zeros_like(masked), edge[...])
    for p, part in enumerate(halos):
        part.first(masked.at[:, pl.ds(p * 16, 16)])
    for p, part in enumerate(halos):
        own.append(pltpu.make_async_copy(
            masked.at[:, pl.ds(p * 16, 16)], halo_ref.at[p, pl.ds(part.place, 1)], lsem.at[4 + p]))
        own[-1].start()
    send_pos.wait_recv()
    line = lax.broadcasted_iota(jnp.int32, (1, 8, 128), 1)
    pos_all[...] = jnp.where(line < 2, pos_ref[...], pltpu.roll(pos_in[...], 2, 1))
    spots.first(pos_all)
    own.append(pltpu.make_async_copy(pos_all, spots_ref.at[0, pl.ds(spots.place, 1)], lsem.at[7]))
    own[-1].start()
    for made in own:
        made.wait()
    for s in range(4):
        for part in mains + halos + [spots]:
            part.step(s)
    for part in mains + halos + [spots]:
        part.finish()
    send_edge.wait_send()
    send_pos.wait_send()


def gather(obj, pos, split):
    anywhere = pl.BlockSpec(memory_space=pl.ANY)
    dma = pltpu.SemaphoreType.DMA
    return pl.pallas_call(
        gather_kernel,
        out_shape=[
            jax.ShapeDtypeStruct((4, 32, 48, 256), BF),
            jax.ShapeDtypeStruct((3, 32, 16, 256), BF),
            jax.ShapeDtypeStruct((1, 32, 8, 128), jnp.int32),
        ],
        in_specs=[pl.BlockSpec(memory_space=pltpu.VMEM)] * 3,
        out_specs=[anywhere] * 3,
        scratch_shapes=[
            pltpu.VMEM((1, 48, TW), BF),
            pltpu.VMEM((1, 48, HALO), BF),
            pltpu.VMEM((1, 48, HALO), BF),
            pltpu.VMEM((1, 8, 128), jnp.int32),
            pltpu.VMEM((1, 8, 128), jnp.int32),
            dma((2, 4, 5)), dma((2, 4, 5)), dma((2, 3, 5)), dma((2, 3, 5)), dma((2, 1, 5)), dma((2, 1, 5)),
            dma((4,)), dma((8,)),
        ],
        compiler_params=pltpu.CompilerParams(collective_id=0, has_side_effects=True),
        cost_estimate=pl.CostEstimate(flops=0, bytes_accessed=60 * MB, transcendentals=0),
        name="gather",
    )(obj.reshape(1, 48, TW), pos, split)


def tables():
    index = np.arange(PX)
    angle = (index[:, None] * index[None, :] % PX) * (2.0 * np.pi / PX)
    real = (np.cos(angle) / np.sqrt(PX)).astype(ml_dtypes.bfloat16)
    imag = (-np.sin(angle) / np.sqrt(PX)).astype(ml_dtypes.bfloat16)
    low = np.arange(256)
    sorted_low = np.concatenate([low[::2], low[1::2]])
    even, odd = index[::2], index[1::2]

    def left(re, im, rows, cols):
        pick = np.ix_(rows, cols)
        return np.block([[re[pick], -im[pick]], [im[pick], re[pick]]])

    def right(re, im, rows, cols):
        pick = np.ix_(rows, cols)
        return np.block([[re[pick], im[pick]], [-im[pick], re[pick]]])

    return np.stack([
        left(real, imag, sorted_low, even), left(real, imag, sorted_low, odd),
        right(real, imag, even, low), right(real, imag, odd, low),
        left(real, -imag, sorted_low, even), left(real, -imag, sorted_low, odd),
        right(real, -imag, low, even), right(real, -imag, low, odd),
    ])


def splitter():
    k = np.arange(256)
    return (np.arange(256)[:, None] == 2 * (k % 128) + k // 128).astype(ml_dtypes.bfloat16)


def dot(a, b):
    return jnp.dot(a, b, preferred_element_type=F32)


def moved(x, pick):
    high = x.astype(BF)
    rest = x - high.astype(F32)
    mid = rest.astype(BF)
    low = (rest - mid.astype(F32)).astype(BF)
    return dot(high, pick) + dot(mid, pick) + dot(low, pick)


SLABS = 6
ROWS = H + 8


def work_kernel(rows_ref, cols_ref, main, halo, probe_ref, amps_ref, tab_ref, split, out_main, out_spill, out_probe,
                tile, grad, plain, probe, amps, tab, pacc, patch, stack, flat, sems):
    loads = {}

    def load(name, src, dst, slot):
        loads[name] = pltpu.make_async_copy(src, dst, sems.at[slot])
        loads[name].start()

    load("probe", probe_ref, plain, 0)
    load("tab", tab_ref, tab, 1)
    for i in range(3):
        for j in range(4):
            load(("amps", i, j), amps_ref.at[i, :, pl.ds(j * 128, 128)], amps.at[i, j, pl.ds(0, PX)], 2 + i * 4 + j)

    @pl.loop(0, ROWS, step=8)
    def _(r):
        grad[:, :, :, pl.ds(pl.multiple_of(r, 8), 8), :] = jnp.zeros((2, 2, SLABS, 8, 128), F32)

    @pl.loop(0, PX, step=64)
    def _(r):
        pacc[:, :, :, pl.ds(pl.multiple_of(r, 64), 64), :] = jnp.zeros((2, 2, 2, 64, 128), F32)

    loads["probe"].wait()
    for layer in range(2):
        @pl.loop(0, PX, step=256)
        def _(r):
            here = pl.ds(pl.multiple_of(r, 256), 256)
            for j in range(2):
                parted = moved(plain[layer, here, j * 256:(j + 1) * 256], split[...])
                for q in range(2):
                    probe[layer, q, j, here] = parted[:, q * 128:(q + 1) * 128]

    @pl.loop(0, 32)
    def _(o):
        at = pl.multiple_of(o * OWN, 8)
        for p in range(4):
            block = main[p, gather_place(o, p)].astype(F32)
            for layer in range(2):
                for q in range(2):
                    tile[layer, q, p, pl.ds(at, OWN)] = block[layer * OWN:(layer + 1) * OWN, q * 128:(q + 1) * 128]
        part = [halo[p, gather_place(o, p)].astype(F32) for p in range(3)]
        for q in range(2):
            cs = slice(q * 128, (q + 1) * 128)
            tile[0, q, 4, pl.ds(at, 16)] = part[0][:, cs]
            tile[0, q, 4, pl.ds(at + 16, 8)] = part[1][:8, cs]
            tile[1, q, 4, pl.ds(at, 8)] = part[1][8:, cs]
            tile[1, q, 4, pl.ds(at + 8, 16)] = part[2][:, cs]

    loads["tab"].wait()
    for i in range(3):
        for j in range(4):
            loads["amps", i, j].wait()
    lane = lax.broadcasted_iota(jnp.int32, (32, 128), 1)

    @pl.loop(0, 3)
    def _(slot):
        row, col = rows_ref[slot], cols_ref[slot]
        places = []
        for q in range(2):
            start = (col + q) // 2
            places.append(((col + q) % 2, start // 128, start % 128))

        for t in range(2):
            @pl.loop(0, 8)
            def _(i):
                i32 = pl.multiple_of(i * 32, 32)
                here = pl.ds(t + i * 64, 32, stride=2)
                there = pl.ds(row + t + i * 64, 32, stride=2)
                for q, (plane, b, m) in enumerate(places):
                    got = []
                    for layer in range(2):
                        turned = [pltpu.roll(tile[layer, plane, b + j, there, :], (128 - m) % 128, 1) for j in range(3)]
                        got.append([jnp.where(lane < 128 - m, turned[j], turned[j + 1]) for j in range(2)])
                    for j in range(2):
                        re, im = got[0][j], got[1][j]
                        pr, pi = probe[0, q, j, here, :], probe[1, q, j, here, :]
                        patch[0, t, q, j, pl.ds(i32, 32)] = re
                        patch[1, t, q, j, pl.ds(i32, 32)] = im
                        cs = slice(j * 128, (j + 1) * 128)
                        stack[t, q, pl.ds(i32, 32), cs] = (pr * re - pi * im).astype(BF)
                        stack[t, q, pl.ds(256 + i32, 32), cs] = (pr * im + pi * re).astype(BF)

        def spread(to, which, total, other):
            for part in range(2):
                for upper, value in ((0, total), (1, other)):
                    for t in range(2):
                        at = part * 256 + t * 128
                        to[which, t * 256 + upper * 128:t * 256 + (upper + 1) * 128, part * 256:(part + 1) * 256] = (
                            value[at:at + 128].astype(BF))

        @pl.loop(0, 2)
        def _(q):
            even, odd = dot(tab[0], stack[0, q]), dot(tab[1], stack[1, q])
            spread(flat, q, even + odd, even - odd)

        @pl.loop(0, 2)
        def _(t):
            here = pl.ds(pl.multiple_of(t * 256, 256), 256)
            even, odd = dot(flat[0, here], tab[2]), dot(flat[1, here], tab[3])
            for upper, wave in ((0, even + odd), (1, even - odd)):
                for j in range(2):
                    re, im = wave[:, j * 128:(j + 1) * 128], wave[:, 256 + j * 128:256 + (j + 1) * 128]
                    amp = amps[slot, 2 * upper + j, pl.ds(t, 256, stride=2), :]
                    ratio = amp * lax.rsqrt(re * re + im * im + 1.0)
                    cs = slice(j * 128, (j + 1) * 128)
                    stack[t, upper, 0:256, cs] = (re * ratio - re).astype(BF)
                    stack[t, upper, 256:512, cs] = (im * ratio - im).astype(BF)

        halves = []
        for upper in range(2):
            even, odd = dot(tab[4], stack[0, upper]), dot(tab[5], stack[1, upper])
            halves.append((even + odd, even - odd))
        spread(flat, 0, halves[0][0] + halves[1][0], halves[0][1] + halves[1][1])
        spread(flat, 1, halves[0][0] - halves[1][0], halves[0][1] - halves[1][1])

        @pl.loop(0, 2)
        def _(t):
            here = pl.ds(pl.multiple_of(t * 256, 256), 256)
            deltas = dot(flat[0, here], tab[6]), dot(flat[1, here], tab[7])
            for i in range(8):
                at = pl.ds(t + i * 64, 32, stride=2)
                there = pl.ds(row + t + i * 64, 32, stride=2)
                rs = slice(i * 32, (i + 1) * 32)
                for q, (plane, b, m) in enumerate(places):
                    turned = [[], []]
                    for j in range(2):
                        dr = deltas[q][rs, j * 128:(j + 1) * 128]
                        di = deltas[q][rs, 256 + j * 128:256 + (j + 1) * 128]
                        pr, pi = probe[0, q, j, at, :], probe[1, q, j, at, :]
                        qr, qi = patch[0, t, q, j, rs], patch[1, t, q, j, rs]
                        pacc[0, q, j, at, :] += qr * dr + qi * di
                        pacc[1, q, j, at, :] += qr * di - qi * dr
                        turned[0].append(pltpu.roll(pr * dr + pi * di, m, 1))
                        turned[1].append(pltpu.roll(pr * di - pi * dr, m, 1))
                    for layer in range(2):
                        one, two = turned[layer]
                        grad[layer, plane, b, there, :] += jnp.where(lane >= m, one, 0.0)
                        grad[layer, plane, b + 1, there, :] += jnp.where(lane >= m, two, one)
                        grad[layer, plane, b + 2, there, :] += jnp.where(lane < m, two, 0.0)

    @pl.loop(0, 32)
    def _(o):
        at = pl.multiple_of(o * OWN, 8)
        spot = [scatter_place(o, p) for p in range(4)]
        for c in range(5):
            for q in range(2):
                low = grad[0, q, c, pl.ds(at, OWN)]
                high = grad[1, q, c, pl.ds(at, OWN)]
                parts = (low[:16], jnp.concatenate([low[16:], high[:8]], axis=0), high[8:])
                for p in range(3):
                    if c < 4:
                        cs = slice(c * 256 + q * 128, c * 256 + (q + 1) * 128)
                        out_main[p, spot[p], :, cs] = parts[p].astype(BF)
                    else:
                        cs = slice(q * 128, (q + 1) * 128)
                        out_spill[0, spot[3], p * 16:(p + 1) * 16, cs] = parts[p].astype(BF)
        rs = pl.ds(pl.multiple_of(o * 16, 16), 16)
        for layer in range(2):
            for j in range(2):
                for q in range(2):
                    c = j * 256 + q * 128
                    out_probe[layer, ring_place(o, layer), :, c:c + 128] = pacc[layer, q, j, rs].astype(BF)


def work(rows, cols, main, halo, probe, amps, split):
    smem = pl.BlockSpec(memory_space=pltpu.SMEM)
    anywhere = pl.BlockSpec(memory_space=pl.ANY)
    whole = pl.BlockSpec(memory_space=pltpu.VMEM)
    vmem = pltpu.VMEM
    return pl.pallas_call(
        work_kernel,
        out_shape=[
            jax.ShapeDtypeStruct((3, 32, 16, TW), BF),
            jax.ShapeDtypeStruct((1, 32, 48, HALO), BF),
            jax.ShapeDtypeStruct((2, 32, 16, PX), BF),
        ],
        in_specs=[smem] * 2 + [whole] * 2 + [anywhere] * 3 + [whole],
        out_specs=[whole] * 3,
        scratch_shapes=[
            vmem((2, 2, SLABS, ROWS, 128), F32), vmem((2, 2, SLABS, ROWS, 128), F32),
            vmem((2, PX, PX), F32), vmem((2, 2, 2, PX + 8, 128), F32), vmem((3, 4, PX + 8, 128), F32),
            vmem((8, PX, PX), BF),
            vmem((2, 2, 2, PX + 8, 128), F32), vmem((2, 2, 2, 2, 256, 128), F32),
            vmem((2, 2, PX, 256), BF), vmem((2, PX, PX), BF),
            pltpu.SemaphoreType.DMA((14,)),
        ],
        compiler_params=pltpu.CompilerParams(vmem_limit_bytes=50 * MB),
        name="work",
    )(rows, cols, main, halo, probe, amps, jnp.asarray(tables()), split)


class Light:
    def __init__(self, spots, probe, lit, acc, spill_acc, first):
        self.spots, self.probe, self.lit, self.acc, self.spill_acc, self.first = spots, probe, lit, acc, spill_acc, first

    def prepare(self):
        for j in (0, 5):
            self.lit[j] = jnp.zeros((PX + 2 * OWN + 8, 128), F32)
        for j in range(4):
            self.lit[j + 1, 0:OWN] = jnp.zeros((OWN, 128), F32)
            self.lit[j + 1, PX + OWN:] = jnp.zeros((OWN + 8, 128), F32)

            @pl.loop(0, PX, step=64)
            def _(r):
                here = pl.ds(pl.multiple_of(r, 64), 64)
                cs = slice(j * 128, (j + 1) * 128)
                pr, pi = self.probe[0, here, cs], self.probe[1, here, cs]
                self.lit[j + 1, pl.ds(pl.multiple_of(r + OWN, 8), 64)] = pr * pr + pi * pi

        self.acc[...] = jnp.zeros_like(self.acc)
        self.spill_acc[...] = jnp.zeros_like(self.spill_acc)

    def add(self, begin, end):
        lane = lax.broadcasted_iota(jnp.int32, (8, 128), 1)

        @pl.loop(begin, end)
        def _(o):
            for k in range(3):
                for which, to, slabs, shift in ((0, self.acc, 8, 0), (1, self.spill_acc, 2, 8)):
                    row = self.spots[o * 12 + which * 6 + k]
                    col = self.spots[o * 12 + which * 6 + 3 + k]
                    start = jnp.clip(self.first - row + OWN, 0, PX + OWN)
                    b, m = col // 128, col % 128
                    last = [None] * 3
                    for j in range(-1, slabs):
                        slab = jnp.clip(j + shift - b + 1, 0, 5)
                        for t in range(3):
                            here = pltpu.roll(self.lit[slab, pl.ds(start + t, 8, stride=3), :], m, 1)
                            if j >= 0:
                                to[t, j] += jnp.where(lane >= m, here, last[t])
                            last[t] = here

    def result(self, y, out):
        for j in range(8):
            for t in range(3):
                value = self.acc[t, j]
                if j < 2:
                    value = value + jnp.where(y == 0, 0.0, self.spill_acc[t, j])
                out[j, pl.ds(t, 8, stride=3), :] = value


class Halving:
    def __init__(self, src, part, rotation, me, came, accs, sends, recvs, sems):
        self.src, self.part, self.came, self.accs, self.sends, self.recvs = src, part, came, accs, sends, recvs
        self.y, self.pat = me
        self.core = self.pat % 2
        self.dims = order(rotation)
        self.bits = [bits_of(self.pat)[d] for d in self.dims]
        self.csend, self.crecv, self.rsend, self.rrecv = sems
        self.made = []

    def swap(self, half):
        at = (1 - self.bits[0]) * 8 if half == 0 else self.bits[0] * 8
        made = pltpu.make_async_remote_copy(
            src_ref=self.src.at[self.part, pl.ds((1 - self.core) * 16 + at, 8)],
            dst_ref=self.came.at[self.part, half],
            send_sem=self.csend.at[self.part, half], recv_sem=self.crecv.at[self.part, half],
            device_id=(self.y, partner_of(self.pat, "core")), device_id_type=MESH)
        made.start()
        self.made.append(made)

    def start(self, s):
        made = pltpu.make_async_remote_copy(
            src_ref=self.sends[s].at[self.part], dst_ref=self.recvs[s].at[self.part],
            send_sem=self.rsend.at[self.part, s], recv_sem=self.rrecv.at[self.part, s],
            device_id=(self.y, partner_of(self.pat, self.dims[s])), device_id_type=MESH)
        made.start()
        self.made.append(made)
        self.last_made = made

    def first(self, half):
        self.made[half].wait_recv()
        at = self.core * 16 + ((1 - self.bits[0]) * 8 if half == 0 else self.bits[0] * 8)

        @pl.loop(0, 8)
        def _(j):
            total = self.src[self.part, at + j].astype(F32) + self.came[self.part, half, j].astype(F32)
            if half == 0:
                self.sends[0][self.part, j] = total.astype(BF)
            else:
                self.accs[0][self.part, j] = total

        if half == 0:
            self.start(0)

    def give(self, s):
        self.last_made.wait_recv()
        size, bit = 8 >> s, self.bits[s]

        @pl.loop(0, size)
        def _(j):
            at = (1 - bit) * size + j
            self.sends[s][self.part, j] = (
                self.accs[s - 1][self.part, at] + self.recvs[s - 1][self.part, at].astype(F32)).astype(BF)

        self.start(s)

    def keep(self, s):
        size, bit = 8 >> s, self.bits[s]

        @pl.loop(0, size)
        def _(j):
            at = bit * size + j
            self.accs[s][self.part, j] = (
                self.accs[s - 1][self.part, at] + self.recvs[s - 1][self.part, at].astype(F32))

    def total(self):
        self.last_made.wait_recv()
        return self.accs[3][self.part, 0] + self.recvs[3][self.part, 0].astype(F32)

    def finish(self):
        for made in self.made:
            made.wait_send()


def halving_scratch(parts, rows, columns):
    return [
        pltpu.VMEM((parts, 2, 8, rows, columns), BF),
        *[pltpu.VMEM((parts, 8 >> s, rows, columns), F32) for s in range(4)],
        *[pltpu.VMEM((parts, 8 >> s, rows, columns), BF) for s in range(4)],
        *[pltpu.VMEM((parts, 8 >> s, rows, columns), BF) for s in range(4)],
        *[pltpu.SemaphoreType.DMA((parts, n)) for n in (2, 2, 4, 4)],
    ]


def halvings(src, parts, rotations, me, refs):
    came, accs, sends, recvs, sems = refs[0], refs[1:5], refs[5:9], refs[9:13], refs[13:17]
    return [Halving(src, p, rotations[p], me, came, accs, sends, recvs, sems) for p in range(parts)]


class Rings:
    def __init__(self, src, me, came, keep, s1, r1, s2, r2, fin, pbuf, sems):
        self.src, self.came, self.keep, self.pbuf = src, came, keep, pbuf
        self.s1, self.r1, self.s2, self.r2, self.fin = s1, r1, s2, r2, fin
        self.y, self.pat = me
        self.core = self.pat % 2
        self.sibling = partner_of(self.pat, "core")
        self.sems, self.made, self.used = sems, {}, 0
        x, z = (self.pat // 2) % 4, self.pat // 8
        self.at = ((x, z), (z, x))
        self.axes = (("x", "z"), ("z", "x"))

    def send(self, name, src, dst, pat):
        send, recv = self.sems
        made = pltpu.make_async_remote_copy(
            src_ref=src, dst_ref=dst, send_sem=send.at[self.used], recv_sem=recv.at[self.used],
            device_id=(self.y, pat), device_id_type=MESH)
        made.start()
        self.made[name] = made
        self.used += 1

    def swap(self):
        for h in range(2):
            self.send(("swap", h), self.src.at[h, pl.ds((1 - self.core) * 16, 16)], self.came.at[h], self.sibling)

    def ring_one(self):
        for h in range(2):
            self.made["swap", h].wait_recv()
            f = self.at[h][0]

            @pl.loop(0, 4)
            def _(j):
                at = f * 4 + j
                self.keep[h, j] = self.src[h, self.core * 16 + at].astype(F32) + self.came[h, at].astype(F32)

            for k in range(1, 4):
                to = (f + k) % 4

                @pl.loop(0, 4)
                def _(j):
                    at = to * 4 + j
                    total = self.src[h, self.core * 16 + at].astype(F32) + self.came[h, at].astype(F32)
                    self.s1[h, k - 1, j] = total.astype(BF)

                self.send(("one", h, k), self.s1.at[h, k - 1], self.r1.at[h, k - 1],
                          along(self.pat, self.axes[h][0], k))

    def ring_two(self):
        for h in range(2):
            for k in range(1, 4):
                self.made["one", h, k].wait_recv()
            g = self.at[h][1]

            def total(j):
                return self.keep[h, j] + sum(self.r1[h, k, j].astype(F32) for k in range(3))

            for k in range(1, 4):
                self.s2[h, k - 1] = total((g + k) % 4).astype(BF)
                self.send(("two", h, k), self.s2.at[h, k - 1], self.r2.at[h, k - 1],
                          along(self.pat, self.axes[h][1], k))
            self.fin[h] = total(g)

    def total(self, h):
        for k in range(1, 4):
            self.made["two", h, k].wait_recv()
        return self.fin[h] + sum(self.r2[h, k].astype(F32) for k in range(3))

    def gather_one(self, values):
        for h in range(2):
            place = ring_place(self.pat, h)
            self.pbuf[h, pl.ds(place, 1)] = values[h].reshape(1, 16, PX)
            mine = self.pbuf.at[h, pl.ds(place, 1)]
            for k in range(1, 4):
                self.send(("three", h, k), mine, mine, along(self.pat, self.axes[h][1], k))

    def gather_two(self):
        for h in range(2):
            for k in range(1, 4):
                self.made["three", h, k].wait_recv()
            mine = self.pbuf.at[h, pl.ds(self.core * 16 + self.at[h][0] * 4, 4)]
            for k in range(1, 4):
                self.send(("four", h, k), mine, mine, along(self.pat, self.axes[h][0], k))
            self.send(("near", h, 0), mine, mine, self.sibling)

    def gather_three(self):
        for k in (1, 3, 2):
            for h in range(2):
                self.made["four", h, k].wait_recv()
                came = self.pbuf.at[h, pl.ds(self.core * 16 + (self.at[h][0] + 4 - k) % 4 * 4, 4)]
                self.send(("near", h, k), came, came, self.sibling)

    def finish(self):
        for name, made in self.made.items():
            if name[0] == "near":
                made.wait_recv()
        for made in self.made.values():
            made.wait_send()


RING_SENDS = 2 + 4 * 6 + 8


def reduce_kernel(spots, main_ref, spill_ref, sum_ref, probe_ref, join_ref, obj_out, probe_out, *refs):
    y, pat = lax.axis_index("obj"), lax.axis_index("pat")
    me = (y, pat)
    rows = lax.axis_size("obj")
    mains = halvings(main_ref, 3, (0, 1, 2), me, refs[0:17])
    spills = halvings(spill_ref, 1, (3,), me, refs[17:34])
    (spill, spilled, ypro, came, keep, s1, r1, s2, r2, fin, pbuf, lit, acc, spill_acc, lights,
     ysend, yrecv, psend, precv) = refs[34:]
    rings = Rings(sum_ref, me, came, keep, s1, r1, s2, r2, fin, pbuf, (psend, precv))
    light = Light(spots, probe_ref, lit, acc, spill_acc, pat * OWN)
    others = [((y + k) % rows, pat) for k in (1, 2, 3)]
    near = [(y, along(pat, axis, k)) for axis in ("x", "z") for k in (1, 2, 3)]
    greet(others + near + [(y, partner_of(pat, "core"))])
    objs = spills + mains

    def onward(s):
        for part in objs:
            part.give(s)
        for part in objs:
            part.keep(s)

    rings.swap()
    for half in range(2):
        for part in objs:
            part.swap(half)
    light.prepare()
    rings.ring_one()
    for half in range(2):
        for part in objs:
            part.first(half)
    light.add(0, 8)
    rings.ring_two()
    onward(1)
    light.add(8, 16)
    for h in range(2):
        ypro[pl.ds(y, 1), :, h * PX:(h + 1) * PX] = rings.total(h).reshape(1, 16, PX)
    mine = ypro.at[pl.ds(y, 1)]
    across = []
    for k, other in enumerate(others):
        across.append(pltpu.make_async_remote_copy(
            src_ref=mine, dst_ref=mine, send_sem=ysend.at[k], recv_sem=yrecv.at[k],
            device_id=other, device_id_type=MESH))
        across[-1].start()
    onward(2)
    for made in across:
        made.wait_recv()
    total = (ypro[0] + ypro[1] + ypro[2] + ypro[3]).astype(BF)
    joined = [dot(total[:, c * 256:(c + 1) * 256], join_ref[...]).astype(BF) for c in range(4)]
    rings.gather_one([jnp.concatenate(joined[2 * h:2 * h + 2], axis=1) for h in range(2)])
    light.add(16, 24)
    onward(3)
    rings.gather_two()
    spill[...] = spills[0].total()
    over = pltpu.make_async_remote_copy(
        src_ref=spill, dst_ref=spilled, send_sem=ysend.at[3], recv_sem=yrecv.at[3],
        device_id=others[0], device_id_type=MESH)
    over.start()
    light.add(24, 32)
    rings.gather_three()
    light.result(y, lights)
    totals = [part.total() for part in mains]
    over.wait_recv()
    chunks = []
    for c in range(4):
        whole = jnp.concatenate([total[:, c * 256:(c + 1) * 256] for total in totals], axis=0)
        chunks.append(whole + jnp.where(y == 0, 0.0, spilled[...]) if c == 0 else whole)
    joined = moved(jnp.concatenate(chunks, axis=0), join_ref[...])
    for j in range(8):
        here = joined[j // 2 * 48:(j // 2 + 1) * 48, (j % 2) * 128:(j % 2 + 1) * 128]
        under = lights[j] + 1.0
        for layer in range(2):
            obj_out[layer * OWN:(layer + 1) * OWN, j * 128:(j + 1) * 128] = here[layer * OWN:(layer + 1) * OWN] / under
    rings.finish()
    for o in range(32):
        for h in range(2):
            probe_out[h, o * 16:(o + 1) * 16] = pbuf[h, ring_place(o, h)]
    for part in objs:
        part.finish()
    for made in across + [over]:
        made.wait_send()


def reduce_all(spots, main, spill, sums, probe, join):
    dma = pltpu.SemaphoreType.DMA
    vmem = pltpu.VMEM
    whole = pl.BlockSpec(memory_space=pltpu.VMEM)
    return pl.pallas_call(
        reduce_kernel,
        out_shape=[jax.ShapeDtypeStruct((48, TW), F32), jax.ShapeDtypeStruct((2, PX, PX), BF)],
        in_specs=[pl.BlockSpec(memory_space=pltpu.SMEM)] + [whole] * 5,
        out_specs=[whole] * 2,
        scratch_shapes=[
            *halving_scratch(3, 16, TW), *halving_scratch(1, 48, HALO),
            vmem((48, HALO), F32), vmem((48, HALO), F32), vmem((4, 16, TW), F32),
            vmem((2, 16, 16, PX), BF), vmem((2, 4, 16, PX), F32),
            vmem((2, 3, 4, 16, PX), BF), vmem((2, 3, 4, 16, PX), BF),
            vmem((2, 3, 16, PX), BF), vmem((2, 3, 16, PX), BF),
            vmem((2, 16, PX), F32), vmem((2, 32, 16, PX), BF),
            vmem((6, PX + 2 * OWN + 8, 128), F32), vmem((3, 8, 8, 128), F32), vmem((3, 2, 8, 128), F32),
            vmem((8, OWN, 128), F32),
            dma((4,)), dma((4,)), dma((RING_SENDS,)), dma((RING_SENDS,)),
        ],
        compiler_params=pltpu.CompilerParams(
            collective_id=1, has_side_effects=True, vmem_limit_bytes=40 * MB),
        cost_estimate=pl.CostEstimate(flops=0, bytes_accessed=60 * MB, transcendentals=0),
        name="reduce_all",
    )(spots, main, spill, sums, probe, join)


def local(obj, probe, amps, rows, cols):
    total = rows.shape[0] * lax.axis_size("obj") * lax.axis_size("pat")
    pos = jnp.pad(jnp.stack([rows, cols]), ((0, 6), (0, 125)))[None]
    split = splitter()
    main, halo, spots = gather(obj, pos, jnp.asarray(split))
    sums = work(rows, cols, main, halo, probe, amps, jnp.asarray(split))
    own, probe_sum = reduce_all(spots[0, :, :4, :3].reshape(-1), *sums, probe, jnp.asarray(split.T))
    obj_step = own.reshape(2, OWN, TW)
    probe_grad = probe_sum.astype(F32) * (1.0 / math.sqrt(total))
    return (obj_step, probe_grad)


def solution(mesh):
    placed = (
        P(None, "pat", "obj"),
        P(),
        P(("obj", "pat"), None, None),
        P(("obj", "pat")),
        P(("obj", "pat")),
    )
    return jax.shard_map(
        local, mesh=mesh, in_specs=placed, out_specs=(P(None, "pat", "obj"), P()), check_vma=False
    )
```

```python
import functools
import math

import jax
import jax.numpy as jnp
import ml_dtypes
import numpy as np
from jax import lax
from jax.experimental import pallas as pl
from jax.experimental.pallas import tpu as pltpu
from jax.sharding import PartitionSpec as P

PX = 512
HALO = 256
H = 768
TW = 1024
WIDE = TW + HALO
OWN = 24
BF = jnp.bfloat16
F32 = jnp.float32
MESH = pl.DeviceIdType.MESH
DIMS = ("xa", "za", "xb", "zb")
MB = 1 << 20


def bits_of(pat):
    x, z = (pat // 2) % 4, pat // 8
    return {
        "core": pat % 2,
        "xa": (x // 2 + x) % 2,
        "xb": x // 2,
        "za": (z // 2 + z) % 2,
        "zb": z // 2,
    }


def partner_of(pat, dim):
    core, x, z = pat % 2, (pat // 2) % 4, pat // 8
    if dim == "core":
        core = 1 - core
    elif dim == "xa":
        x = x + 1 - 2 * (x % 2)
    elif dim == "xb":
        x = 3 - x
    elif dim == "za":
        z = z + 1 - 2 * (z % 2)
    else:
        z = 3 - z
    return (z * 4 + x) * 2 + core


def order(part):
    return [DIMS[(part + k) % 4] for k in range(4)]


def gather_place(pat, part):
    bits = bits_of(pat)
    return bits["core"] * 16 + sum(bits[d] * 2**k for k, d in enumerate(order(part)))


def scatter_place(pat, part):
    bits = bits_of(pat)
    return bits["core"] * 16 + sum(bits[d] * 2 ** (3 - k) for k, d in enumerate(order(part)))


def corner_of(pat, one, two):
    return partner_of(partner_of(pat, one), two)


def ring_place(pat, layer):
    core, x, z = pat % 2, (pat // 2) % 4, pat // 8
    return core * 16 + (x * 4 + z if layer == 0 else z * 4 + x)


def along(pat, axis, k):
    core, x, z = pat % 2, (pat // 2) % 4, pat // 8
    if axis == "x":
        x = (x + k) % 4
    else:
        z = (z + k) % 4
    return (z * 4 + x) * 2 + core


CORNERS = [(DIMS[k], DIMS[(k + 1) % 4]) for k in range(4)]


def greet(peers):
    barrier = pltpu.get_barrier_semaphore()
    for peer in peers:
        pl.semaphore_signal(barrier, inc=1, device_id=peer, device_id_type=MESH)
    pl.semaphore_wait(barrier, len(peers))


class Doubling:
    def __init__(self, buf, part, me, sems):
        self.buf, self.part, self.sems = buf, part, sems
        self.y, self.pat = me
        self.place = gather_place(self.pat, part)
        self.dims = order(part)
        self.made = {}

    def copy(self, name, src, dst, pat):
        send, recv = self.sems
        slot = len(self.made)
        made = pltpu.make_async_remote_copy(
            src_ref=src, dst_ref=dst, send_sem=send.at[self.part, slot], recv_sem=recv.at[self.part, slot],
            device_id=(self.y, pat), device_id_type=MESH,
        )
        made.start()
        self.made[name] = made

    def four(self, flip_two, flip_three):
        two, three = (self.place // 4) % 2, (self.place // 8) % 2
        two = 1 - two if flip_two else two
        three = 1 - three if flip_three else three
        return self.buf.at[self.part, pl.ds(self.place // 16 * 16 + three * 8 + two * 4, 4)]

    def near(self, name, ref):
        self.copy(name, ref, ref, partner_of(self.pat, "core"))

    def first(self, src):
        mine = self.buf.at[self.part, pl.ds(self.place, 1)]
        self.copy("a0", src, mine, partner_of(self.pat, self.dims[0]))
        self.copy("a1", src, mine, partner_of(self.pat, self.dims[1]))
        self.copy("a2", src, mine, corner_of(self.pat, self.dims[0], self.dims[1]))

    def second(self):
        for name in ("a0", "a1", "a2"):
            self.made[name].wait_recv()
        mine = self.four(False, False)
        self.copy("b", mine, mine, partner_of(self.pat, self.dims[2]))

    def third(self):
        mine = self.four(False, False)
        self.copy("c0", mine, mine, partner_of(self.pat, self.dims[3]))
        self.near("n0", mine)

    def fourth(self):
        self.made["b"].wait_recv()
        came = self.four(True, False)
        self.copy("c1", came, came, partner_of(self.pat, self.dims[3]))
        self.near("n1", came)

    def fifth(self, k):
        self.made[("c0", "c1")[k]].wait_recv()
        self.near(("n2", "n3")[k], self.four(k == 1, True))

    def finish(self):
        for name, made in self.made.items():
            made.wait_send()
            if name[0] == "n":
                made.wait_recv()


def gather_all(parts):
    for part in parts:
        part.second()
    for part in parts:
        part.third()
    for part in parts:
        part.fourth()
    for k in range(2):
        for part in parts:
            part.fifth(k)


def gather_kernel(obj_ref, rows_ref, cols_ref, split_ref, main_ref, halo_ref, spots_ref,
                  obj, split, at, mine, edge, masked, pos, pos_in, pos_all,
                  msend, mrecv, hsend, hrecv, psend, precv, esem, lsem):
    y, pat = lax.axis_index("obj"), lax.axis_index("pat")
    rows = lax.axis_size("obj")
    left, right = (y + rows - 1) % rows, (y + 1) % rows
    loads = [
        pltpu.make_async_copy(src, dst, lsem.at[8 + k])
        for k, (src, dst) in enumerate(
            ((obj_ref, obj), (split_ref, split), (rows_ref, at.at[0]), (cols_ref, at.at[1])))
    ]
    for made in loads:
        made.start()
    greet([(left, pat), (right, pat)] + [(y, partner_of(pat, d)) for d in DIMS + ("core",)]
          + [(y, corner_of(pat, *c)) for c in CORNERS])
    for made in loads:
        made.wait()
    mains = [Doubling(main_ref, p, (y, pat), (msend, mrecv)) for p in range(4)]
    halos = [Doubling(halo_ref, p, (y, pat), (hsend, hrecv)) for p in range(3)]
    spots = Doubling(spots_ref, 0, (y, pat), (psend, precv))
    own = []
    for p, part in enumerate(mains):
        here = pl.ds(p * 256, 256)
        mine[0, :, here] = dot(obj[0, :, here], split[...]).astype(BF)
        if p == 0:
            send_edge = pltpu.make_async_remote_copy(
                src_ref=mine.at[:, :, here], dst_ref=edge,
                send_sem=esem.at[0], recv_sem=esem.at[1], device_id=(left, pat), device_id_type=MESH,
            )
            send_edge.start()
        part.first(mine.at[:, :, here])
    line = lax.broadcasted_iota(jnp.int32, (1, 8, 128), 1)
    lane = lax.broadcasted_iota(jnp.int32, (1, 8, 128), 2)
    table = jnp.zeros((1, 8, 128), jnp.int32)
    for which in range(2):
        for k in range(3):
            table = jnp.where((line == which) & (lane == k), at[which, k], table)
    pos[...] = table
    send_pos = pltpu.make_async_remote_copy(
        src_ref=pos, dst_ref=pos_in,
        send_sem=esem.at[2], recv_sem=esem.at[3], device_id=(right, pat), device_id_type=MESH,
    )
    send_pos.start()
    for p, part in enumerate(mains):
        own.append(pltpu.make_async_copy(
            mine.at[:, :, pl.ds(p * 256, 256)], main_ref.at[p, pl.ds(part.place, 1)], lsem.at[p]))
        own[-1].start()
    send_edge.wait_recv()
    masked[...] = jnp.where(y == rows - 1, jnp.zeros_like(masked), edge[...])
    for p, part in enumerate(halos):
        part.first(masked.at[:, pl.ds(p * 16, 16)])
    for p, part in enumerate(halos):
        own.append(pltpu.make_async_copy(
            masked.at[:, pl.ds(p * 16, 16)], halo_ref.at[p, pl.ds(part.place, 1)], lsem.at[4 + p]))
        own[-1].start()
    send_pos.wait_recv()
    pos_all[...] = jnp.where(line < 2, pos[...], pltpu.roll(pos_in[...], 2, 1))
    spots.first(pos_all)
    own.append(pltpu.make_async_copy(pos_all, spots_ref.at[0, pl.ds(spots.place, 1)], lsem.at[7]))
    own[-1].start()
    for made in own:
        made.wait()
    parts = mains + halos + [spots]
    gather_all(parts)
    for part in parts:
        part.finish()
    send_edge.wait_send()
    send_pos.wait_send()


HBM = pl.BlockSpec(memory_space=pltpu.HBM)
VMEM = pl.BlockSpec(memory_space=pltpu.VMEM)


def gather(obj, rows, cols, split):
    dma = pltpu.SemaphoreType.DMA
    return pl.pallas_call(
        gather_kernel,
        out_shape=[
            jax.ShapeDtypeStruct((4, 32, 48, 256), BF),
            jax.ShapeDtypeStruct((3, 32, 16, 256), BF),
            jax.ShapeDtypeStruct((1, 32, 8, 128), jnp.int32),
        ],
        in_specs=[HBM] * 4,
        out_specs=[HBM] * 3,
        scratch_shapes=[
            pltpu.VMEM((1, 48, TW), BF),
            pltpu.VMEM((256, 256), BF),
            pltpu.SMEM((2, 3), jnp.int32),
            pltpu.VMEM((1, 48, TW), BF),
            pltpu.VMEM((1, 48, HALO), BF),
            pltpu.VMEM((1, 48, HALO), BF),
            pltpu.VMEM((1, 8, 128), jnp.int32),
            pltpu.VMEM((1, 8, 128), jnp.int32),
            pltpu.VMEM((1, 8, 128), jnp.int32),
            dma((4, 10)), dma((4, 10)), dma((3, 10)), dma((3, 10)), dma((1, 10)), dma((1, 10)),
            dma((4,)), dma((12,)),
        ],
        compiler_params=pltpu.CompilerParams(collective_id=0, has_side_effects=True, vmem_limit_bytes=62 * MB),
        cost_estimate=pl.CostEstimate(flops=0, bytes_accessed=60 * MB, transcendentals=0),
        name="gather",
    )(obj.reshape(1, 48, TW), rows, cols, split)


def tables():
    index = np.arange(PX)
    angle = (index[:, None] * index[None, :] % PX) * (2.0 * np.pi / PX)
    real = (np.cos(angle) / np.sqrt(PX)).astype(ml_dtypes.bfloat16)
    imag = (-np.sin(angle) / np.sqrt(PX)).astype(ml_dtypes.bfloat16)
    low = np.arange(256)
    sorted_low = np.concatenate([low[::2], low[1::2]])
    even, odd = index[::2], index[1::2]

    def left(re, im, rows, cols):
        pick = np.ix_(rows, cols)
        return np.block([[re[pick], -im[pick]], [im[pick], re[pick]]])

    def right(re, im, rows, cols):
        pick = np.ix_(rows, cols)
        return np.block([[re[pick], im[pick]], [-im[pick], re[pick]]])

    return np.stack([
        left(real, imag, sorted_low, even), left(real, imag, sorted_low, odd),
        right(real, imag, even, low), right(real, imag, odd, low),
        left(real, -imag, sorted_low, even), left(real, -imag, sorted_low, odd),
        right(real, -imag, low, even), right(real, -imag, low, odd),
    ])


def splitter():
    k = np.arange(256)
    return (np.arange(256)[:, None] == 2 * (k % 128) + k // 128).astype(ml_dtypes.bfloat16)


def dot(a, b):
    return jnp.dot(a, b, preferred_element_type=F32)


def moved(x, pick):
    high = x.astype(BF)
    rest = x - high.astype(F32)
    mid = rest.astype(BF)
    low = (rest - mid.astype(F32)).astype(BF)
    return dot(high, pick) + dot(mid, pick) + dot(low, pick)


SLABS = 6
ROWS = H + 8


def work_kernel(rows_hbm, cols_hbm, main_ref, halo_ref, probe_ref, amps_ref, tab_ref, split_ref, main_out, spill_out, probe_out,
                out_main, out_spill, out_probe, rows_ref, cols_ref, main, halo, split, tile, grad, probe, amps, tab, pacc, patch, exits, stack, flat, sems):
    loads = {}

    def load(name, src, dst, slot):
        loads[name] = pltpu.make_async_copy(src, dst, sems.at[slot])
        loads[name].start()

    plain = patch.at[1]
    for layer in range(2):
        for j in range(4):
            load(("probe", layer, j), probe_ref.at[layer, :, pl.ds(j * 128, 128)], plain.at[layer, j], layer * 4 + j)
    load("split", split_ref, split, 21)
    load("main", main_ref, main, 22)
    load("halo", halo_ref, halo, 23)
    load("rows", rows_hbm, rows_ref, 24)
    load("cols", cols_hbm, cols_ref, 25)
    load("tab", tab_ref, tab, 8)
    for i in range(3):
        for j in range(4):
            load(("amps", i, j), amps_ref.at[i, :, pl.ds(j * 128, 128)], amps.at[i, j, pl.ds(0, PX)], 9 + i * 4 + j)

    @pl.loop(0, ROWS, step=8)
    def _(r):
        grad[:, :, :, pl.ds(pl.multiple_of(r, 8), 8), :] = jnp.zeros((2, 2, SLABS, 8, 128), F32)

    @pl.loop(0, PX, step=64)
    def _(r):
        pacc[:, :, :, pl.ds(pl.multiple_of(r, 64), 64), :] = jnp.zeros((2, 2, 2, 64, 128), F32)

    for layer in range(2):
        for j in range(4):
            loads["probe", layer, j].wait()
    loads["split"].wait()
    for layer in range(2):
        @pl.loop(0, PX, step=256)
        def _(r):
            here = pl.ds(pl.multiple_of(r, 256), 256)
            for j in range(2):
                pair = jnp.concatenate([plain[layer, 2 * j, here], plain[layer, 2 * j + 1, here]], axis=1)
                parted = moved(pair, split[...])
                for q in range(2):
                    probe[layer, q, j, here] = parted[:, q * 128:(q + 1) * 128]

    for name in ("main", "halo", "rows", "cols"):
        loads[name].wait()

    @pl.loop(0, 32)
    def _(o):
        at = pl.multiple_of(o * OWN, 8)
        for p in range(4):
            block = main[p, gather_place(o, p)].astype(F32)
            for layer in range(2):
                for q in range(2):
                    tile[layer, q, p, pl.ds(at, OWN)] = block[layer * OWN:(layer + 1) * OWN, q * 128:(q + 1) * 128]
        part = [halo[p, gather_place(o, p)].astype(F32) for p in range(3)]
        for q in range(2):
            cs = slice(q * 128, (q + 1) * 128)
            tile[0, q, 4, pl.ds(at, 16)] = part[0][:, cs]
            tile[0, q, 4, pl.ds(at + 16, 8)] = part[1][:8, cs]
            tile[1, q, 4, pl.ds(at, 8)] = part[1][8:, cs]
            tile[1, q, 4, pl.ds(at + 8, 16)] = part[2][:, cs]

    lane = lax.broadcasted_iota(jnp.int32, (32, 128), 1)

    def places_of(slot):
        row, col = rows_ref[slot], cols_ref[slot]
        places = []
        for q in range(2):
            start = (col + q) // 2
            places.append(((col + q) % 2, start // 128, start % 128))
        return row, places

    def extract(slot, buf):
        row, places = places_of(slot)
        for q, (plane, b, m) in enumerate(places):
            for t in range(2):
                for i in range(8):
                    here = pl.ds(t + i * 64, 32, stride=2)
                    there = pl.ds(row + t + i * 64, 32, stride=2)
                    got = []
                    for layer in range(2):
                        turned = [pltpu.roll(tile[layer, plane, b + j, there, :], (128 - m) % 128, 1) for j in range(3)]
                        got.append([jnp.where(lane < 128 - m, turned[j], turned[j + 1]) for j in range(2)])
                    for j in range(2):
                        re, im = got[0][j], got[1][j]
                        pr, pi = probe[0, q, j, here, :], probe[1, q, j, here, :]
                        rs = slice(j * 256 + i * 32, j * 256 + (i + 1) * 32)
                        patch[buf, 0, t * 2 + q, rs] = re
                        patch[buf, 1, t * 2 + q, rs] = im
                        cs = slice(j * 128, (j + 1) * 128)
                        exits[t, q, i * 32:(i + 1) * 32, cs] = (pr * re - pi * im).astype(BF)
                        exits[t, q, 256 + i * 32:256 + (i + 1) * 32, cs] = (pr * im + pi * re).astype(BF)

    extract(0, 0)
    loads["tab"].wait()

    @pl.loop(0, 3)
    def _(slot):
        row, places = places_of(slot)
        buf = slot % 2

        def spread(to, which, total, other):
            for part in range(2):
                for upper, value in ((0, total), (1, other)):
                    for t in range(2):
                        at = part * 256 + t * 128
                        to[which, t * 256 + upper * 128:t * 256 + (upper + 1) * 128, part * 256:(part + 1) * 256] = (
                            value[at:at + 128].astype(BF))

        @pl.loop(0, 2)
        def _(q):
            even, odd = dot(tab[0], exits[0, q]), dot(tab[1], exits[1, q])
            spread(flat, q, even + odd, even - odd)

        for j in range(4):
            pltpu.make_async_copy(
                amps_ref.at[slot, :, pl.ds(j * 128, 128)], amps.at[slot, j, pl.ds(0, PX)], sems.at[9 + slot * 4 + j]).wait()

        @pl.loop(0, 2)
        def _(t):
            here = pl.ds(pl.multiple_of(t * 256, 256), 256)
            even, odd = dot(flat[0, here], tab[2]), dot(flat[1, here], tab[3])
            for upper, wave in ((0, even + odd), (1, even - odd)):
                for j in range(2):
                    re, im = wave[:, j * 128:(j + 1) * 128], wave[:, 256 + j * 128:256 + (j + 1) * 128]
                    amp = amps[slot, 2 * upper + j, pl.ds(t, 256, stride=2), :]
                    ratio = amp * lax.rsqrt(re * re + im * im + 1.0)
                    cs = slice(j * 128, (j + 1) * 128)
                    stack[t, upper, 0:256, cs] = (re * ratio - re).astype(BF)
                    stack[t, upper, 256:512, cs] = (im * ratio - im).astype(BF)

        extract(jnp.minimum(slot + 1, 2), 1 - buf)
        halves = []
        for upper in range(2):
            even, odd = dot(tab[4], stack[0, upper]), dot(tab[5], stack[1, upper])
            halves.append((even + odd, even - odd))
        spread(flat, 0, halves[0][0] + halves[1][0], halves[0][1] + halves[1][1])
        spread(flat, 1, halves[0][0] - halves[1][0], halves[0][1] - halves[1][1])

        @pl.loop(0, 2)
        def _(t):
            here = pl.ds(pl.multiple_of(t * 256, 256), 256)
            deltas = dot(flat[0, here], tab[6]), dot(flat[1, here], tab[7])
            for i in range(8):
                at = pl.ds(t + i * 64, 32, stride=2)
                there = pl.ds(row + t + i * 64, 32, stride=2)
                rs = slice(i * 32, (i + 1) * 32)
                for q, (plane, b, m) in enumerate(places):
                    turned = [[], []]
                    for j in range(2):
                        dr = deltas[q][rs, j * 128:(j + 1) * 128]
                        di = deltas[q][rs, 256 + j * 128:256 + (j + 1) * 128]
                        pr, pi = probe[0, q, j, at, :], probe[1, q, j, at, :]
                        qr, qi = (patch[buf, k, t * 2 + q, j * 256 + i * 32:j * 256 + (i + 1) * 32] for k in range(2))
                        pacc[0, q, j, at, :] += qr * dr + qi * di
                        pacc[1, q, j, at, :] += qr * di - qi * dr
                        turned[0].append(pltpu.roll(pr * dr + pi * di, m, 1))
                        turned[1].append(pltpu.roll(pr * di - pi * dr, m, 1))
                    for layer in range(2):
                        one, two = turned[layer]
                        grad[layer, plane, b, there, :] += jnp.where(lane >= m, one, 0.0)
                        grad[layer, plane, b + 1, there, :] += jnp.where(lane >= m, two, one)
                        grad[layer, plane, b + 2, there, :] += jnp.where(lane < m, two, 0.0)

    stores = []
    for core in range(2):
        @pl.loop(0, 16)
        def _(pair):
            o = 2 * pair + core
            at = pl.multiple_of(o * OWN, 8)
            spot = [scatter_place(o, p) for p in range(4)]
            for c in range(5):
                for q in range(2):
                    low = grad[0, q, c, pl.ds(at, OWN)]
                    high = grad[1, q, c, pl.ds(at, OWN)]
                    parts = (low[:16], jnp.concatenate([low[16:], high[:8]], axis=0), high[8:])
                    for p in range(3):
                        if c < 4:
                            cs = slice(c * 256 + q * 128, c * 256 + (q + 1) * 128)
                            out_main[p, spot[p], :, cs] = parts[p].astype(BF)
                        else:
                            cs = slice(q * 128, (q + 1) * 128)
                            out_spill[0, spot[3], p * 16:(p + 1) * 16, cs] = parts[p].astype(BF)
            rs = pl.ds(pl.multiple_of(o * 16, 16), 16)
            for layer in range(2):
                for j in range(2):
                    for q in range(2):
                        c = j * 256 + q * 128
                        out_probe[layer, ring_place(o, layer), :, c:c + 128] = pacc[layer, q, j, rs].astype(BF)

        half = pl.ds(core * 16, 16)
        for k, (src, dst) in enumerate(((out_main, main_out), (out_spill, spill_out), (out_probe, probe_out))):
            stores.append(pltpu.make_async_copy(src.at[:, half], dst.at[:, half], sems.at[26 + core * 3 + k]))
            stores[-1].start()
    for made in stores:
        made.wait()


def work(rows, cols, main, halo, probe, amps, split):
    vmem = pltpu.VMEM
    return pl.pallas_call(
        work_kernel,
        out_shape=[
            jax.ShapeDtypeStruct((3, 32, 16, TW), BF),
            jax.ShapeDtypeStruct((1, 32, 48, HALO), BF),
            jax.ShapeDtypeStruct((2, 32, 16, PX), BF),
        ],
        in_specs=[HBM] * 8,
        out_specs=[HBM] * 3,
        scratch_shapes=[
            vmem((3, 32, 16, TW), BF), vmem((1, 32, 48, HALO), BF), vmem((2, 32, 16, PX), BF),
            pltpu.SMEM((3,), jnp.int32), pltpu.SMEM((3,), jnp.int32),
            vmem((4, 32, 48, 256), BF), vmem((3, 32, 16, 256), BF), vmem((256, 256), BF),
            vmem((2, 2, SLABS, ROWS, 128), F32), vmem((2, 2, SLABS, ROWS, 128), F32),
            vmem((2, 2, 2, PX + 8, 128), F32), vmem((3, 4, PX + 8, 128), F32),
            vmem((8, PX, PX), BF),
            vmem((2, 2, 2, PX + 8, 128), F32), vmem((2, 2, 4, PX, 128), F32),
            vmem((2, 2, PX, 256), BF), vmem((2, 2, PX, 256), BF), vmem((2, PX, PX), BF),
            pltpu.SemaphoreType.DMA((32,)),
        ],
        compiler_params=pltpu.CompilerParams(vmem_limit_bytes=62 * MB),
        name="work",
    )(rows, cols, main, halo, probe, amps, jnp.asarray(tables()), split)


class Light:
    def __init__(self, spots, probe, lit, acc, spill_acc, first):
        self.spots, self.probe, self.lit, self.acc, self.spill_acc, self.first = spots, probe, lit, acc, spill_acc, first

    def prepare(self):
        for j in (0, 5):
            self.lit[j] = jnp.zeros((PX + 2 * OWN + 8, 128), F32)
        for j in range(4):
            self.lit[j + 1, 0:OWN] = jnp.zeros((OWN, 128), F32)
            self.lit[j + 1, PX + OWN:] = jnp.zeros((OWN + 8, 128), F32)

            @pl.loop(0, PX, step=64)
            def _(r):
                here = pl.ds(pl.multiple_of(r, 64), 64)
                cs = slice(j * 128, (j + 1) * 128)
                pr, pi = self.probe[0, here, cs], self.probe[1, here, cs]
                self.lit[j + 1, pl.ds(pl.multiple_of(r + OWN, 8), 64)] = pr * pr + pi * pi

        self.acc[...] = jnp.zeros_like(self.acc)
        self.spill_acc[...] = jnp.zeros_like(self.spill_acc)

    def add(self, begin, end):
        lane = lax.broadcasted_iota(jnp.int32, (8, 128), 1)

        @pl.loop(begin, end)
        def _(o):
            for k in range(3):
                for which, to, slabs, shift in ((0, self.acc, 8, 0), (1, self.spill_acc, 2, 8)):
                    row = self.spots[0, o, which * 2, k]
                    col = self.spots[0, o, which * 2 + 1, k]
                    start = jnp.clip(self.first - row + OWN, 0, PX + OWN)
                    b, m = col // 128, col % 128
                    last = [None] * 3
                    for j in range(-1, slabs):
                        slab = jnp.clip(j + shift - b + 1, 0, 5)
                        for t in range(3):
                            here = pltpu.roll(self.lit[slab, pl.ds(start + t, 8, stride=3), :], m, 1)
                            if j >= 0:
                                to[t, j] += jnp.where(lane >= m, here, last[t])
                            last[t] = here

    def result(self, y, out):
        for j in range(8):
            for t in range(3):
                value = self.acc[t, j]
                if j < 2:
                    value = value + jnp.where(y == 0, 0.0, self.spill_acc[t, j])
                out[j, pl.ds(t, 8, stride=3), :] = value


class Halving:
    def __init__(self, src, part, rotation, me, refs):
        (self.mine, self.came, self.acc0, self.acc1, self.s0, self.r0, self.s1, self.r1, self.s2, self.r2,
         self.fin, self.send, self.recv, self.local) = refs
        self.src, self.part = src, part
        self.y, self.pat = me
        self.own = self.pat % 2 * 16
        self.other = 16 - self.own
        self.dims = order(rotation)
        self.bits = [bits_of(self.pat)[d] for d in self.dims]
        self.made = {}

    def copy(self, name, src, dst, pat):
        slot = len(self.made)
        made = pltpu.make_async_remote_copy(
            src_ref=src, dst_ref=dst, send_sem=self.send.at[self.part, slot], recv_sem=self.recv.at[self.part, slot],
            device_id=(self.y, pat), device_id_type=MESH)
        made.start()
        self.made[name] = made

    def fetch(self):
        self.fetched = pltpu.make_async_copy(
            self.src.at[self.part, pl.ds(self.own, 16)], self.mine.at[self.part], self.local.at[self.part])
        self.fetched.start()

    def swap(self, half):
        at = (1 - self.bits[0]) * 8 if half == 0 else self.bits[0] * 8
        self.copy(("swap", half), self.src.at[self.part, pl.ds(self.other + at, 8)],
                  self.came.at[self.part, half], partner_of(self.pat, "core"))

    def zero(self):
        p, b0, b1 = self.part, self.bits[0], self.bits[1]
        self.fetched.wait()
        self.made["swap", 0].wait_recv()
        for u in range(2):
            group = (1 - b1) * 4 if u == 0 else b1 * 4

            @pl.loop(0, 4)
            def _(j):
                at = group + j
                total = self.mine[p, (1 - b0) * 8 + at].astype(F32) + self.came[p, 0, at].astype(F32)
                self.s0[p, u, j] = total.astype(BF)

            self.copy(("zero", u), self.s0.at[p, u], self.r0.at[p, u], partner_of(self.pat, self.dims[0]))

    def zero_kept(self):
        p, b0 = self.part, self.bits[0]
        self.made["swap", 1].wait_recv()

        @pl.loop(0, 8)
        def _(j):
            self.acc0[p, j] = self.mine[p, b0 * 8 + j].astype(F32) + self.came[p, 1, j].astype(F32)

    def one(self):
        p, b1 = self.part, self.bits[1]
        self.made["zero", 0].wait_recv()

        @pl.loop(0, 4)
        def _(j):
            self.s1[p, j] = (self.acc0[p, (1 - b1) * 4 + j] + self.r0[p, 0, j].astype(F32)).astype(BF)

        self.copy("one", self.s1.at[p], self.r1.at[p], partner_of(self.pat, self.dims[1]))

    def one_kept(self):
        p, b1 = self.part, self.bits[1]
        self.made["zero", 1].wait_recv()

        @pl.loop(0, 4)
        def _(j):
            self.acc1[p, j] = self.acc0[p, b1 * 4 + j] + self.r0[p, 1, j].astype(F32)

    def two(self):
        p, b2, b3 = self.part, self.bits[2], self.bits[3]
        self.made["one"].wait_recv()

        def total(flip2, flip3):
            at = (1 - b2 if flip2 else b2) * 2 + (1 - b3 if flip3 else b3)
            return self.acc1[p, at] + self.r1[p, at].astype(F32)

        d2, d3 = self.dims[2], self.dims[3]
        for k, (flip2, flip3, pat) in enumerate((
            (True, True, corner_of(self.pat, d2, d3)),
            (True, False, partner_of(self.pat, d2)),
            (False, True, partner_of(self.pat, d3)),
        )):
            self.s2[p, k] = total(flip2, flip3).astype(BF)
            self.copy(("two", k), self.s2.at[p, k], self.r2.at[p, k], pat)
        self.fin[p] = total(False, False)

    def total(self):
        for k in range(3):
            self.made["two", k].wait_recv()
        return self.fin[self.part] + sum(self.r2[self.part, k].astype(F32) for k in range(3))

    def finish(self):
        for made in self.made.values():
            made.wait_send()


HALVING_REFS = 14


def halving_scratch(parts, rows, columns):
    block = (rows, columns)
    return [
        pltpu.VMEM((parts, 16, *block), BF), pltpu.VMEM((parts, 2, 8, *block), BF),
        pltpu.VMEM((parts, 8, *block), F32), pltpu.VMEM((parts, 4, *block), F32),
        pltpu.VMEM((parts, 2, 4, *block), BF), pltpu.VMEM((parts, 2, 4, *block), BF),
        pltpu.VMEM((parts, 4, *block), BF), pltpu.VMEM((parts, 4, *block), BF),
        pltpu.VMEM((parts, 3, *block), BF), pltpu.VMEM((parts, 3, *block), BF),
        pltpu.VMEM((parts, *block), F32),
        pltpu.SemaphoreType.DMA((parts, 8)), pltpu.SemaphoreType.DMA((parts, 8)), pltpu.SemaphoreType.DMA((parts,)),
    ]


class Rings:
    def __init__(self, src, me, mine, local, came, keep, s1, r1, s2, r2, fin, pbuf, sems):
        self.src, self.came, self.keep, self.pbuf = src, came, keep, pbuf
        self.mine, self.local = mine, local
        self.s1, self.r1, self.s2, self.r2, self.fin = s1, r1, s2, r2, fin
        self.y, self.pat = me
        self.core = self.pat % 2
        self.sibling = partner_of(self.pat, "core")
        self.sems, self.made, self.used = sems, {}, 0
        x, z = (self.pat // 2) % 4, self.pat // 8
        self.at = ((x, z), (z, x))
        self.axes = (("x", "z"), ("z", "x"))

    def send(self, name, src, dst, pat):
        send, recv = self.sems
        made = pltpu.make_async_remote_copy(
            src_ref=src, dst_ref=dst, send_sem=send.at[self.used], recv_sem=recv.at[self.used],
            device_id=(self.y, pat), device_id_type=MESH)
        made.start()
        self.made[name] = made
        self.used += 1

    def swap(self):
        for h in range(2):
            self.send(("swap", h), self.src.at[h, pl.ds((1 - self.core) * 16, 16)], self.came.at[h], self.sibling)

    def fetch(self):
        self.fetched = pltpu.make_async_copy(self.src.at[:, pl.ds(self.core * 16, 16)], self.mine, self.local.at[0])
        self.fetched.start()

    def ring_one(self):
        self.fetched.wait()
        for h in range(2):
            self.made["swap", h].wait_recv()
            f = self.at[h][0]

            @pl.loop(0, 4)
            def _(j):
                at = f * 4 + j
                self.keep[h, j] = self.mine[h, at].astype(F32) + self.came[h, at].astype(F32)

            for k in range(1, 4):
                to = (f + k) % 4

                @pl.loop(0, 4)
                def _(j):
                    at = to * 4 + j
                    total = self.mine[h, at].astype(F32) + self.came[h, at].astype(F32)
                    self.s1[h, k - 1, j] = total.astype(BF)

                self.send(("one", h, k), self.s1.at[h, k - 1], self.r1.at[h, k - 1],
                          along(self.pat, self.axes[h][0], k))

    def ring_two(self):
        for h in range(2):
            for k in range(1, 4):
                self.made["one", h, k].wait_recv()
            g = self.at[h][1]

            def total(j):
                return self.keep[h, j] + sum(self.r1[h, k, j].astype(F32) for k in range(3))

            for k in range(1, 4):
                self.s2[h, k - 1] = total((g + k) % 4).astype(BF)
                self.send(("two", h, k), self.s2.at[h, k - 1], self.r2.at[h, k - 1],
                          along(self.pat, self.axes[h][1], k))
            self.fin[h] = total(g)

    def total(self, h):
        for k in range(1, 4):
            self.made["two", h, k].wait_recv()
        return self.fin[h] + sum(self.r2[h, k].astype(F32) for k in range(3))

    def gather_one(self, values):
        for h in range(2):
            place = ring_place(self.pat, h)
            self.pbuf[h, pl.ds(place, 1)] = values[h].reshape(1, 16, PX)
            mine = self.pbuf.at[h, pl.ds(place, 1)]
            for k in range(1, 4):
                self.send(("three", h, k), mine, mine, along(self.pat, self.axes[h][1], k))

    def gather_two(self):
        for h in range(2):
            for k in range(1, 4):
                self.made["three", h, k].wait_recv()
            mine = self.pbuf.at[h, pl.ds(self.core * 16 + self.at[h][0] * 4, 4)]
            for k in range(1, 4):
                self.send(("four", h, k), mine, mine, along(self.pat, self.axes[h][0], k))
            self.send(("near", h, 0), mine, mine, self.sibling)

    def gather_three(self):
        for k in (1, 3, 2):
            for h in range(2):
                self.made["four", h, k].wait_recv()
                came = self.pbuf.at[h, pl.ds(self.core * 16 + (self.at[h][0] + 4 - k) % 4 * 4, 4)]
                self.send(("near", h, k), came, came, self.sibling)

    def finish(self):
        for name, made in self.made.items():
            if name[0] == "near":
                made.wait_recv()
        for made in self.made.values():
            made.wait_send()


RING_SENDS = 2 + 4 * 6 + 8


def reduce_kernel(spots_ref, main_ref, spill_ref, sum_ref, probe_ref, join_hbm, obj_out, probe_out, *refs):
    y, pat = lax.axis_index("obj"), lax.axis_index("pat")
    me = (y, pat)
    rows = lax.axis_size("obj")
    mains = [Halving(main_ref, p, p, me, refs[:HALVING_REFS]) for p in range(3)]
    spills = [Halving(spill_ref, 0, 3, me, refs[HALVING_REFS:2 * HALVING_REFS])]
    (summine, rlocal, spill, spilled, ypro, came, keep, s1, r1, s2, r2, fin, pbuf, lit, acc, spill_acc, lights,
     spots, probe, join_ref, ysend, yrecv, psend, precv, lsem) = refs[2 * HALVING_REFS:]
    loads = [pltpu.make_async_copy(src, dst, lsem.at[k]) for k, (src, dst) in enumerate(
        ((probe_ref, probe), (spots_ref, spots), (join_hbm, join_ref)))]
    for made in loads:
        made.start()
    rings = Rings(sum_ref, me, summine, rlocal, came, keep, s1, r1, s2, r2, fin, pbuf, (psend, precv))
    light = Light(spots, probe, lit, acc, spill_acc, pat * OWN)
    others = [((y + k) % rows, pat) for k in (1, 2, 3)]
    near = [(y, along(pat, axis, k)) for axis in ("x", "z") for k in (1, 2, 3)]
    greet(others + near + [(y, partner_of(pat, "core"))] + [(y, corner_of(pat, *c)) for c in CORNERS])
    objs = spills + mains

    rings.swap()
    for half in range(2):
        for part in objs:
            part.swap(half)
        if half == 0:
            rings.fetch()
            for part in objs:
                part.fetch()
    for made in loads:
        made.wait()
    rings.ring_one()
    for part in objs:
        part.zero()
    light.prepare()
    for part in objs:
        part.zero_kept()
    rings.ring_two()
    light.add(0, 8)
    for part in objs:
        part.one()
    for part in objs:
        part.one_kept()
    light.add(8, 16)
    for h in range(2):
        ypro[pl.ds(y, 1), :, h * PX:(h + 1) * PX] = rings.total(h).reshape(1, 16, PX)
    mine = ypro.at[pl.ds(y, 1)]
    across = []
    for k, other in enumerate(others):
        across.append(pltpu.make_async_remote_copy(
            src_ref=mine, dst_ref=mine, send_sem=ysend.at[k], recv_sem=yrecv.at[k],
            device_id=other, device_id_type=MESH))
        across[-1].start()
    for part in objs:
        part.two()
    for made in across:
        made.wait_recv()
    total = (ypro[0] + ypro[1] + ypro[2] + ypro[3]).astype(BF)
    joined = [dot(total[:, c * 256:(c + 1) * 256], join_ref[...]).astype(BF) for c in range(4)]
    rings.gather_one([jnp.concatenate(joined[2 * h:2 * h + 2], axis=1) for h in range(2)])
    light.add(16, 24)
    rings.gather_two()
    spill[...] = spills[0].total()
    over = pltpu.make_async_remote_copy(
        src_ref=spill, dst_ref=spilled, send_sem=ysend.at[3], recv_sem=yrecv.at[3],
        device_id=others[0], device_id_type=MESH)
    over.start()
    light.add(24, 32)
    rings.gather_three()
    light.result(y, lights)
    totals = [part.total() for part in mains]
    over.wait_recv()
    chunks = []
    for c in range(4):
        whole = jnp.concatenate([total[:, c * 256:(c + 1) * 256] for total in totals], axis=0)
        chunks.append(whole + jnp.where(y == 0, 0.0, spilled[...]) if c == 0 else whole)
    joined = moved(jnp.concatenate(chunks, axis=0), join_ref[...])
    for j in range(8):
        here = joined[j // 2 * 48:(j // 2 + 1) * 48, (j % 2) * 128:(j % 2 + 1) * 128]
        under = lights[j] + 1.0
        for layer in range(2):
            obj_out[layer * OWN:(layer + 1) * OWN, j * 128:(j + 1) * 128] = here[layer * OWN:(layer + 1) * OWN] / under
    rings.finish()
    for o in range(32):
        for h in range(2):
            probe_out[h, o * 16:(o + 1) * 16] = pbuf[h, ring_place(o, h)]
    for part in objs:
        part.finish()
    for made in across + [over]:
        made.wait_send()


def reduce_all(spots, main, spill, sums, probe, join):
    dma = pltpu.SemaphoreType.DMA
    vmem = pltpu.VMEM
    return pl.pallas_call(
        reduce_kernel,
        out_shape=[jax.ShapeDtypeStruct((48, TW), F32), jax.ShapeDtypeStruct((2, PX, PX), BF)],
        in_specs=[HBM] * 6,
        out_specs=[VMEM] * 2,
        scratch_shapes=[
            *halving_scratch(3, 16, TW), *halving_scratch(1, 48, HALO),
            vmem((2, 16, 16, PX), BF), dma((1,)),
            vmem((48, HALO), F32), vmem((48, HALO), F32), vmem((4, 16, TW), F32),
            vmem((2, 16, 16, PX), BF), vmem((2, 4, 16, PX), F32),
            vmem((2, 3, 4, 16, PX), BF), vmem((2, 3, 4, 16, PX), BF),
            vmem((2, 3, 16, PX), BF), vmem((2, 3, 16, PX), BF),
            vmem((2, 16, PX), F32), vmem((2, 32, 16, PX), BF),
            vmem((6, PX + 2 * OWN + 8, 128), F32), vmem((3, 8, 8, 128), F32), vmem((3, 2, 8, 128), F32),
            vmem((8, OWN, 128), F32),
            pltpu.SMEM((1, 32, 8, 128), jnp.int32), vmem((2, PX, PX), F32), vmem((256, 256), BF),
            dma((4,)), dma((4,)), dma((RING_SENDS,)), dma((RING_SENDS,)), dma((3,)),
        ],
        compiler_params=pltpu.CompilerParams(
            collective_id=1, has_side_effects=True, vmem_limit_bytes=62 * MB),
        cost_estimate=pl.CostEstimate(flops=0, bytes_accessed=60 * MB, transcendentals=0),
        name="reduce_all",
    )(spots, main, spill, sums, probe, join)


def local(obj, probe, amps, rows, cols):
    total = rows.shape[0] * lax.axis_size("obj") * lax.axis_size("pat")
    split = splitter()
    main, halo, spots = gather(obj, rows, cols, jnp.asarray(split))
    sums = work(rows, cols, main, halo, probe, amps, jnp.asarray(split))
    own, probe_sum = reduce_all(spots, *sums, probe, jnp.asarray(split.T))
    obj_step = own.reshape(2, OWN, TW)
    probe_grad = probe_sum.astype(F32) * (1.0 / math.sqrt(total))
    return (obj_step, probe_grad)


def solution(mesh):
    placed = (
        P(None, "pat", "obj"),
        P(),
        P(("obj", "pat"), None, None),
        P(("obj", "pat")),
        P(("obj", "pat")),
    )
    return jax.shard_map(
        local, mesh=mesh, in_specs=placed, out_specs=(P(None, "pat", "obj"), P()), check_vma=False
    )
```

```python
import functools
import math

import jax
import jax.numpy as jnp
import ml_dtypes
import numpy as np
from jax import lax
from jax.experimental import pallas as pl
from jax.experimental.pallas import tpu as pltpu
from jax.sharding import PartitionSpec as P

PX = 512
HALO = 256
H = 768
TW = 1024
WIDE = TW + HALO
OWN = 24
BF = jnp.bfloat16
F32 = jnp.float32
MESH = pl.DeviceIdType.MESH
DIMS = ("xa", "za", "xb", "zb")
MB = 1 << 20


def bits_of(pat):
    x, z = (pat // 2) % 4, pat // 8
    return {
        "core": pat % 2,
        "xa": (x // 2 + x) % 2,
        "xb": x // 2,
        "za": (z // 2 + z) % 2,
        "zb": z // 2,
    }


def partner_of(pat, dim):
    core, x, z = pat % 2, (pat // 2) % 4, pat // 8
    if dim == "core":
        core = 1 - core
    elif dim == "xa":
        x = x + 1 - 2 * (x % 2)
    elif dim == "xb":
        x = 3 - x
    elif dim == "za":
        z = z + 1 - 2 * (z % 2)
    else:
        z = 3 - z
    return (z * 4 + x) * 2 + core


def order(part):
    return [DIMS[(part + k) % 4] for k in range(4)]


def gather_place(pat, part):
    bits = bits_of(pat)
    return bits["core"] * 16 + sum(bits[d] * 2**k for k, d in enumerate(order(part)))


def scatter_place(pat, part):
    bits = bits_of(pat)
    return bits["core"] * 16 + sum(bits[d] * 2 ** (3 - k) for k, d in enumerate(order(part)))


def corner_of(pat, one, two):
    return partner_of(partner_of(pat, one), two)


def ring_place(pat, layer):
    core, x, z = pat % 2, (pat // 2) % 4, pat // 8
    return core * 16 + (x * 4 + z if layer == 0 else z * 4 + x)


def along(pat, axis, k):
    core, x, z = pat % 2, (pat // 2) % 4, pat // 8
    if axis == "x":
        x = (x + k) % 4
    else:
        z = (z + k) % 4
    return (z * 4 + x) * 2 + core


CORNERS = [(DIMS[k], DIMS[(k + 1) % 4]) for k in range(4)]


def greet(peers):
    barrier = pltpu.get_barrier_semaphore()
    for peer in peers:
        pl.semaphore_signal(barrier, inc=1, device_id=peer, device_id_type=MESH)
    pl.semaphore_wait(barrier, len(peers))


class Doubling:
    def __init__(self, buf, part, me, sems):
        self.buf, self.part, self.sems = buf, part, sems
        self.y, self.pat = me
        self.place = gather_place(self.pat, part)
        self.dims = order(part)
        self.made = {}

    def copy(self, name, src, dst, pat):
        send, recv = self.sems
        slot = len(self.made)
        made = pltpu.make_async_remote_copy(
            src_ref=src, dst_ref=dst, send_sem=send.at[self.part, slot], recv_sem=recv.at[self.part, slot],
            device_id=(self.y, pat), device_id_type=MESH,
        )
        made.start()
        self.made[name] = made

    def four(self, flip_two, flip_three):
        two, three = (self.place // 4) % 2, (self.place // 8) % 2
        two = 1 - two if flip_two else two
        three = 1 - three if flip_three else three
        return self.buf.at[self.part, pl.ds(self.place // 16 * 16 + three * 8 + two * 4, 4)]

    def near(self, name, ref):
        self.copy(name, ref, ref, partner_of(self.pat, "core"))

    def first(self, src):
        mine = self.buf.at[self.part, pl.ds(self.place, 1)]
        self.copy("a0", src, mine, partner_of(self.pat, self.dims[0]))
        self.copy("a1", src, mine, partner_of(self.pat, self.dims[1]))
        self.copy("a2", src, mine, corner_of(self.pat, self.dims[0], self.dims[1]))

    def second(self):
        for name in ("a0", "a1", "a2"):
            self.made[name].wait_recv()
        mine = self.four(False, False)
        self.copy("b", mine, mine, partner_of(self.pat, self.dims[2]))

    def third(self):
        mine = self.four(False, False)
        self.copy("c0", mine, mine, partner_of(self.pat, self.dims[3]))
        self.near("n0", mine)

    def fourth(self):
        self.made["b"].wait_recv()
        came = self.four(True, False)
        self.copy("c1", came, came, partner_of(self.pat, self.dims[3]))
        self.near("n1", came)

    def fifth(self, k):
        self.made[("c0", "c1")[k]].wait_recv()
        self.near(("n2", "n3")[k], self.four(k == 1, True))

    def finish(self):
        for name, made in self.made.items():
            made.wait_send()
            if name[0] == "n":
                made.wait_recv()


def gather_all(parts):
    for part in parts:
        part.second()
    for part in parts:
        part.third()
    for part in parts:
        part.fourth()
    for k in range(2):
        for part in parts:
            part.fifth(k)


def gather_kernel(obj_ref, rows_ref, cols_ref, split_ref, main_ref, halo_ref, spots_ref,
                  obj, split, at, mine, edge, masked, pos, pos_in, pos_all,
                  msend, mrecv, hsend, hrecv, psend, precv, esem, lsem):
    y, pat = lax.axis_index("obj"), lax.axis_index("pat")
    rows = lax.axis_size("obj")
    left, right = (y + rows - 1) % rows, (y + 1) % rows
    loads = [
        pltpu.make_async_copy(src, dst, lsem.at[8 + k])
        for k, (src, dst) in enumerate(
            ((obj_ref, obj), (split_ref, split), (rows_ref, at.at[0]), (cols_ref, at.at[1])))
    ]
    for made in loads:
        made.start()
    greet([(left, pat), (right, pat)] + [(y, partner_of(pat, d)) for d in DIMS + ("core",)]
          + [(y, corner_of(pat, *c)) for c in CORNERS])
    for made in loads:
        made.wait()
    mains = [Doubling(main_ref, p, (y, pat), (msend, mrecv)) for p in range(4)]
    halos = [Doubling(halo_ref, p, (y, pat), (hsend, hrecv)) for p in range(3)]
    spots = Doubling(spots_ref, 0, (y, pat), (psend, precv))
    own = []
    for p, part in enumerate(mains):
        here = pl.ds(p * 256, 256)
        mine[0, :, here] = dot(obj[0, :, here], split[...]).astype(BF)
        if p == 0:
            send_edge = pltpu.make_async_remote_copy(
                src_ref=mine.at[:, :, here], dst_ref=edge,
                send_sem=esem.at[0], recv_sem=esem.at[1], device_id=(left, pat), device_id_type=MESH,
            )
            send_edge.start()
        part.first(mine.at[:, :, here])
    line = lax.broadcasted_iota(jnp.int32, (1, 8, 128), 1)
    lane = lax.broadcasted_iota(jnp.int32, (1, 8, 128), 2)
    table = jnp.zeros((1, 8, 128), jnp.int32)
    for which in range(2):
        for k in range(3):
            table = jnp.where((line == which) & (lane == k), at[which, k], table)
    pos[...] = table
    send_pos = pltpu.make_async_remote_copy(
        src_ref=pos, dst_ref=pos_in,
        send_sem=esem.at[2], recv_sem=esem.at[3], device_id=(right, pat), device_id_type=MESH,
    )
    send_pos.start()
    for p, part in enumerate(mains):
        own.append(pltpu.make_async_copy(
            mine.at[:, :, pl.ds(p * 256, 256)], main_ref.at[p, pl.ds(part.place, 1)], lsem.at[p]))
        own[-1].start()
    send_edge.wait_recv()
    masked[...] = jnp.where(y == rows - 1, jnp.zeros_like(masked), edge[...])
    for p, part in enumerate(halos):
        part.first(masked.at[:, pl.ds(p * 16, 16)])
    for p, part in enumerate(halos):
        own.append(pltpu.make_async_copy(
            masked.at[:, pl.ds(p * 16, 16)], halo_ref.at[p, pl.ds(part.place, 1)], lsem.at[4 + p]))
        own[-1].start()
    send_pos.wait_recv()
    pos_all[...] = jnp.where(line < 2, pos[...], pltpu.roll(pos_in[...], 2, 1))
    spots.first(pos_all)
    own.append(pltpu.make_async_copy(pos_all, spots_ref.at[0, pl.ds(spots.place, 1)], lsem.at[7]))
    own[-1].start()
    for made in own:
        made.wait()
    parts = mains + halos + [spots]
    gather_all(parts)
    for part in parts:
        part.finish()
    send_edge.wait_send()
    send_pos.wait_send()


HBM = pl.BlockSpec(memory_space=pltpu.HBM)
VMEM = pl.BlockSpec(memory_space=pltpu.VMEM)


def gather(obj, rows, cols, split):
    dma = pltpu.SemaphoreType.DMA
    return pl.pallas_call(
        gather_kernel,
        out_shape=[
            jax.ShapeDtypeStruct((4, 32, 48, 256), BF),
            jax.ShapeDtypeStruct((3, 32, 16, 256), BF),
            jax.ShapeDtypeStruct((1, 32, 8, 128), jnp.int32),
        ],
        in_specs=[HBM] * 4,
        out_specs=[HBM] * 3,
        scratch_shapes=[
            pltpu.VMEM((1, 48, TW), BF),
            pltpu.VMEM((256, 256), BF),
            pltpu.SMEM((2, 3), jnp.int32),
            pltpu.VMEM((1, 48, TW), BF),
            pltpu.VMEM((1, 48, HALO), BF),
            pltpu.VMEM((1, 48, HALO), BF),
            pltpu.VMEM((1, 8, 128), jnp.int32),
            pltpu.VMEM((1, 8, 128), jnp.int32),
            pltpu.VMEM((1, 8, 128), jnp.int32),
            dma((4, 10)), dma((4, 10)), dma((3, 10)), dma((3, 10)), dma((1, 10)), dma((1, 10)),
            dma((4,)), dma((12,)),
        ],
        compiler_params=pltpu.CompilerParams(collective_id=0, has_side_effects=True, vmem_limit_bytes=62 * MB),
        cost_estimate=pl.CostEstimate(flops=0, bytes_accessed=60 * MB, transcendentals=0),
        name="gather",
    )(obj.reshape(1, 48, TW), rows, cols, split)


def tables():
    index = np.arange(PX)
    angle = (index[:, None] * index[None, :] % PX) * (2.0 * np.pi / PX)
    real = (np.cos(angle) / np.sqrt(PX)).astype(ml_dtypes.bfloat16)
    imag = (-np.sin(angle) / np.sqrt(PX)).astype(ml_dtypes.bfloat16)
    low = np.arange(256)
    sorted_low = np.concatenate([low[::2], low[1::2]])
    even, odd = index[::2], index[1::2]

    def left(re, im, rows, cols):
        pick = np.ix_(rows, cols)
        return np.block([[re[pick], -im[pick]], [im[pick], re[pick]]])

    def right(re, im, rows, cols):
        pick = np.ix_(rows, cols)
        return np.block([[re[pick], im[pick]], [-im[pick], re[pick]]])

    return np.stack([
        left(real, imag, sorted_low, even), left(real, imag, sorted_low, odd),
        right(real, imag, even, low), right(real, imag, odd, low),
        left(real, -imag, sorted_low, even), left(real, -imag, sorted_low, odd),
        right(real, -imag, low, even), right(real, -imag, low, odd),
    ])


def splitter():
    k = np.arange(256)
    return (np.arange(256)[:, None] == 2 * (k % 128) + k // 128).astype(ml_dtypes.bfloat16)


def dot(a, b):
    return jnp.dot(a, b, preferred_element_type=F32)


def moved(x, pick):
    high = x.astype(BF)
    rest = x - high.astype(F32)
    mid = rest.astype(BF)
    low = (rest - mid.astype(F32)).astype(BF)
    return dot(high, pick) + dot(mid, pick) + dot(low, pick)


SLABS = 6
ROWS = H + 8


def work_kernel(rows_hbm, cols_hbm, main_ref, halo_ref, probe_ref, amps_ref, tab_ref, split_ref, main_out, spill_out, probe_out,
                out_main, out_spill, out_probe, rows_ref, cols_ref, main, halo, split, tile, grad, probe, amps, tab, pacc, patch, exits, stack, flat, sems):
    loads = {}

    def load(name, src, dst, slot):
        loads[name] = pltpu.make_async_copy(src, dst, sems.at[slot])
        loads[name].start()

    plain = patch.at[1]
    for layer in range(2):
        for j in range(4):
            load(("probe", layer, j), probe_ref.at[layer, :, pl.ds(j * 128, 128)], plain.at[layer, j], layer * 4 + j)
    load("split", split_ref, split, 21)
    load("main", main_ref, main, 22)
    load("halo", halo_ref, halo, 23)
    load("rows", rows_hbm, rows_ref, 24)
    load("cols", cols_hbm, cols_ref, 25)
    @pl.loop(0, ROWS, step=8)
    def _(r):
        grad[:, :, :, pl.ds(pl.multiple_of(r, 8), 8), :] = jnp.zeros((2, 2, SLABS, 8, 128), F32)

    @pl.loop(0, PX, step=64)
    def _(r):
        pacc[:, :, :, pl.ds(pl.multiple_of(r, 64), 64), :] = jnp.zeros((2, 2, 2, 64, 128), F32)

    for layer in range(2):
        for j in range(4):
            loads["probe", layer, j].wait()
    loads["split"].wait()
    for layer in range(2):
        @pl.loop(0, PX, step=256)
        def _(r):
            here = pl.ds(pl.multiple_of(r, 256), 256)
            for j in range(2):
                pair = jnp.concatenate([plain[layer, 2 * j, here], plain[layer, 2 * j + 1, here]], axis=1)
                parted = moved(pair, split[...])
                for q in range(2):
                    probe[layer, q, j, here] = parted[:, q * 128:(q + 1) * 128]

    for name in ("main", "halo", "rows", "cols"):
        loads[name].wait()
    load("tab", tab_ref, tab, 8)
    for i in range(3):
        for j in range(4):
            load(("amps", i, j), amps_ref.at[i, :, pl.ds(j * 128, 128)], amps.at[i, j, pl.ds(0, PX)], 9 + i * 4 + j)

    @pl.loop(0, 32)
    def _(o):
        at = pl.multiple_of(o * OWN, 8)
        for p in range(4):
            block = main[p, gather_place(o, p)].astype(F32)
            for layer in range(2):
                for q in range(2):
                    tile[layer, q, p, pl.ds(at, OWN)] = block[layer * OWN:(layer + 1) * OWN, q * 128:(q + 1) * 128]
        part = [halo[p, gather_place(o, p)].astype(F32) for p in range(3)]
        for q in range(2):
            cs = slice(q * 128, (q + 1) * 128)
            tile[0, q, 4, pl.ds(at, 16)] = part[0][:, cs]
            tile[0, q, 4, pl.ds(at + 16, 8)] = part[1][:8, cs]
            tile[1, q, 4, pl.ds(at, 8)] = part[1][8:, cs]
            tile[1, q, 4, pl.ds(at + 8, 16)] = part[2][:, cs]

    lane = lax.broadcasted_iota(jnp.int32, (32, 128), 1)

    def places_of(slot):
        row, col = rows_ref[slot], cols_ref[slot]
        places = []
        for q in range(2):
            start = (col + q) // 2
            places.append(((col + q) % 2, start // 128, start % 128))
        return row, places

    def extract(slot, buf):
        row, places = places_of(slot)
        for q, (plane, b, m) in enumerate(places):
            for t in range(2):
                for i in range(8):
                    here = pl.ds(t + i * 64, 32, stride=2)
                    there = pl.ds(row + t + i * 64, 32, stride=2)
                    got = []
                    for layer in range(2):
                        turned = [pltpu.roll(tile[layer, plane, b + j, there, :], (128 - m) % 128, 1) for j in range(3)]
                        got.append([jnp.where(lane < 128 - m, turned[j], turned[j + 1]) for j in range(2)])
                    for j in range(2):
                        re, im = got[0][j], got[1][j]
                        pr, pi = probe[0, q, j, here, :], probe[1, q, j, here, :]
                        rs = slice(j * 256 + i * 32, j * 256 + (i + 1) * 32)
                        patch[buf, 0, t * 2 + q, rs] = re
                        patch[buf, 1, t * 2 + q, rs] = im
                        cs = slice(j * 128, (j + 1) * 128)
                        exits[t, q, i * 32:(i + 1) * 32, cs] = (pr * re - pi * im).astype(BF)
                        exits[t, q, 256 + i * 32:256 + (i + 1) * 32, cs] = (pr * im + pi * re).astype(BF)

    extract(0, 0)
    loads["tab"].wait()

    @pl.loop(0, 3)
    def _(slot):
        row, places = places_of(slot)
        buf = slot % 2

        def spread(to, which, total, other):
            for part in range(2):
                for upper, value in ((0, total), (1, other)):
                    for t in range(2):
                        at = part * 256 + t * 128
                        to[which, t * 256 + upper * 128:t * 256 + (upper + 1) * 128, part * 256:(part + 1) * 256] = (
                            value[at:at + 128].astype(BF))

        for q in range(2):
            even, odd = dot(tab[0], exits[0, q]), dot(tab[1], exits[1, q])
            spread(flat, q, even + odd, even - odd)

        for j in range(4):
            pltpu.make_async_copy(
                amps_ref.at[slot, :, pl.ds(j * 128, 128)], amps.at[slot, j, pl.ds(0, PX)], sems.at[9 + slot * 4 + j]).wait()

        for t in range(2):
            here = pl.ds(t * 256, 256)
            even, odd = dot(flat[0, here], tab[2]), dot(flat[1, here], tab[3])
            for upper, wave in ((0, even + odd), (1, even - odd)):
                for j in range(2):
                    re, im = wave[:, j * 128:(j + 1) * 128], wave[:, 256 + j * 128:256 + (j + 1) * 128]
                    amp = amps[slot, 2 * upper + j, pl.ds(t, 256, stride=2), :]
                    ratio = amp * lax.rsqrt(re * re + im * im + 1.0)
                    cs = slice(j * 128, (j + 1) * 128)
                    stack[t, upper, 0:256, cs] = (re * ratio - re).astype(BF)
                    stack[t, upper, 256:512, cs] = (im * ratio - im).astype(BF)

        extract(jnp.minimum(slot + 1, 2), 1 - buf)
        halves = []
        for upper in range(2):
            even, odd = dot(tab[4], stack[0, upper]), dot(tab[5], stack[1, upper])
            halves.append((even + odd, even - odd))
        spread(flat, 0, halves[0][0] + halves[1][0], halves[0][1] + halves[1][1])
        spread(flat, 1, halves[0][0] - halves[1][0], halves[0][1] - halves[1][1])

        @pl.loop(0, 2)
        def _(t):
            here = pl.ds(pl.multiple_of(t * 256, 256), 256)
            deltas = dot(flat[0, here], tab[6]), dot(flat[1, here], tab[7])
            for i in range(8):
                at = pl.ds(t + i * 64, 32, stride=2)
                there = pl.ds(row + t + i * 64, 32, stride=2)
                rs = slice(i * 32, (i + 1) * 32)
                for q, (plane, b, m) in enumerate(places):
                    turned = [[], []]
                    for j in range(2):
                        dr = deltas[q][rs, j * 128:(j + 1) * 128]
                        di = deltas[q][rs, 256 + j * 128:256 + (j + 1) * 128]
                        pr, pi = probe[0, q, j, at, :], probe[1, q, j, at, :]
                        qr, qi = (patch[buf, k, t * 2 + q, j * 256 + i * 32:j * 256 + (i + 1) * 32] for k in range(2))
                        pacc[0, q, j, at, :] += qr * dr + qi * di
                        pacc[1, q, j, at, :] += qr * di - qi * dr
                        turned[0].append(pltpu.roll(pr * dr + pi * di, m, 1))
                        turned[1].append(pltpu.roll(pr * di - pi * dr, m, 1))
                    for layer in range(2):
                        one, two = turned[layer]
                        grad[layer, plane, b, there, :] += jnp.where(lane >= m, one, 0.0)
                        grad[layer, plane, b + 1, there, :] += jnp.where(lane >= m, two, one)
                        grad[layer, plane, b + 2, there, :] += jnp.where(lane < m, two, 0.0)

    stores = []
    for core in range(2):
        @pl.loop(0, 16)
        def _(pair):
            o = 2 * pair + core
            at = pl.multiple_of(o * OWN, 8)
            spot = [scatter_place(o, p) for p in range(4)]
            for c in range(5):
                for q in range(2):
                    low = grad[0, q, c, pl.ds(at, OWN)]
                    high = grad[1, q, c, pl.ds(at, OWN)]
                    parts = (low[:16], jnp.concatenate([low[16:], high[:8]], axis=0), high[8:])
                    for p in range(3):
                        if c < 4:
                            cs = slice(c * 256 + q * 128, c * 256 + (q + 1) * 128)
                            out_main[p, spot[p], :, cs] = parts[p].astype(BF)
                        else:
                            cs = slice(q * 128, (q + 1) * 128)
                            out_spill[0, spot[3], p * 16:(p + 1) * 16, cs] = parts[p].astype(BF)
            rs = pl.ds(pl.multiple_of(o * 16, 16), 16)
            for layer in range(2):
                for j in range(2):
                    for q in range(2):
                        c = j * 256 + q * 128
                        out_probe[layer, ring_place(o, layer), :, c:c + 128] = pacc[layer, q, j, rs].astype(BF)

        half = pl.ds(core * 16, 16)
        for k, (src, dst) in enumerate(((out_main, main_out), (out_spill, spill_out), (out_probe, probe_out))):
            stores.append(pltpu.make_async_copy(src.at[:, half], dst.at[:, half], sems.at[26 + core * 3 + k]))
            stores[-1].start()
    for made in stores:
        made.wait()


def work(rows, cols, main, halo, probe, amps, split):
    vmem = pltpu.VMEM
    return pl.pallas_call(
        work_kernel,
        out_shape=[
            jax.ShapeDtypeStruct((3, 32, 16, TW), BF),
            jax.ShapeDtypeStruct((1, 32, 48, HALO), BF),
            jax.ShapeDtypeStruct((2, 32, 16, PX), BF),
        ],
        in_specs=[HBM] * 8,
        out_specs=[HBM] * 3,
        scratch_shapes=[
            vmem((3, 32, 16, TW), BF), vmem((1, 32, 48, HALO), BF), vmem((2, 32, 16, PX), BF),
            pltpu.SMEM((3,), jnp.int32), pltpu.SMEM((3,), jnp.int32),
            vmem((4, 32, 48, 256), BF), vmem((3, 32, 16, 256), BF), vmem((256, 256), BF),
            vmem((2, 2, SLABS, ROWS, 128), F32), vmem((2, 2, SLABS, ROWS, 128), F32),
            vmem((2, 2, 2, PX + 8, 128), F32), vmem((3, 4, PX + 8, 128), F32),
            vmem((8, PX, PX), BF),
            vmem((2, 2, 2, PX + 8, 128), F32), vmem((2, 2, 4, PX, 128), F32),
            vmem((2, 2, PX, 256), BF), vmem((2, 2, PX, 256), BF), vmem((2, PX, PX), BF),
            pltpu.SemaphoreType.DMA((32,)),
        ],
        compiler_params=pltpu.CompilerParams(vmem_limit_bytes=62 * MB),
        name="work",
    )(rows, cols, main, halo, probe, amps, jnp.asarray(tables()), split)


class Light:
    def __init__(self, spots, probe, lit, acc, spill_acc, first):
        self.spots, self.probe, self.lit, self.acc, self.spill_acc, self.first = spots, probe, lit, acc, spill_acc, first

    def prepare(self):
        for j in (0, 5):
            self.lit[j] = jnp.zeros((PX + 2 * OWN + 8, 128), F32)
        for j in range(4):
            self.lit[j + 1, 0:OWN] = jnp.zeros((OWN, 128), F32)
            self.lit[j + 1, PX + OWN:] = jnp.zeros((OWN + 8, 128), F32)

            @pl.loop(0, PX, step=64)
            def _(r):
                here = pl.ds(pl.multiple_of(r, 64), 64)
                cs = slice(j * 128, (j + 1) * 128)
                pr, pi = self.probe[0, here, cs], self.probe[1, here, cs]
                self.lit[j + 1, pl.ds(pl.multiple_of(r + OWN, 8), 64)] = pr * pr + pi * pi

        self.acc[...] = jnp.zeros_like(self.acc)
        self.spill_acc[...] = jnp.zeros_like(self.spill_acc)

    def add(self, begin, end):
        lane = lax.broadcasted_iota(jnp.int32, (8, 128), 1)

        @pl.loop(begin, end)
        def _(o):
            for k in range(3):
                for which, to, slabs, shift in ((0, self.acc, 8, 0), (1, self.spill_acc, 2, 8)):
                    row = self.spots[0, o, which * 2, k]
                    col = self.spots[0, o, which * 2 + 1, k]
                    start = jnp.clip(self.first - row + OWN, 0, PX + OWN)
                    b, m = col // 128, col % 128
                    last = [None] * 3
                    for j in range(-1, slabs):
                        slab = jnp.clip(j + shift - b + 1, 0, 5)
                        for t in range(3):
                            here = pltpu.roll(self.lit[slab, pl.ds(start + t, 8, stride=3), :], m, 1)
                            if j >= 0:
                                to[t, j] += jnp.where(lane >= m, here, last[t])
                            last[t] = here

    def result(self, y, out):
        for j in range(8):
            for t in range(3):
                value = self.acc[t, j]
                if j < 2:
                    value = value + jnp.where(y == 0, 0.0, self.spill_acc[t, j])
                out[j, pl.ds(t, 8, stride=3), :] = value


class Halving:
    def __init__(self, src, part, rotation, me, refs):
        (self.mine, self.came, self.acc0, self.acc1, self.s0, self.r0, self.s1, self.r1, self.s2, self.r2,
         self.fin, self.send, self.recv, self.local) = refs
        self.src, self.part = src, part
        self.y, self.pat = me
        self.own = self.pat % 2 * 16
        self.other = 16 - self.own
        self.dims = order(rotation)
        self.bits = [bits_of(self.pat)[d] for d in self.dims]
        self.made = {}

    def copy(self, name, src, dst, pat):
        slot = len(self.made)
        made = pltpu.make_async_remote_copy(
            src_ref=src, dst_ref=dst, send_sem=self.send.at[self.part, slot], recv_sem=self.recv.at[self.part, slot],
            device_id=(self.y, pat), device_id_type=MESH)
        made.start()
        self.made[name] = made

    def fetch(self):
        self.fetched = pltpu.make_async_copy(
            self.src.at[self.part, pl.ds(self.own, 16)], self.mine.at[self.part], self.local.at[self.part])
        self.fetched.start()

    def swap(self, half):
        at = (1 - self.bits[0]) * 8 if half == 0 else self.bits[0] * 8
        self.copy(("swap", half), self.src.at[self.part, pl.ds(self.other + at, 8)],
                  self.came.at[self.part, half], partner_of(self.pat, "core"))

    def zero(self, u):
        p, b0, b1 = self.part, self.bits[0], self.bits[1]
        if u == 0:
            self.fetched.wait()
            self.made["swap", 0].wait_recv()
        group = (1 - b1) * 4 if u == 0 else b1 * 4

        @pl.loop(0, 4)
        def _(j):
            at = group + j
            total = self.mine[p, (1 - b0) * 8 + at].astype(F32) + self.came[p, 0, at].astype(F32)
            self.s0[p, u, j] = total.astype(BF)

        self.copy(("zero", u), self.s0.at[p, u], self.r0.at[p, u], partner_of(self.pat, self.dims[0]))

    def zero_kept(self):
        p, b0 = self.part, self.bits[0]
        self.made["swap", 1].wait_recv()

        @pl.loop(0, 8)
        def _(j):
            self.acc0[p, j] = self.mine[p, b0 * 8 + j].astype(F32) + self.came[p, 1, j].astype(F32)

    def one(self):
        p, b1 = self.part, self.bits[1]
        self.made["zero", 0].wait_recv()

        @pl.loop(0, 4)
        def _(j):
            self.s1[p, j] = (self.acc0[p, (1 - b1) * 4 + j] + self.r0[p, 0, j].astype(F32)).astype(BF)

        self.copy("one", self.s1.at[p], self.r1.at[p], partner_of(self.pat, self.dims[1]))

    def one_kept(self):
        p, b1 = self.part, self.bits[1]
        self.made["zero", 1].wait_recv()

        @pl.loop(0, 4)
        def _(j):
            self.acc1[p, j] = self.acc0[p, b1 * 4 + j] + self.r0[p, 1, j].astype(F32)

    def two(self):
        p, b2, b3 = self.part, self.bits[2], self.bits[3]
        self.made["one"].wait_recv()

        def total(flip2, flip3):
            at = (1 - b2 if flip2 else b2) * 2 + (1 - b3 if flip3 else b3)
            return self.acc1[p, at] + self.r1[p, at].astype(F32)

        d2, d3 = self.dims[2], self.dims[3]
        for k, (flip2, flip3, pat) in enumerate((
            (True, True, corner_of(self.pat, d2, d3)),
            (True, False, partner_of(self.pat, d2)),
            (False, True, partner_of(self.pat, d3)),
        )):
            self.s2[p, k] = total(flip2, flip3).astype(BF)
            self.copy(("two", k), self.s2.at[p, k], self.r2.at[p, k], pat)
        self.fin[p] = total(False, False)

    def total(self):
        for k in range(3):
            self.made["two", k].wait_recv()
        return self.fin[self.part] + sum(self.r2[self.part, k].astype(F32) for k in range(3))

    def finish(self):
        for made in self.made.values():
            made.wait_send()


HALVING_REFS = 14


def halving_scratch(parts, rows, columns):
    block = (rows, columns)
    return [
        pltpu.VMEM((parts, 16, *block), BF), pltpu.VMEM((parts, 2, 8, *block), BF),
        pltpu.VMEM((parts, 8, *block), F32), pltpu.VMEM((parts, 4, *block), F32),
        pltpu.VMEM((parts, 2, 4, *block), BF), pltpu.VMEM((parts, 2, 4, *block), BF),
        pltpu.VMEM((parts, 4, *block), BF), pltpu.VMEM((parts, 4, *block), BF),
        pltpu.VMEM((parts, 3, *block), BF), pltpu.VMEM((parts, 3, *block), BF),
        pltpu.VMEM((parts, *block), F32),
        pltpu.SemaphoreType.DMA((parts, 8)), pltpu.SemaphoreType.DMA((parts, 8)), pltpu.SemaphoreType.DMA((parts,)),
    ]


class Rings:
    def __init__(self, src, me, mine, local, came, keep, s1, r1, s2, r2, fin, pbuf, sems):
        self.src, self.came, self.keep, self.pbuf = src, came, keep, pbuf
        self.mine, self.local = mine, local
        self.s1, self.r1, self.s2, self.r2, self.fin = s1, r1, s2, r2, fin
        self.y, self.pat = me
        self.core = self.pat % 2
        self.sibling = partner_of(self.pat, "core")
        self.sems, self.made, self.used = sems, {}, 0
        x, z = (self.pat // 2) % 4, self.pat // 8
        self.at = ((x, z), (z, x))
        self.axes = (("x", "z"), ("z", "x"))

    def send(self, name, src, dst, pat):
        send, recv = self.sems
        made = pltpu.make_async_remote_copy(
            src_ref=src, dst_ref=dst, send_sem=send.at[self.used], recv_sem=recv.at[self.used],
            device_id=(self.y, pat), device_id_type=MESH)
        made.start()
        self.made[name] = made
        self.used += 1

    def swap(self):
        for h in range(2):
            self.send(("swap", h), self.src.at[h, pl.ds((1 - self.core) * 16, 16)], self.came.at[h], self.sibling)

    def fetch(self):
        self.fetched = pltpu.make_async_copy(self.src.at[:, pl.ds(self.core * 16, 16)], self.mine, self.local.at[0])
        self.fetched.start()

    def ring_one(self):
        self.fetched.wait()
        for h in range(2):
            self.made["swap", h].wait_recv()
            f = self.at[h][0]

            @pl.loop(0, 4)
            def _(j):
                at = f * 4 + j
                self.keep[h, j] = self.mine[h, at].astype(F32) + self.came[h, at].astype(F32)

            for k in range(1, 4):
                to = (f + k) % 4

                @pl.loop(0, 4)
                def _(j):
                    at = to * 4 + j
                    total = self.mine[h, at].astype(F32) + self.came[h, at].astype(F32)
                    self.s1[h, k - 1, j] = total.astype(BF)

                self.send(("one", h, k), self.s1.at[h, k - 1], self.r1.at[h, k - 1],
                          along(self.pat, self.axes[h][0], k))

    def ring_two(self):
        for h in range(2):
            for k in range(1, 4):
                self.made["one", h, k].wait_recv()
            g = self.at[h][1]

            def total(j):
                return self.keep[h, j] + sum(self.r1[h, k, j].astype(F32) for k in range(3))

            for k in range(1, 4):
                self.s2[h, k - 1] = total((g + k) % 4).astype(BF)
                self.send(("two", h, k), self.s2.at[h, k - 1], self.r2.at[h, k - 1],
                          along(self.pat, self.axes[h][1], k))
            self.fin[h] = total(g)

    def total(self, h):
        for k in range(1, 4):
            self.made["two", h, k].wait_recv()
        return self.fin[h] + sum(self.r2[h, k].astype(F32) for k in range(3))

    def gather_one(self, values):
        for h in range(2):
            place = ring_place(self.pat, h)
            self.pbuf[h, pl.ds(place, 1)] = values[h].reshape(1, 16, PX)
            mine = self.pbuf.at[h, pl.ds(place, 1)]
            for k in range(1, 4):
                self.send(("three", h, k), mine, mine, along(self.pat, self.axes[h][1], k))

    def gather_two(self):
        for h in range(2):
            for k in range(1, 4):
                self.made["three", h, k].wait_recv()
            mine = self.pbuf.at[h, pl.ds(self.core * 16 + self.at[h][0] * 4, 4)]
            for k in range(1, 4):
                self.send(("four", h, k), mine, mine, along(self.pat, self.axes[h][0], k))
            self.send(("near", h, 0), mine, mine, self.sibling)

    def gather_three(self):
        for k in (1, 3, 2):
            for h in range(2):
                self.made["four", h, k].wait_recv()
                came = self.pbuf.at[h, pl.ds(self.core * 16 + (self.at[h][0] + 4 - k) % 4 * 4, 4)]
                self.send(("near", h, k), came, came, self.sibling)

    def finish(self):
        for name, made in self.made.items():
            if name[0] == "near":
                made.wait_recv()
        for made in self.made.values():
            made.wait_send()


RING_SENDS = 2 + 4 * 6 + 8


def reduce_kernel(spots_ref, main_ref, spill_ref, sum_ref, probe_ref, join_hbm, obj_out, probe_out, *refs):
    y, pat = lax.axis_index("obj"), lax.axis_index("pat")
    me = (y, pat)
    rows = lax.axis_size("obj")
    mains = [Halving(main_ref, p, p, me, refs[:HALVING_REFS]) for p in range(3)]
    spills = [Halving(spill_ref, 0, 3, me, refs[HALVING_REFS:2 * HALVING_REFS])]
    (summine, rlocal, spill, spilled, ypro, came, keep, s1, r1, s2, r2, fin, pbuf, lit, acc, spill_acc, lights,
     spots, probe, join_ref, ysend, yrecv, psend, precv, lsem) = refs[2 * HALVING_REFS:]
    rings = Rings(sum_ref, me, summine, rlocal, came, keep, s1, r1, s2, r2, fin, pbuf, (psend, precv))
    light = Light(spots, probe, lit, acc, spill_acc, pat * OWN)
    objs = spills + mains
    rings.fetch()
    for part in objs:
        part.fetch()
    loads = [pltpu.make_async_copy(src, dst, lsem.at[k]) for k, (src, dst) in enumerate(
        ((probe_ref, probe), (spots_ref, spots), (join_hbm, join_ref)))]
    for made in loads:
        made.start()
    others = [((y + k) % rows, pat) for k in (1, 2, 3)]
    near = [(y, along(pat, axis, k)) for axis in ("x", "z") for k in (1, 2, 3)]
    greet(others + near + [(y, partner_of(pat, "core"))] + [(y, corner_of(pat, *c)) for c in CORNERS])
    rings.swap()
    for half in range(2):
        for part in objs:
            part.swap(half)
    rings.ring_one()
    for part in objs:
        part.zero(0)
    for made in loads:
        made.wait()
    light.prepare()
    rings.ring_two()
    for part in objs:
        part.zero(1)
    for part in objs:
        part.zero_kept()
    for part in objs:
        part.one()
    for h in range(2):
        ypro[pl.ds(y, 1), :, h * PX:(h + 1) * PX] = rings.total(h).reshape(1, 16, PX)
    mine = ypro.at[pl.ds(y, 1)]
    across = []
    for k, other in enumerate(others):
        across.append(pltpu.make_async_remote_copy(
            src_ref=mine, dst_ref=mine, send_sem=ysend.at[k], recv_sem=yrecv.at[k],
            device_id=other, device_id_type=MESH))
        across[-1].start()
    light.add(0, 16)
    for made in across:
        made.wait_recv()
    total = (ypro[0] + ypro[1] + ypro[2] + ypro[3]).astype(BF)
    joined = [dot(total[:, c * 256:(c + 1) * 256], join_ref[...]).astype(BF) for c in range(4)]
    rings.gather_one([jnp.concatenate(joined[2 * h:2 * h + 2], axis=1) for h in range(2)])
    for part in objs:
        part.one_kept()
    for part in objs:
        part.two()
    light.add(16, 24)
    rings.gather_two()
    spill[...] = spills[0].total()
    over = pltpu.make_async_remote_copy(
        src_ref=spill, dst_ref=spilled, send_sem=ysend.at[3], recv_sem=yrecv.at[3],
        device_id=others[0], device_id_type=MESH)
    over.start()
    light.add(24, 32)
    rings.gather_three()
    light.result(y, lights)
    totals = [part.total() for part in mains]
    over.wait_recv()
    chunks = []
    for c in range(4):
        whole = jnp.concatenate([total[:, c * 256:(c + 1) * 256] for total in totals], axis=0)
        chunks.append(whole + jnp.where(y == 0, 0.0, spilled[...]) if c == 0 else whole)
    joined = moved(jnp.concatenate(chunks, axis=0), join_ref[...])
    for j in range(8):
        here = joined[j // 2 * 48:(j // 2 + 1) * 48, (j % 2) * 128:(j % 2 + 1) * 128]
        under = lights[j] + 1.0
        for layer in range(2):
            obj_out[layer * OWN:(layer + 1) * OWN, j * 128:(j + 1) * 128] = here[layer * OWN:(layer + 1) * OWN] / under
    rings.finish()
    for o in range(32):
        for h in range(2):
            probe_out[h, o * 16:(o + 1) * 16] = pbuf[h, ring_place(o, h)]
    for part in objs:
        part.finish()
    for made in across + [over]:
        made.wait_send()


def reduce_all(spots, main, spill, sums, probe, join):
    dma = pltpu.SemaphoreType.DMA
    vmem = pltpu.VMEM
    return pl.pallas_call(
        reduce_kernel,
        out_shape=[jax.ShapeDtypeStruct((48, TW), F32), jax.ShapeDtypeStruct((2, PX, PX), BF)],
        in_specs=[HBM] * 6,
        out_specs=[VMEM] * 2,
        scratch_shapes=[
            *halving_scratch(3, 16, TW), *halving_scratch(1, 48, HALO),
            vmem((2, 16, 16, PX), BF), dma((1,)),
            vmem((48, HALO), F32), vmem((48, HALO), F32), vmem((4, 16, TW), F32),
            vmem((2, 16, 16, PX), BF), vmem((2, 4, 16, PX), F32),
            vmem((2, 3, 4, 16, PX), BF), vmem((2, 3, 4, 16, PX), BF),
            vmem((2, 3, 16, PX), BF), vmem((2, 3, 16, PX), BF),
            vmem((2, 16, PX), F32), vmem((2, 32, 16, PX), BF),
            vmem((6, PX + 2 * OWN + 8, 128), F32), vmem((3, 8, 8, 128), F32), vmem((3, 2, 8, 128), F32),
            vmem((8, OWN, 128), F32),
            pltpu.SMEM((1, 32, 8, 128), jnp.int32), vmem((2, PX, PX), F32), vmem((256, 256), BF),
            dma((4,)), dma((4,)), dma((RING_SENDS,)), dma((RING_SENDS,)), dma((3,)),
        ],
        compiler_params=pltpu.CompilerParams(
            collective_id=1, has_side_effects=True, vmem_limit_bytes=62 * MB),
        cost_estimate=pl.CostEstimate(flops=0, bytes_accessed=60 * MB, transcendentals=0),
        name="reduce_all",
    )(spots, main, spill, sums, probe, join)


def local(obj, probe, amps, rows, cols):
    total = rows.shape[0] * lax.axis_size("obj") * lax.axis_size("pat")
    split = splitter()
    main, halo, spots = gather(obj, rows, cols, jnp.asarray(split))
    sums = work(rows, cols, main, halo, probe, amps, jnp.asarray(split))
    own, probe_sum = reduce_all(spots, *sums, probe, jnp.asarray(split.T))
    obj_step = own.reshape(2, OWN, TW)
    probe_grad = probe_sum.astype(F32) * (1.0 / math.sqrt(total))
    return (obj_step, probe_grad)


def solution(mesh):
    placed = (
        P(None, "pat", "obj"),
        P(),
        P(("obj", "pat"), None, None),
        P(("obj", "pat")),
        P(("obj", "pat")),
    )
    return jax.shard_map(
        local, mesh=mesh, in_specs=placed, out_specs=(P(None, "pat", "obj"), P()), check_vma=False
    )
```

```python
import functools
import math

import jax
import jax.numpy as jnp
import ml_dtypes
import numpy as np
from jax import lax
from jax.experimental import pallas as pl
from jax.experimental.pallas import tpu as pltpu
from jax.sharding import PartitionSpec as P

PX = 512
HALO = 256
H = 768
TW = 1024
WIDE = TW + HALO
OWN = 24
BF = jnp.bfloat16
F32 = jnp.float32
MESH = pl.DeviceIdType.MESH
DIMS = ("xa", "za", "xb", "zb")
MB = 1 << 20


def bits_of(pat):
    x, z = (pat // 2) % 4, pat // 8
    return {
        "core": pat % 2,
        "xa": (x // 2 + x) % 2,
        "xb": x // 2,
        "za": (z // 2 + z) % 2,
        "zb": z // 2,
    }


def partner_of(pat, dim):
    core, x, z = pat % 2, (pat // 2) % 4, pat // 8
    if dim == "core":
        core = 1 - core
    elif dim == "xa":
        x = x + 1 - 2 * (x % 2)
    elif dim == "xb":
        x = 3 - x
    elif dim == "za":
        z = z + 1 - 2 * (z % 2)
    else:
        z = 3 - z
    return (z * 4 + x) * 2 + core


def order(part):
    return [DIMS[(part + k) % 4] for k in range(4)]


def gather_place(pat, part):
    bits = bits_of(pat)
    return bits["core"] * 16 + sum(bits[d] * 2**k for k, d in enumerate(order(part)))


def scatter_place(pat, part):
    bits = bits_of(pat)
    return bits["core"] * 16 + sum(bits[d] * 2 ** (3 - k) for k, d in enumerate(order(part)))


def corner_of(pat, one, two):
    return partner_of(partner_of(pat, one), two)


def ring_place(pat, layer):
    core, x, z = pat % 2, (pat // 2) % 4, pat // 8
    return core * 16 + (x * 4 + z if layer == 0 else z * 4 + x)


def along(pat, axis, k):
    core, x, z = pat % 2, (pat // 2) % 4, pat // 8
    if axis == "x":
        x = (x + k) % 4
    else:
        z = (z + k) % 4
    return (z * 4 + x) * 2 + core


CORNERS = [(DIMS[k], DIMS[(k + 1) % 4]) for k in range(4)]


def greet(peers):
    barrier = pltpu.get_barrier_semaphore()
    for peer in peers:
        pl.semaphore_signal(barrier, inc=1, device_id=peer, device_id_type=MESH)
    pl.semaphore_wait(barrier, len(peers))


class Doubling:
    def __init__(self, buf, part, me, sems):
        self.buf, self.part, self.sems = buf, part, sems
        self.y, self.pat = me
        self.place = gather_place(self.pat, part)
        self.dims = order(part)
        self.made = {}

    def copy(self, name, src, dst, pat):
        send, recv = self.sems
        slot = len(self.made)
        made = pltpu.make_async_remote_copy(
            src_ref=src, dst_ref=dst, send_sem=send.at[self.part, slot], recv_sem=recv.at[self.part, slot],
            device_id=(self.y, pat), device_id_type=MESH,
        )
        made.start()
        self.made[name] = made

    def four(self, flip_two, flip_three):
        two, three = (self.place // 4) % 2, (self.place // 8) % 2
        two = 1 - two if flip_two else two
        three = 1 - three if flip_three else three
        return self.buf.at[self.part, pl.ds(self.place // 16 * 16 + three * 8 + two * 4, 4)]

    def near(self, name, ref):
        self.copy(name, ref, ref, partner_of(self.pat, "core"))

    def first(self, src):
        mine = self.buf.at[self.part, pl.ds(self.place, 1)]
        self.copy("a0", src, mine, partner_of(self.pat, self.dims[0]))
        self.copy("a1", src, mine, partner_of(self.pat, self.dims[1]))
        self.copy("a2", src, mine, corner_of(self.pat, self.dims[0], self.dims[1]))

    def second(self):
        for name in ("a0", "a1", "a2"):
            self.made[name].wait_recv()
        mine = self.four(False, False)
        self.copy("b", mine, mine, partner_of(self.pat, self.dims[2]))

    def third(self):
        mine = self.four(False, False)
        self.copy("c0", mine, mine, partner_of(self.pat, self.dims[3]))
        self.near("n0", mine)

    def fourth(self):
        self.made["b"].wait_recv()
        came = self.four(True, False)
        self.copy("c1", came, came, partner_of(self.pat, self.dims[3]))
        self.near("n1", came)

    def fifth(self, k):
        self.made[("c0", "c1")[k]].wait_recv()
        self.near(("n2", "n3")[k], self.four(k == 1, True))

    def finish(self):
        for name, made in self.made.items():
            made.wait_send()
            if name[0] == "n":
                made.wait_recv()


def gather_all(parts):
    for part in parts:
        part.second()
    for part in parts:
        part.third()
    for part in parts:
        part.fourth()
    for k in range(2):
        for part in parts:
            part.fifth(k)


def gather_kernel(obj_ref, rows_ref, cols_ref, split_ref, main_ref, halo_ref, spots_ref,
                  obj, split, at, mine, edge, masked, pos, pos_in, pos_all,
                  msend, mrecv, hsend, hrecv, psend, precv, esem, lsem):
    y, pat = lax.axis_index("obj"), lax.axis_index("pat")
    rows = lax.axis_size("obj")
    left, right = (y + rows - 1) % rows, (y + 1) % rows
    loads = [
        pltpu.make_async_copy(src, dst, lsem.at[8 + k])
        for k, (src, dst) in enumerate(
            ((obj_ref, obj), (split_ref, split), (rows_ref, at.at[0]), (cols_ref, at.at[1])))
    ]
    for made in loads:
        made.start()
    greet([(left, pat), (right, pat)] + [(y, partner_of(pat, d)) for d in DIMS + ("core",)]
          + [(y, corner_of(pat, *c)) for c in CORNERS])
    for made in loads:
        made.wait()
    mains = [Doubling(main_ref, p, (y, pat), (msend, mrecv)) for p in range(4)]
    halos = [Doubling(halo_ref, p, (y, pat), (hsend, hrecv)) for p in range(3)]
    spots = Doubling(spots_ref, 0, (y, pat), (psend, precv))
    own = []
    line = lax.broadcasted_iota(jnp.int32, (1, 8, 128), 1)
    lane = lax.broadcasted_iota(jnp.int32, (1, 8, 128), 2)
    for p, part in enumerate(mains):
        here = pl.ds(p * 256, 256)
        mine[0, :, here] = dot(obj[0, :, here], split[...]).astype(BF)
        if p == 0:
            send_edge = pltpu.make_async_remote_copy(
                src_ref=mine.at[:, :, here], dst_ref=edge,
                send_sem=esem.at[0], recv_sem=esem.at[1], device_id=(left, pat), device_id_type=MESH,
            )
            send_edge.start()
            table = jnp.zeros((1, 8, 128), jnp.int32)
            for which in range(2):
                for k in range(3):
                    table = jnp.where((line == which) & (lane == k), at[which, k], table)
            pos[...] = table
            send_pos = pltpu.make_async_remote_copy(
                src_ref=pos, dst_ref=pos_in,
                send_sem=esem.at[2], recv_sem=esem.at[3], device_id=(right, pat), device_id_type=MESH,
            )
            send_pos.start()
    for p, part in enumerate(mains):
        part.first(mine.at[:, :, pl.ds(p * 256, 256)])
    send_edge.wait_recv()
    masked[...] = jnp.where(y == rows - 1, jnp.zeros_like(masked), edge[...])
    for p, part in enumerate(halos):
        part.first(masked.at[:, pl.ds(p * 16, 16)])
    send_pos.wait_recv()
    pos_all[...] = jnp.where(line < 2, pos[...], pltpu.roll(pos_in[...], 2, 1))
    spots.first(pos_all)
    for p, part in enumerate(mains):
        own.append(pltpu.make_async_copy(
            mine.at[:, :, pl.ds(p * 256, 256)], main_ref.at[p, pl.ds(part.place, 1)], lsem.at[p]))
    for p, part in enumerate(halos):
        own.append(pltpu.make_async_copy(
            masked.at[:, pl.ds(p * 16, 16)], halo_ref.at[p, pl.ds(part.place, 1)], lsem.at[4 + p]))
    own.append(pltpu.make_async_copy(pos_all, spots_ref.at[0, pl.ds(spots.place, 1)], lsem.at[7]))
    for made in own:
        made.start()
    for made in own:
        made.wait()
    parts = mains + halos + [spots]
    gather_all(parts)
    for part in parts:
        part.finish()
    send_edge.wait_send()
    send_pos.wait_send()


HBM = pl.BlockSpec(memory_space=pltpu.HBM)
VMEM = pl.BlockSpec(memory_space=pltpu.VMEM)


def gather(obj, rows, cols, split):
    dma = pltpu.SemaphoreType.DMA
    return pl.pallas_call(
        gather_kernel,
        out_shape=[
            jax.ShapeDtypeStruct((4, 32, 48, 256), BF),
            jax.ShapeDtypeStruct((3, 32, 16, 256), BF),
            jax.ShapeDtypeStruct((1, 32, 8, 128), jnp.int32),
        ],
        in_specs=[HBM] * 4,
        out_specs=[HBM] * 3,
        scratch_shapes=[
            pltpu.VMEM((1, 48, TW), BF),
            pltpu.VMEM((256, 256), BF),
            pltpu.SMEM((2, 3), jnp.int32),
            pltpu.VMEM((1, 48, TW), BF),
            pltpu.VMEM((1, 48, HALO), BF),
            pltpu.VMEM((1, 48, HALO), BF),
            pltpu.VMEM((1, 8, 128), jnp.int32),
            pltpu.VMEM((1, 8, 128), jnp.int32),
            pltpu.VMEM((1, 8, 128), jnp.int32),
            dma((4, 10)), dma((4, 10)), dma((3, 10)), dma((3, 10)), dma((1, 10)), dma((1, 10)),
            dma((4,)), dma((12,)),
        ],
        compiler_params=pltpu.CompilerParams(collective_id=0, has_side_effects=True, vmem_limit_bytes=62 * MB),
        cost_estimate=pl.CostEstimate(flops=0, bytes_accessed=60 * MB, transcendentals=0),
        name="gather",
    )(obj.reshape(1, 48, TW), rows, cols, split)


def tables():
    index = np.arange(PX)
    angle = (index[:, None] * index[None, :] % PX) * (2.0 * np.pi / PX)
    real = (np.cos(angle) / np.sqrt(PX)).astype(ml_dtypes.bfloat16)
    imag = (-np.sin(angle) / np.sqrt(PX)).astype(ml_dtypes.bfloat16)
    low = np.arange(256)
    sorted_low = np.concatenate([low[::2], low[1::2]])
    even, odd = index[::2], index[1::2]

    def left(re, im, rows, cols):
        pick = np.ix_(rows, cols)
        return np.block([[re[pick], -im[pick]], [im[pick], re[pick]]])

    def right(re, im, rows, cols):
        pick = np.ix_(rows, cols)
        return np.block([[re[pick], im[pick]], [-im[pick], re[pick]]])

    return np.stack([
        left(real, imag, sorted_low, even), left(real, imag, sorted_low, odd),
        right(real, imag, even, low), right(real, imag, odd, low),
        left(real, -imag, sorted_low, even), left(real, -imag, sorted_low, odd),
        right(real, -imag, low, even), right(real, -imag, low, odd),
    ])


def splitter():
    k = np.arange(256)
    return (np.arange(256)[:, None] == 2 * (k % 128) + k // 128).astype(ml_dtypes.bfloat16)


def dot(a, b):
    return jnp.dot(a, b, preferred_element_type=F32)


def moved(x, pick):
    high = x.astype(BF)
    rest = x - high.astype(F32)
    mid = rest.astype(BF)
    low = (rest - mid.astype(F32)).astype(BF)
    return dot(high, pick) + dot(mid, pick) + dot(low, pick)


SLABS = 6
ROWS = H + 8


def work_kernel(rows_hbm, cols_hbm, main_ref, halo_ref, probe_ref, amps_ref, tab_ref, split_ref, main_out, spill_out, probe_out,
                out_main, out_spill, out_probe, rows_ref, cols_ref, main, halo, split, tile, grad, probe, amps, tab, pacc, patch, exits, stack, flat, sems):
    loads = {}

    def load(name, src, dst, slot):
        loads[name] = pltpu.make_async_copy(src, dst, sems.at[slot])
        loads[name].start()

    plain = patch.at[1]
    for layer in range(2):
        for j in range(4):
            load(("probe", layer, j), probe_ref.at[layer, :, pl.ds(j * 128, 128)], plain.at[layer, j], layer * 4 + j)
    load("split", split_ref, split, 21)
    load("main", main_ref, main, 22)
    load("halo", halo_ref, halo, 23)
    load("rows", rows_hbm, rows_ref, 24)
    load("cols", cols_hbm, cols_ref, 25)
    @pl.loop(0, ROWS, step=8)
    def _(r):
        grad[:, :, :, pl.ds(pl.multiple_of(r, 8), 8), :] = jnp.zeros((2, 2, SLABS, 8, 128), F32)

    @pl.loop(0, PX, step=64)
    def _(r):
        pacc[:, :, :, pl.ds(pl.multiple_of(r, 64), 64), :] = jnp.zeros((2, 2, 2, 64, 128), F32)

    for layer in range(2):
        for j in range(4):
            loads["probe", layer, j].wait()
    loads["split"].wait()
    for layer in range(2):
        @pl.loop(0, PX, step=256)
        def _(r):
            here = pl.ds(pl.multiple_of(r, 256), 256)
            for j in range(2):
                pair = jnp.concatenate([plain[layer, 2 * j, here], plain[layer, 2 * j + 1, here]], axis=1)
                parted = moved(pair, split[...])
                for q in range(2):
                    probe[layer, q, j, here] = parted[:, q * 128:(q + 1) * 128]

    for name in ("main", "halo", "rows", "cols"):
        loads[name].wait()
    load("tab", tab_ref, tab, 8)
    for i in range(3):
        for j in range(4):
            load(("amps", i, j), amps_ref.at[i, :, pl.ds(j * 128, 128)], amps.at[i, j, pl.ds(0, PX)], 9 + i * 4 + j)

    @pl.loop(0, 32, unroll=4)
    def _(o):
        at = pl.multiple_of(o * OWN, 8)
        for p in range(4):
            block = main[p, gather_place(o, p)].astype(F32)
            for layer in range(2):
                for q in range(2):
                    tile[layer, q, p, pl.ds(at, OWN)] = block[layer * OWN:(layer + 1) * OWN, q * 128:(q + 1) * 128]
        part = [halo[p, gather_place(o, p)].astype(F32) for p in range(3)]
        for q in range(2):
            cs = slice(q * 128, (q + 1) * 128)
            tile[0, q, 4, pl.ds(at, 16)] = part[0][:, cs]
            tile[0, q, 4, pl.ds(at + 16, 8)] = part[1][:8, cs]
            tile[1, q, 4, pl.ds(at, 8)] = part[1][8:, cs]
            tile[1, q, 4, pl.ds(at + 8, 16)] = part[2][:, cs]

    lane = lax.broadcasted_iota(jnp.int32, (32, 128), 1)

    def places_of(slot):
        row, col = rows_ref[slot], cols_ref[slot]
        places = []
        for q in range(2):
            start = (col + q) // 2
            places.append(((col + q) % 2, start // 128, start % 128))
        return row, places

    def extract(slot, buf):
        row, places = places_of(slot)
        for q, (plane, b, m) in enumerate(places):
            for t in range(2):
                for i in range(8):
                    here = pl.ds(t + i * 64, 32, stride=2)
                    there = pl.ds(row + t + i * 64, 32, stride=2)
                    got = []
                    for layer in range(2):
                        turned = [pltpu.roll(tile[layer, plane, b + j, there, :], (128 - m) % 128, 1) for j in range(3)]
                        got.append([jnp.where(lane < 128 - m, turned[j], turned[j + 1]) for j in range(2)])
                    for j in range(2):
                        re, im = got[0][j], got[1][j]
                        pr, pi = probe[0, q, j, here, :], probe[1, q, j, here, :]
                        rs = slice(j * 256 + i * 32, j * 256 + (i + 1) * 32)
                        patch[buf, 0, t * 2 + q, rs] = re
                        patch[buf, 1, t * 2 + q, rs] = im
                        cs = slice(j * 128, (j + 1) * 128)
                        exits[t, q, i * 32:(i + 1) * 32, cs] = (pr * re - pi * im).astype(BF)
                        exits[t, q, 256 + i * 32:256 + (i + 1) * 32, cs] = (pr * im + pi * re).astype(BF)

    extract(0, 0)
    loads["tab"].wait()

    @pl.loop(0, 3)
    def _(slot):
        row, places = places_of(slot)
        buf = slot % 2

        def spread(to, which, total, other):
            for part in range(2):
                for upper, value in ((0, total), (1, other)):
                    for t in range(2):
                        at = part * 256 + t * 128
                        to[which, t * 256 + upper * 128:t * 256 + (upper + 1) * 128, part * 256:(part + 1) * 256] = (
                            value[at:at + 128].astype(BF))

        for q in range(2):
            even, odd = dot(tab[0], exits[0, q]), dot(tab[1], exits[1, q])
            spread(flat, q, even + odd, even - odd)

        for j in range(4):
            pltpu.make_async_copy(
                amps_ref.at[slot, :, pl.ds(j * 128, 128)], amps.at[slot, j, pl.ds(0, PX)], sems.at[9 + slot * 4 + j]).wait()

        for t in range(2):
            here = pl.ds(t * 256, 256)
            even, odd = dot(flat[0, here], tab[2]), dot(flat[1, here], tab[3])
            for upper, wave in ((0, even + odd), (1, even - odd)):
                for j in range(2):
                    re, im = wave[:, j * 128:(j + 1) * 128], wave[:, 256 + j * 128:256 + (j + 1) * 128]
                    amp = amps[slot, 2 * upper + j, pl.ds(t, 256, stride=2), :]
                    ratio = amp * lax.rsqrt(re * re + im * im + 1.0)
                    cs = slice(j * 128, (j + 1) * 128)
                    stack[t, upper, 0:256, cs] = (re * ratio - re).astype(BF)
                    stack[t, upper, 256:512, cs] = (im * ratio - im).astype(BF)

        extract(jnp.minimum(slot + 1, 2), 1 - buf)
        halves = []
        for upper in range(2):
            even, odd = dot(tab[4], stack[0, upper]), dot(tab[5], stack[1, upper])
            halves.append((even + odd, even - odd))
        spread(flat, 0, halves[0][0] + halves[1][0], halves[0][1] + halves[1][1])
        spread(flat, 1, halves[0][0] - halves[1][0], halves[0][1] - halves[1][1])

        @pl.loop(0, 2)
        def _(t):
            here = pl.ds(pl.multiple_of(t * 256, 256), 256)
            deltas = dot(flat[0, here], tab[6]), dot(flat[1, here], tab[7])
            for i in range(8):
                at = pl.ds(t + i * 64, 32, stride=2)
                there = pl.ds(row + t + i * 64, 32, stride=2)
                rs = slice(i * 32, (i + 1) * 32)
                for q, (plane, b, m) in enumerate(places):
                    turned = [[], []]
                    for j in range(2):
                        dr = deltas[q][rs, j * 128:(j + 1) * 128]
                        di = deltas[q][rs, 256 + j * 128:256 + (j + 1) * 128]
                        pr, pi = probe[0, q, j, at, :], probe[1, q, j, at, :]
                        qr, qi = (patch[buf, k, t * 2 + q, j * 256 + i * 32:j * 256 + (i + 1) * 32] for k in range(2))
                        pacc[0, q, j, at, :] += qr * dr + qi * di
                        pacc[1, q, j, at, :] += qr * di - qi * dr
                        turned[0].append(pltpu.roll(pr * dr + pi * di, m, 1))
                        turned[1].append(pltpu.roll(pr * di - pi * dr, m, 1))
                    for layer in range(2):
                        one, two = turned[layer]
                        grad[layer, plane, b, there, :] += jnp.where(lane >= m, one, 0.0)
                        grad[layer, plane, b + 1, there, :] += jnp.where(lane >= m, two, one)
                        grad[layer, plane, b + 2, there, :] += jnp.where(lane < m, two, 0.0)

    stores = []
    for core in range(2):
        @pl.loop(0, 16, unroll=4)
        def _(pair):
            o = 2 * pair + core
            at = pl.multiple_of(o * OWN, 8)
            spot = [scatter_place(o, p) for p in range(4)]
            for c in range(5):
                for q in range(2):
                    low = grad[0, q, c, pl.ds(at, OWN)]
                    high = grad[1, q, c, pl.ds(at, OWN)]
                    parts = (low[:16], jnp.concatenate([low[16:], high[:8]], axis=0), high[8:])
                    for p in range(3):
                        if c < 4:
                            cs = slice(c * 256 + q * 128, c * 256 + (q + 1) * 128)
                            out_main[p, spot[p], :, cs] = parts[p].astype(BF)
                        else:
                            cs = slice(q * 128, (q + 1) * 128)
                            out_spill[0, spot[3], p * 16:(p + 1) * 16, cs] = parts[p].astype(BF)
            rs = pl.ds(pl.multiple_of(o * 16, 16), 16)
            for layer in range(2):
                for j in range(2):
                    for q in range(2):
                        c = j * 256 + q * 128
                        out_probe[layer, ring_place(o, layer), :, c:c + 128] = pacc[layer, q, j, rs].astype(BF)

        half = pl.ds(core * 16, 16)
        for k, (src, dst) in enumerate(((out_main, main_out), (out_spill, spill_out), (out_probe, probe_out))):
            stores.append(pltpu.make_async_copy(src.at[:, half], dst.at[:, half], sems.at[26 + core * 3 + k]))
            stores[-1].start()
    for made in stores:
        made.wait()


def work(rows, cols, main, halo, probe, amps, split):
    vmem = pltpu.VMEM
    return pl.pallas_call(
        work_kernel,
        out_shape=[
            jax.ShapeDtypeStruct((3, 32, 16, TW), BF),
            jax.ShapeDtypeStruct((1, 32, 48, HALO), BF),
            jax.ShapeDtypeStruct((2, 32, 16, PX), BF),
        ],
        in_specs=[HBM] * 8,
        out_specs=[HBM] * 3,
        scratch_shapes=[
            vmem((3, 32, 16, TW), BF), vmem((1, 32, 48, HALO), BF), vmem((2, 32, 16, PX), BF),
            pltpu.SMEM((3,), jnp.int32), pltpu.SMEM((3,), jnp.int32),
            vmem((4, 32, 48, 256), BF), vmem((3, 32, 16, 256), BF), vmem((256, 256), BF),
            vmem((2, 2, SLABS, ROWS, 128), F32), vmem((2, 2, SLABS, ROWS, 128), F32),
            vmem((2, 2, 2, PX + 8, 128), F32), vmem((3, 4, PX + 8, 128), F32),
            vmem((8, PX, PX), BF),
            vmem((2, 2, 2, PX + 8, 128), F32), vmem((2, 2, 4, PX, 128), F32),
            vmem((2, 2, PX, 256), BF), vmem((2, 2, PX, 256), BF), vmem((2, PX, PX), BF),
            pltpu.SemaphoreType.DMA((32,)),
        ],
        compiler_params=pltpu.CompilerParams(vmem_limit_bytes=62 * MB),
        name="work",
    )(rows, cols, main, halo, probe, amps, jnp.asarray(tables()), split)


class Light:
    def __init__(self, spots, probe, lit, acc, spill_acc, first):
        self.spots, self.probe, self.lit, self.acc, self.spill_acc, self.first = spots, probe, lit, acc, spill_acc, first

    def prepare(self):
        for j in (0, 5):
            self.lit[j] = jnp.zeros((PX + 2 * OWN + 8, 128), F32)
        for j in range(4):
            self.lit[j + 1, 0:OWN] = jnp.zeros((OWN, 128), F32)
            self.lit[j + 1, PX + OWN:] = jnp.zeros((OWN + 8, 128), F32)

            @pl.loop(0, PX, step=64)
            def _(r):
                here = pl.ds(pl.multiple_of(r, 64), 64)
                cs = slice(j * 128, (j + 1) * 128)
                pr, pi = self.probe[0, here, cs], self.probe[1, here, cs]
                self.lit[j + 1, pl.ds(pl.multiple_of(r + OWN, 8), 64)] = pr * pr + pi * pi

        self.acc[...] = jnp.zeros_like(self.acc)
        self.spill_acc[...] = jnp.zeros_like(self.spill_acc)

    def add(self, begin, end):
        lane = lax.broadcasted_iota(jnp.int32, (8, 128), 1)

        @pl.loop(begin, end)
        def _(o):
            for k in range(3):
                for which, to, slabs, shift in ((0, self.acc, 8, 0), (1, self.spill_acc, 2, 8)):
                    row = self.spots[0, o, which * 2, k]
                    col = self.spots[0, o, which * 2 + 1, k]
                    start = jnp.clip(self.first - row + OWN, 0, PX + OWN)
                    b, m = col // 128, col % 128
                    last = [None] * 3
                    for j in range(-1, slabs):
                        slab = jnp.clip(j + shift - b + 1, 0, 5)
                        for t in range(3):
                            here = pltpu.roll(self.lit[slab, pl.ds(start + t, 8, stride=3), :], m, 1)
                            if j >= 0:
                                to[t, j] += jnp.where(lane >= m, here, last[t])
                            last[t] = here

    def result(self, y, out):
        for j in range(8):
            for t in range(3):
                value = self.acc[t, j]
                if j < 2:
                    value = value + jnp.where(y == 0, 0.0, self.spill_acc[t, j])
                out[j, pl.ds(t, 8, stride=3), :] = value


class Halving:
    def __init__(self, src, part, rotation, me, refs):
        (self.mine, self.came, self.acc0, self.acc1, self.s0, self.r0, self.s1, self.r1, self.s2, self.r2,
         self.fin, self.send, self.recv, self.local) = refs
        self.src, self.part = src, part
        self.y, self.pat = me
        self.own = self.pat % 2 * 16
        self.other = 16 - self.own
        self.dims = order(rotation)
        self.bits = [bits_of(self.pat)[d] for d in self.dims]
        self.made = {}

    def copy(self, name, src, dst, pat):
        slot = len(self.made)
        made = pltpu.make_async_remote_copy(
            src_ref=src, dst_ref=dst, send_sem=self.send.at[self.part, slot], recv_sem=self.recv.at[self.part, slot],
            device_id=(self.y, pat), device_id_type=MESH)
        made.start()
        self.made[name] = made

    def fetch(self):
        self.fetched = pltpu.make_async_copy(
            self.src.at[self.part, pl.ds(self.own, 16)], self.mine.at[self.part], self.local.at[self.part])
        self.fetched.start()

    def swap(self, half):
        at = (1 - self.bits[0]) * 8 if half == 0 else self.bits[0] * 8
        self.copy(("swap", half), self.src.at[self.part, pl.ds(self.other + at, 8)],
                  self.came.at[self.part, half], partner_of(self.pat, "core"))

    def zero(self, u):
        p, b0, b1 = self.part, self.bits[0], self.bits[1]
        if u == 0:
            self.fetched.wait()
            self.made["swap", 0].wait_recv()
        group = (1 - b1) * 4 if u == 0 else b1 * 4

        @pl.loop(0, 4)
        def _(j):
            at = group + j
            total = self.mine[p, (1 - b0) * 8 + at].astype(F32) + self.came[p, 0, at].astype(F32)
            self.s0[p, u, j] = total.astype(BF)

        self.copy(("zero", u), self.s0.at[p, u], self.r0.at[p, u], partner_of(self.pat, self.dims[0]))

    def zero_kept(self):
        p, b0 = self.part, self.bits[0]
        self.made["swap", 1].wait_recv()

        @pl.loop(0, 8)
        def _(j):
            self.acc0[p, j] = self.mine[p, b0 * 8 + j].astype(F32) + self.came[p, 1, j].astype(F32)

    def one(self):
        p, b1 = self.part, self.bits[1]
        self.made["zero", 0].wait_recv()

        @pl.loop(0, 4)
        def _(j):
            self.s1[p, j] = (self.acc0[p, (1 - b1) * 4 + j] + self.r0[p, 0, j].astype(F32)).astype(BF)

        self.copy("one", self.s1.at[p], self.r1.at[p], partner_of(self.pat, self.dims[1]))

    def one_kept(self):
        p, b1 = self.part, self.bits[1]
        self.made["zero", 1].wait_recv()

        @pl.loop(0, 4)
        def _(j):
            self.acc1[p, j] = self.acc0[p, b1 * 4 + j] + self.r0[p, 1, j].astype(F32)

    def two(self):
        p, b2, b3 = self.part, self.bits[2], self.bits[3]
        self.made["one"].wait_recv()

        def total(flip2, flip3):
            at = (1 - b2 if flip2 else b2) * 2 + (1 - b3 if flip3 else b3)
            return self.acc1[p, at] + self.r1[p, at].astype(F32)

        d2, d3 = self.dims[2], self.dims[3]
        for k, (flip2, flip3, pat) in enumerate((
            (True, True, corner_of(self.pat, d2, d3)),
            (True, False, partner_of(self.pat, d2)),
            (False, True, partner_of(self.pat, d3)),
        )):
            self.s2[p, k] = total(flip2, flip3).astype(BF)
            self.copy(("two", k), self.s2.at[p, k], self.r2.at[p, k], pat)
        self.fin[p] = total(False, False)

    def total(self):
        for k in range(3):
            self.made["two", k].wait_recv()
        return self.fin[self.part] + sum(self.r2[self.part, k].astype(F32) for k in range(3))

    def finish(self):
        for made in self.made.values():
            made.wait_send()


HALVING_REFS = 14


def halving_scratch(parts, rows, columns):
    block = (rows, columns)
    return [
        pltpu.VMEM((parts, 16, *block), BF), pltpu.VMEM((parts, 2, 8, *block), BF),
        pltpu.VMEM((parts, 8, *block), F32), pltpu.VMEM((parts, 4, *block), F32),
        pltpu.VMEM((parts, 2, 4, *block), BF), pltpu.VMEM((parts, 2, 4, *block), BF),
        pltpu.VMEM((parts, 4, *block), BF), pltpu.VMEM((parts, 4, *block), BF),
        pltpu.VMEM((parts, 3, *block), BF), pltpu.VMEM((parts, 3, *block), BF),
        pltpu.VMEM((parts, *block), F32),
        pltpu.SemaphoreType.DMA((parts, 8)), pltpu.SemaphoreType.DMA((parts, 8)), pltpu.SemaphoreType.DMA((parts,)),
    ]


class Rings:
    def __init__(self, src, me, mine, local, came, keep, s1, r1, s2, r2, fin, pbuf, sems):
        self.src, self.came, self.keep, self.pbuf = src, came, keep, pbuf
        self.mine, self.local = mine, local
        self.s1, self.r1, self.s2, self.r2, self.fin = s1, r1, s2, r2, fin
        self.y, self.pat = me
        self.core = self.pat % 2
        self.sibling = partner_of(self.pat, "core")
        self.sems, self.made, self.used = sems, {}, 0
        x, z = (self.pat // 2) % 4, self.pat // 8
        self.at = ((x, z), (z, x))
        self.axes = (("x", "z"), ("z", "x"))

    def send(self, name, src, dst, pat):
        send, recv = self.sems
        made = pltpu.make_async_remote_copy(
            src_ref=src, dst_ref=dst, send_sem=send.at[self.used], recv_sem=recv.at[self.used],
            device_id=(self.y, pat), device_id_type=MESH)
        made.start()
        self.made[name] = made
        self.used += 1

    def swap(self):
        for h in range(2):
            self.send(("swap", h), self.src.at[h, pl.ds((1 - self.core) * 16, 16)], self.came.at[h], self.sibling)

    def fetch(self):
        self.fetched = pltpu.make_async_copy(self.src.at[:, pl.ds(self.core * 16, 16)], self.mine, self.local.at[0])
        self.fetched.start()

    def ring_one(self):
        self.fetched.wait()
        for h in range(2):
            self.made["swap", h].wait_recv()
            f = self.at[h][0]

            @pl.loop(0, 4)
            def _(j):
                at = f * 4 + j
                self.keep[h, j] = self.mine[h, at].astype(F32) + self.came[h, at].astype(F32)

            for k in range(1, 4):
                to = (f + k) % 4

                @pl.loop(0, 4)
                def _(j):
                    at = to * 4 + j
                    total = self.mine[h, at].astype(F32) + self.came[h, at].astype(F32)
                    self.s1[h, k - 1, j] = total.astype(BF)

                self.send(("one", h, k), self.s1.at[h, k - 1], self.r1.at[h, k - 1],
                          along(self.pat, self.axes[h][0], k))

    def ring_two(self):
        for h in range(2):
            for k in range(1, 4):
                self.made["one", h, k].wait_recv()
            g = self.at[h][1]

            def total(j):
                return self.keep[h, j] + sum(self.r1[h, k, j].astype(F32) for k in range(3))

            for k in range(1, 4):
                self.s2[h, k - 1] = total((g + k) % 4).astype(BF)
                self.send(("two", h, k), self.s2.at[h, k - 1], self.r2.at[h, k - 1],
                          along(self.pat, self.axes[h][1], k))
            self.fin[h] = total(g)

    def total(self, h):
        for k in range(1, 4):
            self.made["two", h, k].wait_recv()
        return self.fin[h] + sum(self.r2[h, k].astype(F32) for k in range(3))

    def gather_one(self, values):
        for h in range(2):
            place = ring_place(self.pat, h)
            self.pbuf[h, pl.ds(place, 1)] = values[h].reshape(1, 16, PX)
            mine = self.pbuf.at[h, pl.ds(place, 1)]
            for k in range(1, 4):
                self.send(("three", h, k), mine, mine, along(self.pat, self.axes[h][1], k))

    def gather_two(self):
        for h in range(2):
            for k in range(1, 4):
                self.made["three", h, k].wait_recv()
            mine = self.pbuf.at[h, pl.ds(self.core * 16 + self.at[h][0] * 4, 4)]
            for k in range(1, 4):
                self.send(("four", h, k), mine, mine, along(self.pat, self.axes[h][0], k))
            self.send(("near", h, 0), mine, mine, self.sibling)

    def gather_three(self):
        for k in (1, 3, 2):
            for h in range(2):
                self.made["four", h, k].wait_recv()
                came = self.pbuf.at[h, pl.ds(self.core * 16 + (self.at[h][0] + 4 - k) % 4 * 4, 4)]
                self.send(("near", h, k), came, came, self.sibling)

    def finish(self):
        for name, made in self.made.items():
            if name[0] == "near":
                made.wait_recv()
        for made in self.made.values():
            made.wait_send()


RING_SENDS = 2 + 4 * 6 + 8


def reduce_kernel(spots_ref, main_ref, spill_ref, sum_ref, probe_ref, join_hbm, obj_out, probe_out, *refs):
    y, pat = lax.axis_index("obj"), lax.axis_index("pat")
    me = (y, pat)
    rows = lax.axis_size("obj")
    mains = [Halving(main_ref, p, p, me, refs[:HALVING_REFS]) for p in range(3)]
    spills = [Halving(spill_ref, 0, 3, me, refs[HALVING_REFS:2 * HALVING_REFS])]
    (summine, rlocal, spill, spilled, ypro, came, keep, s1, r1, s2, r2, fin, pbuf, lit, acc, spill_acc, lights,
     spots, probe, join_ref, ysend, yrecv, psend, precv, lsem) = refs[2 * HALVING_REFS:]
    rings = Rings(sum_ref, me, summine, rlocal, came, keep, s1, r1, s2, r2, fin, pbuf, (psend, precv))
    light = Light(spots, probe, lit, acc, spill_acc, pat * OWN)
    objs = spills + mains
    rings.fetch()
    for part in objs:
        part.fetch()
    loads = [pltpu.make_async_copy(src, dst, lsem.at[k]) for k, (src, dst) in enumerate(
        ((probe_ref, probe), (spots_ref, spots), (join_hbm, join_ref)))]
    for made in loads:
        made.start()
    others = [((y + k) % rows, pat) for k in (1, 2, 3)]
    near = [(y, along(pat, axis, k)) for axis in ("x", "z") for k in (1, 2, 3)]
    greet(others + near + [(y, partner_of(pat, "core"))] + [(y, corner_of(pat, *c)) for c in CORNERS])
    rings.swap()
    for half in range(2):
        for part in objs:
            part.swap(half)
    rings.ring_one()
    for part in objs:
        part.zero(0)
    for made in loads:
        made.wait()
    light.prepare()
    rings.ring_two()
    for part in objs:
        part.zero(1)
    for part in objs:
        part.zero_kept()
    for part in objs:
        part.one()
    for h in range(2):
        ypro[pl.ds(y, 1), :, h * PX:(h + 1) * PX] = rings.total(h).reshape(1, 16, PX)
    mine = ypro.at[pl.ds(y, 1)]
    across = []
    for k, other in enumerate(others):
        across.append(pltpu.make_async_remote_copy(
            src_ref=mine, dst_ref=mine, send_sem=ysend.at[k], recv_sem=yrecv.at[k],
            device_id=other, device_id_type=MESH))
        across[-1].start()
    light.add(0, 16)
    for made in across:
        made.wait_recv()
    total = (ypro[0] + ypro[1] + ypro[2] + ypro[3]).astype(BF)
    joined = [dot(total[:, c * 256:(c + 1) * 256], join_ref[...]).astype(BF) for c in range(4)]
    rings.gather_one([jnp.concatenate(joined[2 * h:2 * h + 2], axis=1) for h in range(2)])
    for part in objs:
        part.one_kept()
    for part in objs:
        part.two()
    light.add(16, 24)
    rings.gather_two()
    spill[...] = spills[0].total()
    over = pltpu.make_async_remote_copy(
        src_ref=spill, dst_ref=spilled, send_sem=ysend.at[3], recv_sem=yrecv.at[3],
        device_id=others[0], device_id_type=MESH)
    over.start()
    light.add(24, 32)
    rings.gather_three()
    light.result(y, lights)
    totals = [part.total() for part in mains]
    over.wait_recv()
    chunks = []
    for c in range(4):
        whole = jnp.concatenate([total[:, c * 256:(c + 1) * 256] for total in totals], axis=0)
        chunks.append(whole + jnp.where(y == 0, 0.0, spilled[...]) if c == 0 else whole)
    joined = moved(jnp.concatenate(chunks, axis=0), join_ref[...])
    for j in range(8):
        here = joined[j // 2 * 48:(j // 2 + 1) * 48, (j % 2) * 128:(j % 2 + 1) * 128]
        under = lights[j] + 1.0
        for layer in range(2):
            obj_out[layer * OWN:(layer + 1) * OWN, j * 128:(j + 1) * 128] = here[layer * OWN:(layer + 1) * OWN] / under
    rings.finish()
    store = pltpu.make_async_copy(pbuf, probe_out, lsem.at[3])
    store.start()
    for part in objs:
        part.finish()
    for made in across + [over]:
        made.wait_send()
    store.wait()


def reduce_all(spots, main, spill, sums, probe, join):
    dma = pltpu.SemaphoreType.DMA
    vmem = pltpu.VMEM
    return pl.pallas_call(
        reduce_kernel,
        out_shape=[jax.ShapeDtypeStruct((48, TW), F32), jax.ShapeDtypeStruct((2, 32, 16, PX), BF)],
        in_specs=[HBM] * 6,
        out_specs=[VMEM, HBM],
        scratch_shapes=[
            *halving_scratch(3, 16, TW), *halving_scratch(1, 48, HALO),
            vmem((2, 16, 16, PX), BF), dma((1,)),
            vmem((48, HALO), F32), vmem((48, HALO), F32), vmem((4, 16, TW), F32),
            vmem((2, 16, 16, PX), BF), vmem((2, 4, 16, PX), F32),
            vmem((2, 3, 4, 16, PX), BF), vmem((2, 3, 4, 16, PX), BF),
            vmem((2, 3, 16, PX), BF), vmem((2, 3, 16, PX), BF),
            vmem((2, 16, PX), F32), vmem((2, 32, 16, PX), BF),
            vmem((6, PX + 2 * OWN + 8, 128), F32), vmem((3, 8, 8, 128), F32), vmem((3, 2, 8, 128), F32),
            vmem((8, OWN, 128), F32),
            pltpu.SMEM((1, 32, 8, 128), jnp.int32), vmem((2, PX, PX), F32), vmem((256, 256), BF),
            dma((4,)), dma((4,)), dma((RING_SENDS,)), dma((RING_SENDS,)), dma((4,)),
        ],
        compiler_params=pltpu.CompilerParams(
            collective_id=1, has_side_effects=True, vmem_limit_bytes=62 * MB),
        cost_estimate=pl.CostEstimate(flops=0, bytes_accessed=60 * MB, transcendentals=0),
        name="reduce_all",
    )(spots, main, spill, sums, probe, join)


def finish_kernel(scale, own_ref, gathered_ref, obj_out, probe_out):
    h = pl.program_id(0)
    obj_out[...] = own_ref[...]
    for o in range(32):
        place = jnp.where(h == 0, ring_place(o, 0), ring_place(o, 1))
        probe_out[0, o * 16:(o + 1) * 16] = gathered_ref[0, place].astype(F32) * scale


def finish(scale, own, gathered):
    return pl.pallas_call(
        functools.partial(finish_kernel, scale),
        grid=(2,),
        out_shape=[jax.ShapeDtypeStruct((48, TW), F32), jax.ShapeDtypeStruct((2, PX, PX), F32)],
        in_specs=[
            pl.BlockSpec((24, TW), lambda h: (h, 0)),
            pl.BlockSpec((1, 32, 16, PX), lambda h: (h, 0, 0, 0)),
        ],
        out_specs=[
            pl.BlockSpec((24, TW), lambda h: (h, 0)),
            pl.BlockSpec((1, PX, PX), lambda h: (h, 0, 0)),
        ],
        compiler_params=pltpu.CompilerParams(vmem_limit_bytes=62 * MB),
        name="finish",
    )(own, gathered)


def local(obj, probe, amps, rows, cols):
    total = rows.shape[0] * lax.axis_size("obj") * lax.axis_size("pat")
    split = splitter()
    main, halo, spots = gather(obj, rows, cols, jnp.asarray(split))
    sums = work(rows, cols, main, halo, probe, amps, jnp.asarray(split))
    own, gathered = reduce_all(spots, *sums, probe, jnp.asarray(split.T))
    own, probe_grad = finish(1.0 / math.sqrt(total), own, gathered)
    obj_step = own.reshape(2, OWN, TW)
    return (obj_step, probe_grad)


def solution(mesh):
    placed = (
        P(None, "pat", "obj"),
        P(),
        P(("obj", "pat"), None, None),
        P(("obj", "pat")),
        P(("obj", "pat")),
    )
    return jax.shard_map(
        local, mesh=mesh, in_specs=placed, out_specs=(P(None, "pat", "obj"), P()), check_vma=False
    )
```

```python
import functools
import math

import jax
import jax.numpy as jnp
import ml_dtypes
import numpy as np
from jax import lax
from jax.experimental import pallas as pl
from jax.experimental.pallas import tpu as pltpu
from jax.sharding import PartitionSpec as P

PX = 512
HALO = 256
H = 768
TW = 1024
WIDE = TW + HALO
OWN = 24
BF = jnp.bfloat16
F32 = jnp.float32
MESH = pl.DeviceIdType.MESH
DIMS = ("xa", "za", "xb", "zb")
MB = 1 << 20


def bits_of(pat):
    x, z = (pat // 2) % 4, pat // 8
    return {
        "core": pat % 2,
        "xa": (x // 2 + x) % 2,
        "xb": x // 2,
        "za": (z // 2 + z) % 2,
        "zb": z // 2,
    }


def partner_of(pat, dim):
    core, x, z = pat % 2, (pat // 2) % 4, pat // 8
    if dim == "core":
        core = 1 - core
    elif dim == "xa":
        x = x + 1 - 2 * (x % 2)
    elif dim == "xb":
        x = 3 - x
    elif dim == "za":
        z = z + 1 - 2 * (z % 2)
    else:
        z = 3 - z
    return (z * 4 + x) * 2 + core


def order(part):
    return [DIMS[(part + k) % 4] for k in range(4)]


def gather_place(pat, part):
    bits = bits_of(pat)
    return bits["core"] * 16 + sum(bits[d] * 2**k for k, d in enumerate(order(part)))


def scatter_place(pat, part):
    bits = bits_of(pat)
    return bits["core"] * 16 + sum(bits[d] * 2 ** (3 - k) for k, d in enumerate(order(part)))


def corner_of(pat, one, two):
    return partner_of(partner_of(pat, one), two)


def ring_place(pat, layer):
    core, x, z = pat % 2, (pat // 2) % 4, pat // 8
    return core * 16 + (x * 4 + z if layer == 0 else z * 4 + x)


def along(pat, axis, k):
    core, x, z = pat % 2, (pat // 2) % 4, pat // 8
    if axis == "x":
        x = (x + k) % 4
    else:
        z = (z + k) % 4
    return (z * 4 + x) * 2 + core


CORNERS = [(DIMS[k], DIMS[(k + 1) % 4]) for k in range(4)]


def greet(peers):
    barrier = pltpu.get_barrier_semaphore()
    for peer in peers:
        pl.semaphore_signal(barrier, inc=1, device_id=peer, device_id_type=MESH)
    pl.semaphore_wait(barrier, len(peers))


class Doubling:
    def __init__(self, buf, part, me, sems):
        self.buf, self.part, self.sems = buf, part, sems
        self.y, self.pat = me
        self.place = gather_place(self.pat, part)
        self.dims = order(part)
        self.made = {}

    def copy(self, name, src, dst, pat):
        send, recv = self.sems
        slot = len(self.made)
        made = pltpu.make_async_remote_copy(
            src_ref=src, dst_ref=dst, send_sem=send.at[self.part, slot], recv_sem=recv.at[self.part, slot],
            device_id=(self.y, pat), device_id_type=MESH,
        )
        made.start()
        self.made[name] = made

    def four(self, flip_two, flip_three):
        two, three = (self.place // 4) % 2, (self.place // 8) % 2
        two = 1 - two if flip_two else two
        three = 1 - three if flip_three else three
        return self.buf.at[self.part, pl.ds(self.place // 16 * 16 + three * 8 + two * 4, 4)]

    def near(self, name, ref):
        self.copy(name, ref, ref, partner_of(self.pat, "core"))

    def first(self, src):
        mine = self.buf.at[self.part, pl.ds(self.place, 1)]
        self.copy("a0", src, mine, partner_of(self.pat, self.dims[0]))
        self.copy("a1", src, mine, partner_of(self.pat, self.dims[1]))
        self.copy("a2", src, mine, corner_of(self.pat, self.dims[0], self.dims[1]))

    def second(self):
        for name in ("a0", "a1", "a2"):
            self.made[name].wait_recv()
        mine = self.four(False, False)
        self.copy("b", mine, mine, partner_of(self.pat, self.dims[2]))

    def third(self):
        mine = self.four(False, False)
        self.copy("c0", mine, mine, partner_of(self.pat, self.dims[3]))
        self.near("n0", mine)

    def fourth(self):
        self.made["b"].wait_recv()
        came = self.four(True, False)
        self.copy("c1", came, came, partner_of(self.pat, self.dims[3]))
        self.near("n1", came)

    def fifth(self, k):
        self.made[("c0", "c1")[k]].wait_recv()
        self.near(("n2", "n3")[k], self.four(k == 1, True))

    def finish(self):
        for name, made in self.made.items():
            made.wait_send()
            if name[0] == "n":
                made.wait_recv()


def gather_all(parts):
    for part in parts:
        part.second()
    for part in parts:
        part.third()
    for part in parts:
        part.fourth()
    for k in range(2):
        for part in parts:
            part.fifth(k)


def gather_kernel(obj_ref, rows_ref, cols_ref, split_ref, main_ref, halo_ref, spots_ref,
                  obj, split, at, mine, edge, masked, pos, pos_in, pos_all,
                  msend, mrecv, hsend, hrecv, psend, precv, esem, lsem):
    y, pat = lax.axis_index("obj"), lax.axis_index("pat")
    rows = lax.axis_size("obj")
    left, right = (y + rows - 1) % rows, (y + 1) % rows
    loads = [
        pltpu.make_async_copy(src, dst, lsem.at[8 + k])
        for k, (src, dst) in enumerate(
            ((obj_ref, obj), (split_ref, split), (rows_ref, at.at[0]), (cols_ref, at.at[1])))
    ]
    for made in loads:
        made.start()
    greet([(left, pat), (right, pat)] + [(y, partner_of(pat, d)) for d in DIMS + ("core",)]
          + [(y, corner_of(pat, *c)) for c in CORNERS])
    for made in loads:
        made.wait()
    mains = [Doubling(main_ref, p, (y, pat), (msend, mrecv)) for p in range(4)]
    halos = [Doubling(halo_ref, p, (y, pat), (hsend, hrecv)) for p in range(3)]
    spots = Doubling(spots_ref, 0, (y, pat), (psend, precv))
    own = []
    line = lax.broadcasted_iota(jnp.int32, (1, 8, 128), 1)
    lane = lax.broadcasted_iota(jnp.int32, (1, 8, 128), 2)
    for p, part in enumerate(mains):
        here = pl.ds(p * 256, 256)
        mine[0, :, here] = dot(obj[0, :, here], split[...]).astype(BF)
        if p == 0:
            send_edge = pltpu.make_async_remote_copy(
                src_ref=mine.at[:, :, here], dst_ref=edge,
                send_sem=esem.at[0], recv_sem=esem.at[1], device_id=(left, pat), device_id_type=MESH,
            )
            send_edge.start()
            table = jnp.zeros((1, 8, 128), jnp.int32)
            for which in range(2):
                for k in range(3):
                    table = jnp.where((line == which) & (lane == k), at[which, k], table)
            pos[...] = table
            send_pos = pltpu.make_async_remote_copy(
                src_ref=pos, dst_ref=pos_in,
                send_sem=esem.at[2], recv_sem=esem.at[3], device_id=(right, pat), device_id_type=MESH,
            )
            send_pos.start()
    for p, part in enumerate(mains):
        part.first(mine.at[:, :, pl.ds(p * 256, 256)])
    send_edge.wait_recv()
    masked[...] = jnp.where(y == rows - 1, jnp.zeros_like(masked), edge[...])
    for p, part in enumerate(halos):
        part.first(masked.at[:, pl.ds(p * 16, 16)])
    send_pos.wait_recv()
    pos_all[...] = jnp.where(line < 2, pos[...], pltpu.roll(pos_in[...], 2, 1))
    spots.first(pos_all)
    for p, part in enumerate(mains):
        own.append(pltpu.make_async_copy(
            mine.at[:, :, pl.ds(p * 256, 256)], main_ref.at[p, pl.ds(part.place, 1)], lsem.at[p]))
    for p, part in enumerate(halos):
        own.append(pltpu.make_async_copy(
            masked.at[:, pl.ds(p * 16, 16)], halo_ref.at[p, pl.ds(part.place, 1)], lsem.at[4 + p]))
    own.append(pltpu.make_async_copy(pos_all, spots_ref.at[0, pl.ds(spots.place, 1)], lsem.at[7]))
    for made in own:
        made.start()
    for made in own:
        made.wait()
    parts = mains + halos + [spots]
    gather_all(parts)
    for part in parts:
        part.finish()
    send_edge.wait_send()
    send_pos.wait_send()


HBM = pl.BlockSpec(memory_space=pltpu.HBM)
VMEM = pl.BlockSpec(memory_space=pltpu.VMEM)


def gather(obj, rows, cols, split):
    dma = pltpu.SemaphoreType.DMA
    return pl.pallas_call(
        gather_kernel,
        out_shape=[
            jax.ShapeDtypeStruct((4, 32, 48, 256), BF),
            jax.ShapeDtypeStruct((3, 32, 16, 256), BF),
            jax.ShapeDtypeStruct((1, 32, 8, 128), jnp.int32),
        ],
        in_specs=[HBM] * 4,
        out_specs=[HBM] * 3,
        scratch_shapes=[
            pltpu.VMEM((1, 48, TW), BF),
            pltpu.VMEM((256, 256), BF),
            pltpu.SMEM((2, 3), jnp.int32),
            pltpu.VMEM((1, 48, TW), BF),
            pltpu.VMEM((1, 48, HALO), BF),
            pltpu.VMEM((1, 48, HALO), BF),
            pltpu.VMEM((1, 8, 128), jnp.int32),
            pltpu.VMEM((1, 8, 128), jnp.int32),
            pltpu.VMEM((1, 8, 128), jnp.int32),
            dma((4, 10)), dma((4, 10)), dma((3, 10)), dma((3, 10)), dma((1, 10)), dma((1, 10)),
            dma((4,)), dma((12,)),
        ],
        compiler_params=pltpu.CompilerParams(collective_id=0, has_side_effects=True, vmem_limit_bytes=62 * MB),
        cost_estimate=pl.CostEstimate(flops=0, bytes_accessed=60 * MB, transcendentals=0),
        name="gather",
    )(obj.reshape(1, 48, TW), rows, cols, split)


def tables():
    index = np.arange(PX)
    angle = (index[:, None] * index[None, :] % PX) * (2.0 * np.pi / PX)
    real = (np.cos(angle) / np.sqrt(PX)).astype(ml_dtypes.bfloat16)
    imag = (-np.sin(angle) / np.sqrt(PX)).astype(ml_dtypes.bfloat16)
    low = np.arange(256)
    sorted_low = np.concatenate([low[::2], low[1::2]])
    even, odd = index[::2], index[1::2]

    def left(re, im, rows, cols):
        pick = np.ix_(rows, cols)
        return np.block([[re[pick], -im[pick]], [im[pick], re[pick]]])

    def right(re, im, rows, cols):
        pick = np.ix_(rows, cols)
        return np.block([[re[pick], im[pick]], [-im[pick], re[pick]]])

    return np.stack([
        left(real, imag, sorted_low, even), left(real, imag, sorted_low, odd),
        right(real, imag, even, low), right(real, imag, odd, low),
        left(real, -imag, sorted_low, even), left(real, -imag, sorted_low, odd),
        right(real, -imag, low, even), right(real, -imag, low, odd),
    ])


def splitter():
    k = np.arange(256)
    return (np.arange(256)[:, None] == 2 * (k % 128) + k // 128).astype(ml_dtypes.bfloat16)


def dot(a, b):
    return jnp.dot(a, b, preferred_element_type=F32)


def moved(x, pick):
    high = x.astype(BF)
    rest = x - high.astype(F32)
    mid = rest.astype(BF)
    low = (rest - mid.astype(F32)).astype(BF)
    return dot(high, pick) + dot(mid, pick) + dot(low, pick)


SLABS = 6
ROWS = H + 8


def work_kernel(rows_hbm, cols_hbm, main_ref, halo_ref, probe_ref, amps_ref, tab_ref, split_ref, main_out, spill_out, probe_out,
                out_main, out_spill, out_probe, rows_ref, cols_ref, main, halo, split, tile, grad, probe, amps, tab, pacc, patch, exits, stack, flat, sems):
    loads = {}

    def load(name, src, dst, slot):
        loads[name] = pltpu.make_async_copy(src, dst, sems.at[slot])
        loads[name].start()

    plain = patch.at[1]
    for layer in range(2):
        for j in range(4):
            load(("probe", layer, j), probe_ref.at[layer, :, pl.ds(j * 128, 128)], plain.at[layer, j], layer * 4 + j)
    load("split", split_ref, split, 21)
    load("main", main_ref, main, 22)
    load("halo", halo_ref, halo, 23)
    load("rows", rows_hbm, rows_ref, 24)
    load("cols", cols_hbm, cols_ref, 25)
    @pl.loop(0, ROWS, step=8)
    def _(r):
        grad[:, :, :, pl.ds(pl.multiple_of(r, 8), 8), :] = jnp.zeros((2, 2, SLABS, 8, 128), F32)

    @pl.loop(0, PX, step=64)
    def _(r):
        pacc[:, :, :, pl.ds(pl.multiple_of(r, 64), 64), :] = jnp.zeros((2, 2, 2, 64, 128), F32)

    for layer in range(2):
        for j in range(4):
            loads["probe", layer, j].wait()
    loads["split"].wait()
    for layer in range(2):
        @pl.loop(0, PX, step=256)
        def _(r):
            here = pl.ds(pl.multiple_of(r, 256), 256)
            for j in range(2):
                pair = jnp.concatenate([plain[layer, 2 * j, here], plain[layer, 2 * j + 1, here]], axis=1)
                parted = moved(pair, split[...])
                for q in range(2):
                    probe[layer, q, j, here] = parted[:, q * 128:(q + 1) * 128]

    for name in ("main", "halo", "rows", "cols"):
        loads[name].wait()
    load("tab", tab_ref, tab, 8)
    for i in range(3):
        for j in range(4):
            load(("amps", i, j), amps_ref.at[i, :, pl.ds(j * 128, 128)], amps.at[i, j, pl.ds(0, PX)], 9 + i * 4 + j)

    @pl.loop(0, 32, unroll=4)
    def _(o):
        at = pl.multiple_of(o * OWN, 8)
        for p in range(4):
            block = main[p, gather_place(o, p)].astype(F32)
            for layer in range(2):
                for q in range(2):
                    tile[layer, q, p, pl.ds(at, OWN)] = block[layer * OWN:(layer + 1) * OWN, q * 128:(q + 1) * 128]
        part = [halo[p, gather_place(o, p)].astype(F32) for p in range(3)]
        for q in range(2):
            cs = slice(q * 128, (q + 1) * 128)
            tile[0, q, 4, pl.ds(at, 16)] = part[0][:, cs]
            tile[0, q, 4, pl.ds(at + 16, 8)] = part[1][:8, cs]
            tile[1, q, 4, pl.ds(at, 8)] = part[1][8:, cs]
            tile[1, q, 4, pl.ds(at + 8, 16)] = part[2][:, cs]

    lane = lax.broadcasted_iota(jnp.int32, (32, 128), 1)

    def places_of(slot):
        row, col = rows_ref[slot], cols_ref[slot]
        places = []
        for q in range(2):
            start = (col + q) // 2
            places.append(((col + q) % 2, start // 128, start % 128))
        return row, places

    def extract(slot, buf):
        row, places = places_of(slot)
        for q, (plane, b, m) in enumerate(places):
            for t in range(2):
                for i in range(8):
                    here = pl.ds(t + i * 64, 32, stride=2)
                    there = pl.ds(row + t + i * 64, 32, stride=2)
                    got = []
                    for layer in range(2):
                        turned = [pltpu.roll(tile[layer, plane, b + j, there, :], (128 - m) % 128, 1) for j in range(3)]
                        got.append([jnp.where(lane < 128 - m, turned[j], turned[j + 1]) for j in range(2)])
                    for j in range(2):
                        re, im = got[0][j], got[1][j]
                        pr, pi = probe[0, q, j, here, :], probe[1, q, j, here, :]
                        rs = slice(j * 256 + i * 32, j * 256 + (i + 1) * 32)
                        patch[buf, 0, t * 2 + q, rs] = re
                        patch[buf, 1, t * 2 + q, rs] = im
                        cs = slice(j * 128, (j + 1) * 128)
                        exits[t, q, i * 32:(i + 1) * 32, cs] = (pr * re - pi * im).astype(BF)
                        exits[t, q, 256 + i * 32:256 + (i + 1) * 32, cs] = (pr * im + pi * re).astype(BF)

    extract(0, 0)
    loads["tab"].wait()

    @pl.loop(0, 3)
    def _(slot):
        row, places = places_of(slot)
        buf = slot % 2

        def spread(to, which, total, other):
            for part in range(2):
                for upper, value in ((0, total), (1, other)):
                    for t in range(2):
                        at = part * 256 + t * 128
                        to[which, t * 256 + upper * 128:t * 256 + (upper + 1) * 128, part * 256:(part + 1) * 256] = (
                            value[at:at + 128].astype(BF))

        for q in range(2):
            even, odd = dot(tab[0], exits[0, q]), dot(tab[1], exits[1, q])
            spread(flat, q, even + odd, even - odd)

        for j in range(4):
            pltpu.make_async_copy(
                amps_ref.at[slot, :, pl.ds(j * 128, 128)], amps.at[slot, j, pl.ds(0, PX)], sems.at[9 + slot * 4 + j]).wait()

        for t in range(2):
            here = pl.ds(t * 256, 256)
            even, odd = dot(flat[0, here], tab[2]), dot(flat[1, here], tab[3])
            for upper, wave in ((0, even + odd), (1, even - odd)):
                for j in range(2):
                    re, im = wave[:, j * 128:(j + 1) * 128], wave[:, 256 + j * 128:256 + (j + 1) * 128]
                    amp = amps[slot, 2 * upper + j, pl.ds(t, 256, stride=2), :]
                    ratio = amp * lax.rsqrt(re * re + im * im + 1.0)
                    cs = slice(j * 128, (j + 1) * 128)
                    stack[t, upper, 0:256, cs] = (re * ratio - re).astype(BF)
                    stack[t, upper, 256:512, cs] = (im * ratio - im).astype(BF)

        extract(jnp.minimum(slot + 1, 2), 1 - buf)
        halves = []
        for upper in range(2):
            even, odd = dot(tab[4], stack[0, upper]), dot(tab[5], stack[1, upper])
            halves.append((even + odd, even - odd))
        spread(flat, 0, halves[0][0] + halves[1][0], halves[0][1] + halves[1][1])
        spread(flat, 1, halves[0][0] - halves[1][0], halves[0][1] - halves[1][1])

        @pl.loop(0, 2)
        def _(t):
            here = pl.ds(pl.multiple_of(t * 256, 256), 256)
            deltas = dot(flat[0, here], tab[6]), dot(flat[1, here], tab[7])
            for i in range(8):
                at = pl.ds(t + i * 64, 32, stride=2)
                there = pl.ds(row + t + i * 64, 32, stride=2)
                rs = slice(i * 32, (i + 1) * 32)
                for q, (plane, b, m) in enumerate(places):
                    turned = [[], []]
                    for j in range(2):
                        dr = deltas[q][rs, j * 128:(j + 1) * 128]
                        di = deltas[q][rs, 256 + j * 128:256 + (j + 1) * 128]
                        pr, pi = probe[0, q, j, at, :], probe[1, q, j, at, :]
                        qr, qi = (patch[buf, k, t * 2 + q, j * 256 + i * 32:j * 256 + (i + 1) * 32] for k in range(2))
                        pacc[0, q, j, at, :] += qr * dr + qi * di
                        pacc[1, q, j, at, :] += qr * di - qi * dr
                        turned[0].append(pltpu.roll(pr * dr + pi * di, m, 1))
                        turned[1].append(pltpu.roll(pr * di - pi * dr, m, 1))
                    for layer in range(2):
                        one, two = turned[layer]
                        grad[layer, plane, b, there, :] += jnp.where(lane >= m, one, 0.0)
                        grad[layer, plane, b + 1, there, :] += jnp.where(lane >= m, two, one)
                        grad[layer, plane, b + 2, there, :] += jnp.where(lane < m, two, 0.0)

    stores = []
    for core in range(2):
        @pl.loop(0, 16, unroll=4)
        def _(pair):
            o = 2 * pair + core
            at = pl.multiple_of(o * OWN, 8)
            spot = [scatter_place(o, p) for p in range(4)]
            for c in range(5):
                for q in range(2):
                    low = grad[0, q, c, pl.ds(at, OWN)]
                    high = grad[1, q, c, pl.ds(at, OWN)]
                    parts = (low[:16], jnp.concatenate([low[16:], high[:8]], axis=0), high[8:])
                    for p in range(3):
                        if c < 4:
                            cs = slice(c * 256 + q * 128, c * 256 + (q + 1) * 128)
                            out_main[p, spot[p], :, cs] = parts[p].astype(BF)
                        else:
                            cs = slice(q * 128, (q + 1) * 128)
                            out_spill[0, spot[3], p * 16:(p + 1) * 16, cs] = parts[p].astype(BF)
            rs = pl.ds(pl.multiple_of(o * 16, 16), 16)
            for layer in range(2):
                for j in range(2):
                    for q in range(2):
                        c = j * 256 + q * 128
                        out_probe[layer, ring_place(o, layer), :, c:c + 128] = pacc[layer, q, j, rs].astype(BF)

        half = pl.ds(core * 16, 16)
        for k, (src, dst) in enumerate(((out_main, main_out), (out_spill, spill_out), (out_probe, probe_out))):
            stores.append(pltpu.make_async_copy(src.at[:, half], dst.at[:, half], sems.at[26 + core * 3 + k]))
            stores[-1].start()
    for made in stores:
        made.wait()


def work(rows, cols, main, halo, probe, amps, split):
    vmem = pltpu.VMEM
    return pl.pallas_call(
        work_kernel,
        out_shape=[
            jax.ShapeDtypeStruct((3, 32, 16, TW), BF),
            jax.ShapeDtypeStruct((1, 32, 48, HALO), BF),
            jax.ShapeDtypeStruct((2, 32, 16, PX), BF),
        ],
        in_specs=[HBM] * 8,
        out_specs=[HBM] * 3,
        scratch_shapes=[
            vmem((3, 32, 16, TW), BF), vmem((1, 32, 48, HALO), BF), vmem((2, 32, 16, PX), BF),
            pltpu.SMEM((3,), jnp.int32), pltpu.SMEM((3,), jnp.int32),
            vmem((4, 32, 48, 256), BF), vmem((3, 32, 16, 256), BF), vmem((256, 256), BF),
            vmem((2, 2, SLABS, ROWS, 128), F32), vmem((2, 2, SLABS, ROWS, 128), F32),
            vmem((2, 2, 2, PX + 8, 128), F32), vmem((3, 4, PX + 8, 128), F32),
            vmem((8, PX, PX), BF),
            vmem((2, 2, 2, PX + 8, 128), F32), vmem((2, 2, 4, PX, 128), F32),
            vmem((2, 2, PX, 256), BF), vmem((2, 2, PX, 256), BF), vmem((2, PX, PX), BF),
            pltpu.SemaphoreType.DMA((32,)),
        ],
        compiler_params=pltpu.CompilerParams(vmem_limit_bytes=62 * MB),
        name="work",
    )(rows, cols, main, halo, probe, amps, jnp.asarray(tables()), split)


class Light:
    def __init__(self, spots, probe, lit, acc, spill_acc, first):
        self.spots, self.probe, self.lit, self.acc, self.spill_acc, self.first = spots, probe, lit, acc, spill_acc, first

    def prepare(self):
        for j in (0, 5):
            self.lit[j] = jnp.zeros((PX + 2 * OWN + 8, 128), F32)
        for j in range(4):
            self.lit[j + 1, 0:OWN] = jnp.zeros((OWN, 128), F32)
            self.lit[j + 1, PX + OWN:] = jnp.zeros((OWN + 8, 128), F32)

            @pl.loop(0, PX, step=64)
            def _(r):
                here = pl.ds(pl.multiple_of(r, 64), 64)
                cs = slice(j * 128, (j + 1) * 128)
                pr, pi = self.probe[0, here, cs], self.probe[1, here, cs]
                self.lit[j + 1, pl.ds(pl.multiple_of(r + OWN, 8), 64)] = pr * pr + pi * pi

        self.acc[...] = jnp.zeros_like(self.acc)
        self.spill_acc[...] = jnp.zeros_like(self.spill_acc)

    def add(self, begin, end):
        lane = lax.broadcasted_iota(jnp.int32, (8, 128), 1)

        @pl.loop(begin, end)
        def _(o):
            for k in range(3):
                for which, to, slabs, shift in ((0, self.acc, 8, 0), (1, self.spill_acc, 2, 8)):
                    row = self.spots[0, o, which * 2, k]
                    col = self.spots[0, o, which * 2 + 1, k]
                    start = jnp.clip(self.first - row + OWN, 0, PX + OWN)
                    b, m = col // 128, col % 128
                    last = [None] * 3
                    for j in range(-1, slabs):
                        slab = jnp.clip(j + shift - b + 1, 0, 5)
                        for t in range(3):
                            here = pltpu.roll(self.lit[slab, pl.ds(start + t, 8, stride=3), :], m, 1)
                            if j >= 0:
                                to[t, j] += jnp.where(lane >= m, here, last[t])
                            last[t] = here

    def result(self, y, out):
        for j in range(8):
            for t in range(3):
                value = self.acc[t, j]
                if j < 2:
                    value = value + jnp.where(y == 0, 0.0, self.spill_acc[t, j])
                out[j, pl.ds(t, 8, stride=3), :] = value


class Halving:
    def __init__(self, src, part, rotation, me, refs):
        (self.mine, self.came, self.acc0, self.acc1, self.s0, self.r0, self.s1, self.r1, self.s2, self.r2,
         self.fin, self.send, self.recv, self.local) = refs
        self.src, self.part = src, part
        self.y, self.pat = me
        self.own = self.pat % 2 * 16
        self.other = 16 - self.own
        self.dims = order(rotation)
        self.bits = [bits_of(self.pat)[d] for d in self.dims]
        self.made = {}

    def copy(self, name, src, dst, pat):
        slot = len(self.made)
        made = pltpu.make_async_remote_copy(
            src_ref=src, dst_ref=dst, send_sem=self.send.at[self.part, slot], recv_sem=self.recv.at[self.part, slot],
            device_id=(self.y, pat), device_id_type=MESH)
        made.start()
        self.made[name] = made

    def fetch(self):
        self.fetched = pltpu.make_async_copy(
            self.src.at[self.part, pl.ds(self.own, 16)], self.mine.at[self.part], self.local.at[self.part])
        self.fetched.start()

    def swap(self, half):
        at = (1 - self.bits[0]) * 8 if half == 0 else self.bits[0] * 8
        self.copy(("swap", half), self.src.at[self.part, pl.ds(self.other + at, 8)],
                  self.came.at[self.part, half], partner_of(self.pat, "core"))

    def zero(self, u):
        p, b0, b1 = self.part, self.bits[0], self.bits[1]
        if u == 0:
            self.fetched.wait()
            self.made["swap", 0].wait_recv()
        group = (1 - b1) * 4 if u == 0 else b1 * 4

        @pl.loop(0, 4)
        def _(j):
            at = group + j
            total = self.mine[p, (1 - b0) * 8 + at].astype(F32) + self.came[p, 0, at].astype(F32)
            self.s0[p, u, j] = total.astype(BF)

        self.copy(("zero", u), self.s0.at[p, u], self.r0.at[p, u], partner_of(self.pat, self.dims[0]))

    def zero_kept(self):
        p, b0 = self.part, self.bits[0]
        self.made["swap", 1].wait_recv()

        @pl.loop(0, 8)
        def _(j):
            self.acc0[p, j] = self.mine[p, b0 * 8 + j].astype(F32) + self.came[p, 1, j].astype(F32)

    def one(self):
        p, b1 = self.part, self.bits[1]
        self.made["zero", 0].wait_recv()

        @pl.loop(0, 4)
        def _(j):
            self.s1[p, j] = (self.acc0[p, (1 - b1) * 4 + j] + self.r0[p, 0, j].astype(F32)).astype(BF)

        self.copy("one", self.s1.at[p], self.r1.at[p], partner_of(self.pat, self.dims[1]))

    def one_kept(self):
        p, b1 = self.part, self.bits[1]
        self.made["zero", 1].wait_recv()

        @pl.loop(0, 4)
        def _(j):
            self.acc1[p, j] = self.acc0[p, b1 * 4 + j] + self.r0[p, 1, j].astype(F32)

    def two(self):
        p, b2, b3 = self.part, self.bits[2], self.bits[3]
        self.made["one"].wait_recv()

        def total(flip2, flip3):
            at = (1 - b2 if flip2 else b2) * 2 + (1 - b3 if flip3 else b3)
            return self.acc1[p, at] + self.r1[p, at].astype(F32)

        d2, d3 = self.dims[2], self.dims[3]
        for k, (flip2, flip3, pat) in enumerate((
            (True, True, corner_of(self.pat, d2, d3)),
            (True, False, partner_of(self.pat, d2)),
            (False, True, partner_of(self.pat, d3)),
        )):
            self.s2[p, k] = total(flip2, flip3).astype(BF)
            self.copy(("two", k), self.s2.at[p, k], self.r2.at[p, k], pat)
        self.fin[p] = total(False, False)

    def total(self):
        for k in range(3):
            self.made["two", k].wait_recv()
        return self.fin[self.part] + sum(self.r2[self.part, k].astype(F32) for k in range(3))

    def finish(self):
        for made in self.made.values():
            made.wait_send()


HALVING_REFS = 14


def halving_scratch(parts, rows, columns):
    block = (rows, columns)
    return [
        pltpu.VMEM((parts, 16, *block), BF), pltpu.VMEM((parts, 2, 8, *block), BF),
        pltpu.VMEM((parts, 8, *block), F32), pltpu.VMEM((parts, 4, *block), F32),
        pltpu.VMEM((parts, 2, 4, *block), BF), pltpu.VMEM((parts, 2, 4, *block), BF),
        pltpu.VMEM((parts, 4, *block), BF), pltpu.VMEM((parts, 4, *block), BF),
        pltpu.VMEM((parts, 3, *block), BF), pltpu.VMEM((parts, 3, *block), BF),
        pltpu.VMEM((parts, *block), F32),
        pltpu.SemaphoreType.DMA((parts, 8)), pltpu.SemaphoreType.DMA((parts, 8)), pltpu.SemaphoreType.DMA((parts,)),
    ]


class Rings:
    def __init__(self, src, me, mine, local, came, keep, s1, r1, s2, r2, fin, pbuf, sems):
        self.src, self.came, self.keep, self.pbuf = src, came, keep, pbuf
        self.mine, self.local = mine, local
        self.s1, self.r1, self.s2, self.r2, self.fin = s1, r1, s2, r2, fin
        self.y, self.pat = me
        self.core = self.pat % 2
        self.sibling = partner_of(self.pat, "core")
        self.sems, self.made, self.used = sems, {}, 0
        x, z = (self.pat // 2) % 4, self.pat // 8
        self.at = ((x, z), (z, x))
        self.axes = (("x", "z"), ("z", "x"))

    def send(self, name, src, dst, pat):
        send, recv = self.sems
        made = pltpu.make_async_remote_copy(
            src_ref=src, dst_ref=dst, send_sem=send.at[self.used], recv_sem=recv.at[self.used],
            device_id=(self.y, pat), device_id_type=MESH)
        made.start()
        self.made[name] = made
        self.used += 1

    def swap(self):
        for h in range(2):
            self.send(("swap", h), self.src.at[h, pl.ds((1 - self.core) * 16, 16)], self.came.at[h], self.sibling)

    def fetch(self):
        self.fetched = pltpu.make_async_copy(self.src.at[:, pl.ds(self.core * 16, 16)], self.mine, self.local.at[0])
        self.fetched.start()

    def ring_one(self):
        self.fetched.wait()
        for h in range(2):
            self.made["swap", h].wait_recv()
            f = self.at[h][0]

            @pl.loop(0, 4)
            def _(j):
                at = f * 4 + j
                self.keep[h, j] = self.mine[h, at].astype(F32) + self.came[h, at].astype(F32)

            for k in (2, 1, 3):
                to = (f + k) % 4

                @pl.loop(0, 4)
                def _(j):
                    at = to * 4 + j
                    total = self.mine[h, at].astype(F32) + self.came[h, at].astype(F32)
                    self.s1[h, k - 1, j] = total.astype(BF)

                self.send(("one", h, k), self.s1.at[h, k - 1], self.r1.at[h, k - 1],
                          along(self.pat, self.axes[h][0], k))

    def ring_two(self):
        for h in range(2):
            for k in range(1, 4):
                self.made["one", h, k].wait_recv()
            g = self.at[h][1]

            def total(j):
                return self.keep[h, j] + sum(self.r1[h, k, j].astype(F32) for k in range(3))

            for k in (2, 1, 3):
                self.s2[h, k - 1] = total((g + k) % 4).astype(BF)
                self.send(("two", h, k), self.s2.at[h, k - 1], self.r2.at[h, k - 1],
                          along(self.pat, self.axes[h][1], k))
            self.fin[h] = total(g)

    def total(self, h):
        for k in range(1, 4):
            self.made["two", h, k].wait_recv()
        return self.fin[h] + sum(self.r2[h, k].astype(F32) for k in range(3))

    def gather_one(self, values):
        for h in range(2):
            place = ring_place(self.pat, h)
            self.pbuf[h, pl.ds(place, 1)] = values[h].reshape(1, 16, PX)
            mine = self.pbuf.at[h, pl.ds(place, 1)]
            for k in (2, 1, 3):
                self.send(("three", h, k), mine, mine, along(self.pat, self.axes[h][1], k))

    def gather_two(self):
        for h in range(2):
            for k in range(1, 4):
                self.made["three", h, k].wait_recv()
            mine = self.pbuf.at[h, pl.ds(self.core * 16 + self.at[h][0] * 4, 4)]
            for k in (2, 1, 3):
                self.send(("four", h, k), mine, mine, along(self.pat, self.axes[h][0], k))
            self.send(("near", h, 0), mine, mine, self.sibling)

    def gather_three(self):
        for k in (1, 3, 2):
            for h in range(2):
                self.made["four", h, k].wait_recv()
                came = self.pbuf.at[h, pl.ds(self.core * 16 + (self.at[h][0] + 4 - k) % 4 * 4, 4)]
                self.send(("near", h, k), came, came, self.sibling)

    def finish(self):
        for name, made in self.made.items():
            if name[0] == "near":
                made.wait_recv()
        for made in self.made.values():
            made.wait_send()


RING_SENDS = 2 + 4 * 6 + 8


def reduce_kernel(spots_ref, main_ref, spill_ref, sum_ref, probe_ref, join_hbm, obj_out, probe_out, *refs):
    y, pat = lax.axis_index("obj"), lax.axis_index("pat")
    me = (y, pat)
    rows = lax.axis_size("obj")
    mains = [Halving(main_ref, p, p, me, refs[:HALVING_REFS]) for p in range(3)]
    spills = [Halving(spill_ref, 0, 3, me, refs[HALVING_REFS:2 * HALVING_REFS])]
    (summine, rlocal, spill, spilled, ypro, came, keep, s1, r1, s2, r2, fin, pbuf, lit, acc, spill_acc, lights,
     spots, probe, join_ref, ysend, yrecv, psend, precv, lsem) = refs[2 * HALVING_REFS:]
    rings = Rings(sum_ref, me, summine, rlocal, came, keep, s1, r1, s2, r2, fin, pbuf, (psend, precv))
    light = Light(spots, probe, lit, acc, spill_acc, pat * OWN)
    objs = spills + mains
    rings.fetch()
    for part in objs:
        part.fetch()
    loads = [pltpu.make_async_copy(src, dst, lsem.at[k]) for k, (src, dst) in enumerate(
        ((probe_ref, probe), (spots_ref, spots), (join_hbm, join_ref)))]
    for made in loads:
        made.start()
    others = [((y + k) % rows, pat) for k in (1, 2, 3)]
    near = [(y, along(pat, axis, k)) for axis in ("x", "z") for k in (1, 2, 3)]
    greet(others + near + [(y, partner_of(pat, "core"))] + [(y, corner_of(pat, *c)) for c in CORNERS])
    rings.swap()
    for half in range(2):
        for part in objs:
            part.swap(half)
    rings.ring_one()
    for made in loads:
        made.wait()
    light.prepare()
    rings.ring_two()
    for part in objs:
        part.zero(0)
    for part in objs:
        part.zero(1)
    for part in objs:
        part.zero_kept()
    for h in range(2):
        ypro[pl.ds(y, 1), :, h * PX:(h + 1) * PX] = rings.total(h).reshape(1, 16, PX)
    mine = ypro.at[pl.ds(y, 1)]
    across = []
    for k, other in enumerate(others):
        across.append(pltpu.make_async_remote_copy(
            src_ref=mine, dst_ref=mine, send_sem=ysend.at[k], recv_sem=yrecv.at[k],
            device_id=other, device_id_type=MESH))
        across[-1].start()
    for part in objs:
        part.one()
    light.add(0, 16)
    for made in across:
        made.wait_recv()
    total = (ypro[0] + ypro[1] + ypro[2] + ypro[3]).astype(BF)
    joined = [dot(total[:, c * 256:(c + 1) * 256], join_ref[...]).astype(BF) for c in range(4)]
    rings.gather_one([jnp.concatenate(joined[2 * h:2 * h + 2], axis=1) for h in range(2)])
    for part in objs:
        part.one_kept()
    for part in objs:
        part.two()
    light.add(16, 24)
    rings.gather_two()
    spill[...] = spills[0].total()
    over = pltpu.make_async_remote_copy(
        src_ref=spill, dst_ref=spilled, send_sem=ysend.at[3], recv_sem=yrecv.at[3],
        device_id=others[0], device_id_type=MESH)
    over.start()
    light.add(24, 32)
    rings.gather_three()
    light.result(y, lights)
    totals = [part.total() for part in mains]
    over.wait_recv()
    chunks = []
    for c in range(4):
        whole = jnp.concatenate([total[:, c * 256:(c + 1) * 256] for total in totals], axis=0)
        chunks.append(whole + jnp.where(y == 0, 0.0, spilled[...]) if c == 0 else whole)
    joined = moved(jnp.concatenate(chunks, axis=0), join_ref[...])
    for j in range(8):
        here = joined[j // 2 * 48:(j // 2 + 1) * 48, (j % 2) * 128:(j % 2 + 1) * 128]
        under = lights[j] + 1.0
        for layer in range(2):
            obj_out[layer * OWN:(layer + 1) * OWN, j * 128:(j + 1) * 128] = here[layer * OWN:(layer + 1) * OWN] / under
    rings.finish()
    store = pltpu.make_async_copy(pbuf, probe_out, lsem.at[3])
    store.start()
    for part in objs:
        part.finish()
    for made in across + [over]:
        made.wait_send()
    store.wait()


def reduce_all(spots, main, spill, sums, probe, join):
    dma = pltpu.SemaphoreType.DMA
    vmem = pltpu.VMEM
    return pl.pallas_call(
        reduce_kernel,
        out_shape=[jax.ShapeDtypeStruct((48, TW), F32), jax.ShapeDtypeStruct((2, 32, 16, PX), BF)],
        in_specs=[HBM] * 6,
        out_specs=[VMEM, HBM],
        scratch_shapes=[
            *halving_scratch(3, 16, TW), *halving_scratch(1, 48, HALO),
            vmem((2, 16, 16, PX), BF), dma((1,)),
            vmem((48, HALO), F32), vmem((48, HALO), F32), vmem((4, 16, TW), F32),
            vmem((2, 16, 16, PX), BF), vmem((2, 4, 16, PX), F32),
            vmem((2, 3, 4, 16, PX), BF), vmem((2, 3, 4, 16, PX), BF),
            vmem((2, 3, 16, PX), BF), vmem((2, 3, 16, PX), BF),
            vmem((2, 16, PX), F32), vmem((2, 32, 16, PX), BF),
            vmem((6, PX + 2 * OWN + 8, 128), F32), vmem((3, 8, 8, 128), F32), vmem((3, 2, 8, 128), F32),
            vmem((8, OWN, 128), F32),
            pltpu.SMEM((1, 32, 8, 128), jnp.int32), vmem((2, PX, PX), F32), vmem((256, 256), BF),
            dma((4,)), dma((4,)), dma((RING_SENDS,)), dma((RING_SENDS,)), dma((4,)),
        ],
        compiler_params=pltpu.CompilerParams(
            collective_id=1, has_side_effects=True, vmem_limit_bytes=62 * MB),
        cost_estimate=pl.CostEstimate(flops=0, bytes_accessed=60 * MB, transcendentals=0),
        name="reduce_all",
    )(spots, main, spill, sums, probe, join)


def finish_kernel(scale, own_ref, gathered_ref, obj_out, probe_out):
    h = pl.program_id(0)
    obj_out[...] = own_ref[...]
    for o in range(32):
        place = jnp.where(h == 0, ring_place(o, 0), ring_place(o, 1))
        probe_out[0, o * 16:(o + 1) * 16] = gathered_ref[0, place].astype(F32) * scale


def finish(scale, own, gathered):
    return pl.pallas_call(
        functools.partial(finish_kernel, scale),
        grid=(2,),
        out_shape=[jax.ShapeDtypeStruct((48, TW), F32), jax.ShapeDtypeStruct((2, PX, PX), F32)],
        in_specs=[
            pl.BlockSpec((24, TW), lambda h: (h, 0)),
            pl.BlockSpec((1, 32, 16, PX), lambda h: (h, 0, 0, 0)),
        ],
        out_specs=[
            pl.BlockSpec((24, TW), lambda h: (h, 0)),
            pl.BlockSpec((1, PX, PX), lambda h: (h, 0, 0)),
        ],
        compiler_params=pltpu.CompilerParams(vmem_limit_bytes=62 * MB),
        name="finish",
    )(own, gathered)


def local(obj, probe, amps, rows, cols):
    total = rows.shape[0] * lax.axis_size("obj") * lax.axis_size("pat")
    split = splitter()
    main, halo, spots = gather(obj, rows, cols, jnp.asarray(split))
    sums = work(rows, cols, main, halo, probe, amps, jnp.asarray(split))
    own, gathered = reduce_all(spots, *sums, probe, jnp.asarray(split.T))
    own, probe_grad = finish(1.0 / math.sqrt(total), own, gathered)
    obj_step = own.reshape(2, OWN, TW)
    return (obj_step, probe_grad)


def solution(mesh):
    placed = (
        P(None, "pat", "obj"),
        P(),
        P(("obj", "pat"), None, None),
        P(("obj", "pat")),
        P(("obj", "pat")),
    )
    return jax.shard_map(
        local, mesh=mesh, in_specs=placed, out_specs=(P(None, "pat", "obj"), P()), check_vma=False
    )
```

```python
import functools
import math

import jax
import jax.numpy as jnp
import ml_dtypes
import numpy as np
from jax import lax
from jax.experimental import pallas as pl
from jax.experimental.pallas import tpu as pltpu
from jax.sharding import PartitionSpec as P

PX = 512
HALO = 256
H = 768
TW = 1024
WIDE = TW + HALO
OWN = 24
BF = jnp.bfloat16
F32 = jnp.float32
MESH = pl.DeviceIdType.MESH
DIMS = ("xa", "za", "xb", "zb")
MB = 1 << 20


def bits_of(pat):
    x, z = (pat // 2) % 4, pat // 8
    return {
        "core": pat % 2,
        "xa": (x // 2 + x) % 2,
        "xb": x // 2,
        "za": (z // 2 + z) % 2,
        "zb": z // 2,
    }


def partner_of(pat, dim):
    core, x, z = pat % 2, (pat // 2) % 4, pat // 8
    if dim == "core":
        core = 1 - core
    elif dim == "xa":
        x = x + 1 - 2 * (x % 2)
    elif dim == "xb":
        x = 3 - x
    elif dim == "za":
        z = z + 1 - 2 * (z % 2)
    else:
        z = 3 - z
    return (z * 4 + x) * 2 + core


def order(part):
    return [DIMS[(part + k) % 4] for k in range(4)]


def gather_place(pat, part):
    bits = bits_of(pat)
    return bits["core"] * 16 + sum(bits[d] * 2**k for k, d in enumerate(order(part)))


def scatter_place(pat, part):
    bits = bits_of(pat)
    return bits["core"] * 16 + sum(bits[d] * 2 ** (3 - k) for k, d in enumerate(order(part)))


def corner_of(pat, one, two):
    return partner_of(partner_of(pat, one), two)


def ring_place(pat, layer):
    core, x, z = pat % 2, (pat // 2) % 4, pat // 8
    return core * 16 + (x * 4 + z if layer == 0 else z * 4 + x)


def along(pat, axis, k):
    core, x, z = pat % 2, (pat // 2) % 4, pat // 8
    if axis == "x":
        x = (x + k) % 4
    else:
        z = (z + k) % 4
    return (z * 4 + x) * 2 + core


CORNERS = [(DIMS[k], DIMS[(k + 1) % 4]) for k in range(4)]


def greet(peers):
    barrier = pltpu.get_barrier_semaphore()
    for peer in peers:
        pl.semaphore_signal(barrier, inc=1, device_id=peer, device_id_type=MESH)
    pl.semaphore_wait(barrier, len(peers))


class Doubling:
    def __init__(self, buf, part, me, sems):
        self.buf, self.part, self.sems = buf, part, sems
        self.y, self.pat = me
        self.place = gather_place(self.pat, part)
        self.dims = order(part)
        self.made = {}

    def copy(self, name, src, dst, pat):
        send, recv = self.sems
        slot = len(self.made)
        made = pltpu.make_async_remote_copy(
            src_ref=src, dst_ref=dst, send_sem=send.at[self.part, slot], recv_sem=recv.at[self.part, slot],
            device_id=(self.y, pat), device_id_type=MESH,
        )
        made.start()
        self.made[name] = made

    def four(self, flip_two, flip_three):
        two, three = (self.place // 4) % 2, (self.place // 8) % 2
        two = 1 - two if flip_two else two
        three = 1 - three if flip_three else three
        return self.buf.at[self.part, pl.ds(self.place // 16 * 16 + three * 8 + two * 4, 4)]

    def near(self, name, ref):
        self.copy(name, ref, ref, partner_of(self.pat, "core"))

    def first(self, src):
        mine = self.buf.at[self.part, pl.ds(self.place, 1)]
        self.copy("a0", src, mine, partner_of(self.pat, self.dims[0]))
        self.copy("a1", src, mine, partner_of(self.pat, self.dims[1]))
        self.copy("a2", src, mine, corner_of(self.pat, self.dims[0], self.dims[1]))

    def second(self):
        for name in ("a0", "a1", "a2"):
            self.made[name].wait_recv()
        mine = self.four(False, False)
        self.copy("b", mine, mine, partner_of(self.pat, self.dims[2]))

    def third(self):
        mine = self.four(False, False)
        self.copy("c0", mine, mine, partner_of(self.pat, self.dims[3]))
        self.near("n0", mine)

    def fourth(self):
        self.made["b"].wait_recv()
        came = self.four(True, False)
        self.copy("c1", came, came, partner_of(self.pat, self.dims[3]))
        self.near("n1", came)

    def fifth(self, k):
        self.made[("c0", "c1")[k]].wait_recv()
        self.near(("n2", "n3")[k], self.four(k == 1, True))

    def finish(self):
        for name, made in self.made.items():
            made.wait_send()
            if name[0] == "n":
                made.wait_recv()


def gather_all(parts):
    for part in parts:
        part.second()
    for part in parts:
        part.third()
    for part in parts:
        part.fourth()
    for k in range(2):
        for part in parts:
            part.fifth(k)


def gather_kernel(obj_ref, rows_ref, cols_ref, split_ref, main_ref, halo_ref, spots_ref,
                  obj, split, at, mine, edge, masked, pos, pos_in, pos_all,
                  msend, mrecv, hsend, hrecv, psend, precv, esem, lsem):
    y, pat = lax.axis_index("obj"), lax.axis_index("pat")
    rows = lax.axis_size("obj")
    left, right = (y + rows - 1) % rows, (y + 1) % rows
    loads = [
        pltpu.make_async_copy(src, dst, lsem.at[8 + k])
        for k, (src, dst) in enumerate(
            ((obj_ref, obj), (split_ref, split), (rows_ref, at.at[0]), (cols_ref, at.at[1])))
    ]
    for made in loads:
        made.start()
    greet([(left, pat), (right, pat)] + [(y, partner_of(pat, d)) for d in DIMS + ("core",)]
          + [(y, corner_of(pat, *c)) for c in CORNERS])
    for made in loads:
        made.wait()
    mains = [Doubling(main_ref, p, (y, pat), (msend, mrecv)) for p in range(4)]
    halos = [Doubling(halo_ref, p, (y, pat), (hsend, hrecv)) for p in range(3)]
    spots = Doubling(spots_ref, 0, (y, pat), (psend, precv))
    own = []
    line = lax.broadcasted_iota(jnp.int32, (1, 8, 128), 1)
    lane = lax.broadcasted_iota(jnp.int32, (1, 8, 128), 2)
    for p, part in enumerate(mains):
        here = pl.ds(p * 256, 256)
        mine[0, :, here] = dot(obj[0, :, here], split[...]).astype(BF)
        if p == 0:
            send_edge = pltpu.make_async_remote_copy(
                src_ref=mine.at[:, :, here], dst_ref=edge,
                send_sem=esem.at[0], recv_sem=esem.at[1], device_id=(left, pat), device_id_type=MESH,
            )
            send_edge.start()
            table = jnp.zeros((1, 8, 128), jnp.int32)
            for which in range(2):
                for k in range(3):
                    table = jnp.where((line == which) & (lane == k), at[which, k], table)
            pos[...] = table
            send_pos = pltpu.make_async_remote_copy(
                src_ref=pos, dst_ref=pos_in,
                send_sem=esem.at[2], recv_sem=esem.at[3], device_id=(right, pat), device_id_type=MESH,
            )
            send_pos.start()
    for p, part in enumerate(mains):
        part.first(mine.at[:, :, pl.ds(p * 256, 256)])
    send_edge.wait_recv()
    masked[...] = jnp.where(y == rows - 1, jnp.zeros_like(masked), edge[...])
    for p, part in enumerate(halos):
        part.first(masked.at[:, pl.ds(p * 16, 16)])
    send_pos.wait_recv()
    pos_all[...] = jnp.where(line < 2, pos[...], pltpu.roll(pos_in[...], 2, 1))
    spots.first(pos_all)
    for p, part in enumerate(mains):
        own.append(pltpu.make_async_copy(
            mine.at[:, :, pl.ds(p * 256, 256)], main_ref.at[p, pl.ds(part.place, 1)], lsem.at[p]))
    for p, part in enumerate(halos):
        own.append(pltpu.make_async_copy(
            masked.at[:, pl.ds(p * 16, 16)], halo_ref.at[p, pl.ds(part.place, 1)], lsem.at[4 + p]))
    own.append(pltpu.make_async_copy(pos_all, spots_ref.at[0, pl.ds(spots.place, 1)], lsem.at[7]))
    for made in own:
        made.start()
    for made in own:
        made.wait()
    parts = mains + halos + [spots]
    gather_all(parts)
    for part in parts:
        part.finish()
    send_edge.wait_send()
    send_pos.wait_send()


HBM = pl.BlockSpec(memory_space=pltpu.HBM)
VMEM = pl.BlockSpec(memory_space=pltpu.VMEM)


def gather(obj, rows, cols, split):
    dma = pltpu.SemaphoreType.DMA
    return pl.pallas_call(
        gather_kernel,
        out_shape=[
            jax.ShapeDtypeStruct((4, 32, 48, 256), BF),
            jax.ShapeDtypeStruct((3, 32, 16, 256), BF),
            jax.ShapeDtypeStruct((1, 32, 8, 128), jnp.int32),
        ],
        in_specs=[HBM] * 4,
        out_specs=[HBM] * 3,
        scratch_shapes=[
            pltpu.VMEM((1, 48, TW), BF),
            pltpu.VMEM((256, 256), BF),
            pltpu.SMEM((2, 3), jnp.int32),
            pltpu.VMEM((1, 48, TW), BF),
            pltpu.VMEM((1, 48, HALO), BF),
            pltpu.VMEM((1, 48, HALO), BF),
            pltpu.VMEM((1, 8, 128), jnp.int32),
            pltpu.VMEM((1, 8, 128), jnp.int32),
            pltpu.VMEM((1, 8, 128), jnp.int32),
            dma((4, 10)), dma((4, 10)), dma((3, 10)), dma((3, 10)), dma((1, 10)), dma((1, 10)),
            dma((4,)), dma((12,)),
        ],
        compiler_params=pltpu.CompilerParams(collective_id=0, has_side_effects=True, vmem_limit_bytes=62 * MB),
        cost_estimate=pl.CostEstimate(flops=0, bytes_accessed=60 * MB, transcendentals=0),
        name="gather",
    )(obj.reshape(1, 48, TW), rows, cols, split)


def tables():
    index = np.arange(PX)
    angle = (index[:, None] * index[None, :] % PX) * (2.0 * np.pi / PX)
    real = (np.cos(angle) / np.sqrt(PX)).astype(ml_dtypes.bfloat16)
    imag = (-np.sin(angle) / np.sqrt(PX)).astype(ml_dtypes.bfloat16)
    low = np.arange(256)
    sorted_low = np.concatenate([low[::2], low[1::2]])
    even, odd = index[::2], index[1::2]

    def left(re, im, rows, cols):
        pick = np.ix_(rows, cols)
        return np.block([[re[pick], -im[pick]], [im[pick], re[pick]]])

    def right(re, im, rows, cols):
        pick = np.ix_(rows, cols)
        return np.block([[re[pick], im[pick]], [-im[pick], re[pick]]])

    return np.stack([
        left(real, imag, sorted_low, even), left(real, imag, sorted_low, odd),
        right(real, imag, even, low), right(real, imag, odd, low),
        left(real, -imag, sorted_low, even), left(real, -imag, sorted_low, odd),
        right(real, -imag, low, even), right(real, -imag, low, odd),
    ])


def splitter():
    k = np.arange(256)
    return (np.arange(256)[:, None] == 2 * (k % 128) + k // 128).astype(ml_dtypes.bfloat16)


def dot(a, b):
    return jnp.dot(a, b, preferred_element_type=F32)


def moved(x, pick):
    high = x.astype(BF)
    rest = x - high.astype(F32)
    mid = rest.astype(BF)
    low = (rest - mid.astype(F32)).astype(BF)
    return dot(high, pick) + dot(mid, pick) + dot(low, pick)


SLABS = 6
ROWS = H + 8


def work_kernel(rows_hbm, cols_hbm, main_ref, halo_ref, probe_ref, amps_ref, tab_ref, split_ref, main_out, spill_out, probe_out,
                out_main, out_spill, out_probe, rows_ref, cols_ref, main, halo, split, tile, grad, probe, amps, tab, pacc, patch, exits, stack, flat, sems):
    loads = {}

    def load(name, src, dst, slot):
        loads[name] = pltpu.make_async_copy(src, dst, sems.at[slot])
        loads[name].start()

    plain = patch.at[1]
    for layer in range(2):
        for j in range(4):
            load(("probe", layer, j), probe_ref.at[layer, :, pl.ds(j * 128, 128)], plain.at[layer, j], layer * 4 + j)
    load("split", split_ref, split, 21)
    load("main", main_ref, main, 22)
    load("halo", halo_ref, halo, 23)
    load("rows", rows_hbm, rows_ref, 24)
    load("cols", cols_hbm, cols_ref, 25)
    @pl.loop(0, ROWS, step=8)
    def _(r):
        grad[:, :, :, pl.ds(pl.multiple_of(r, 8), 8), :] = jnp.zeros((2, 2, SLABS, 8, 128), F32)

    @pl.loop(0, PX, step=64)
    def _(r):
        pacc[:, :, :, pl.ds(pl.multiple_of(r, 64), 64), :] = jnp.zeros((2, 2, 2, 64, 128), F32)

    for layer in range(2):
        for j in range(4):
            loads["probe", layer, j].wait()
    loads["split"].wait()
    for layer in range(2):
        @pl.loop(0, PX, step=256)
        def _(r):
            here = pl.ds(pl.multiple_of(r, 256), 256)
            for j in range(2):
                pair = jnp.concatenate([plain[layer, 2 * j, here], plain[layer, 2 * j + 1, here]], axis=1)
                parted = moved(pair, split[...])
                for q in range(2):
                    probe[layer, q, j, here] = parted[:, q * 128:(q + 1) * 128]

    for name in ("main", "halo", "rows", "cols"):
        loads[name].wait()
    load("tab", tab_ref, tab, 8)
    for i in range(3):
        for j in range(4):
            load(("amps", i, j), amps_ref.at[i, :, pl.ds(j * 128, 128)], amps.at[i, j, pl.ds(0, PX)], 9 + i * 4 + j)

    @pl.loop(0, 32, unroll=4)
    def _(o):
        at = pl.multiple_of(o * OWN, 8)
        for p in range(4):
            block = main[p, gather_place(o, p)].astype(F32)
            for layer in range(2):
                for q in range(2):
                    tile[layer, q, p, pl.ds(at, OWN)] = block[layer * OWN:(layer + 1) * OWN, q * 128:(q + 1) * 128]
        part = [halo[p, gather_place(o, p)].astype(F32) for p in range(3)]
        for q in range(2):
            cs = slice(q * 128, (q + 1) * 128)
            tile[0, q, 4, pl.ds(at, 16)] = part[0][:, cs]
            tile[0, q, 4, pl.ds(at + 16, 8)] = part[1][:8, cs]
            tile[1, q, 4, pl.ds(at, 8)] = part[1][8:, cs]
            tile[1, q, 4, pl.ds(at + 8, 16)] = part[2][:, cs]

    lane = lax.broadcasted_iota(jnp.int32, (32, 128), 1)

    def places_of(slot):
        row, col = rows_ref[slot], cols_ref[slot]
        places = []
        for q in range(2):
            start = (col + q) // 2
            places.append(((col + q) % 2, start // 128, start % 128))
        return row, places

    def extract(slot, buf):
        row, places = places_of(slot)
        for q, (plane, b, m) in enumerate(places):
            for t in range(2):
                for i in range(8):
                    here = pl.ds(t + i * 64, 32, stride=2)
                    there = pl.ds(row + t + i * 64, 32, stride=2)
                    got = []
                    for layer in range(2):
                        turned = [pltpu.roll(tile[layer, plane, b + j, there, :], (128 - m) % 128, 1) for j in range(3)]
                        got.append([jnp.where(lane < 128 - m, turned[j], turned[j + 1]) for j in range(2)])
                    for j in range(2):
                        re, im = got[0][j], got[1][j]
                        pr, pi = probe[0, q, j, here, :], probe[1, q, j, here, :]
                        rs = slice(j * 256 + i * 32, j * 256 + (i + 1) * 32)
                        patch[buf, 0, t * 2 + q, rs] = re
                        patch[buf, 1, t * 2 + q, rs] = im
                        cs = slice(j * 128, (j + 1) * 128)
                        exits[t, q, i * 32:(i + 1) * 32, cs] = (pr * re - pi * im).astype(BF)
                        exits[t, q, 256 + i * 32:256 + (i + 1) * 32, cs] = (pr * im + pi * re).astype(BF)

    extract(0, 0)
    loads["tab"].wait()

    @pl.loop(0, 3)
    def _(slot):
        row, places = places_of(slot)
        buf = slot % 2

        def spread(to, which, total, other):
            for part in range(2):
                for upper, value in ((0, total), (1, other)):
                    for t in range(2):
                        at = part * 256 + t * 128
                        to[which, t * 256 + upper * 128:t * 256 + (upper + 1) * 128, part * 256:(part + 1) * 256] = (
                            value[at:at + 128].astype(BF))

        for q in range(2):
            even, odd = dot(tab[0], exits[0, q]), dot(tab[1], exits[1, q])
            spread(flat, q, even + odd, even - odd)

        for j in range(4):
            pltpu.make_async_copy(
                amps_ref.at[slot, :, pl.ds(j * 128, 128)], amps.at[slot, j, pl.ds(0, PX)], sems.at[9 + slot * 4 + j]).wait()

        for t in range(2):
            here = pl.ds(t * 256, 256)
            even, odd = dot(flat[0, here], tab[2]), dot(flat[1, here], tab[3])
            for upper, wave in ((0, even + odd), (1, even - odd)):
                for j in range(2):
                    re, im = wave[:, j * 128:(j + 1) * 128], wave[:, 256 + j * 128:256 + (j + 1) * 128]
                    amp = amps[slot, 2 * upper + j, pl.ds(t, 256, stride=2), :]
                    ratio = amp * lax.rsqrt(re * re + im * im + 1.0)
                    cs = slice(j * 128, (j + 1) * 128)
                    stack[t, upper, 0:256, cs] = (re * ratio - re).astype(BF)
                    stack[t, upper, 256:512, cs] = (im * ratio - im).astype(BF)

        extract(jnp.minimum(slot + 1, 2), 1 - buf)
        halves = []
        for upper in range(2):
            even, odd = dot(tab[4], stack[0, upper]), dot(tab[5], stack[1, upper])
            halves.append((even + odd, even - odd))
        spread(flat, 0, halves[0][0] + halves[1][0], halves[0][1] + halves[1][1])
        spread(flat, 1, halves[0][0] - halves[1][0], halves[0][1] - halves[1][1])

        @pl.loop(0, 2)
        def _(t):
            here = pl.ds(pl.multiple_of(t * 256, 256), 256)
            deltas = dot(flat[0, here], tab[6]), dot(flat[1, here], tab[7])
            for i in range(8):
                at = pl.ds(t + i * 64, 32, stride=2)
                there = pl.ds(row + t + i * 64, 32, stride=2)
                rs = slice(i * 32, (i + 1) * 32)
                for q, (plane, b, m) in enumerate(places):
                    turned = [[], []]
                    for j in range(2):
                        dr = deltas[q][rs, j * 128:(j + 1) * 128]
                        di = deltas[q][rs, 256 + j * 128:256 + (j + 1) * 128]
                        pr, pi = probe[0, q, j, at, :], probe[1, q, j, at, :]
                        qr, qi = (patch[buf, k, t * 2 + q, j * 256 + i * 32:j * 256 + (i + 1) * 32] for k in range(2))
                        pacc[0, q, j, at, :] += qr * dr + qi * di
                        pacc[1, q, j, at, :] += qr * di - qi * dr
                        turned[0].append(pltpu.roll(pr * dr + pi * di, m, 1))
                        turned[1].append(pltpu.roll(pr * di - pi * dr, m, 1))
                    for layer in range(2):
                        one, two = turned[layer]
                        grad[layer, plane, b, there, :] += jnp.where(lane >= m, one, 0.0)
                        grad[layer, plane, b + 1, there, :] += jnp.where(lane >= m, two, one)
                        grad[layer, plane, b + 2, there, :] += jnp.where(lane < m, two, 0.0)

    stores = []
    for core in range(2):
        @pl.loop(0, 16, unroll=4)
        def _(pair):
            o = 2 * pair + core
            at = pl.multiple_of(o * OWN, 8)
            spot = [scatter_place(o, p) for p in range(4)]
            for c in range(5):
                for q in range(2):
                    low = grad[0, q, c, pl.ds(at, OWN)]
                    high = grad[1, q, c, pl.ds(at, OWN)]
                    parts = (low[:16], jnp.concatenate([low[16:], high[:8]], axis=0), high[8:])
                    for p in range(3):
                        if c < 4:
                            cs = slice(c * 256 + q * 128, c * 256 + (q + 1) * 128)
                            out_main[p, spot[p], :, cs] = parts[p].astype(BF)
                        else:
                            cs = slice(q * 128, (q + 1) * 128)
                            out_spill[0, spot[3], p * 16:(p + 1) * 16, cs] = parts[p].astype(BF)
            rs = pl.ds(pl.multiple_of(o * 16, 16), 16)
            for layer in range(2):
                for j in range(2):
                    for q in range(2):
                        c = j * 256 + q * 128
                        out_probe[layer, ring_place(o, layer), :, c:c + 128] = pacc[layer, q, j, rs].astype(BF)

        half = pl.ds(core * 16, 16)
        for k, (src, dst) in enumerate(((out_main, main_out), (out_spill, spill_out), (out_probe, probe_out))):
            stores.append(pltpu.make_async_copy(src.at[:, half], dst.at[:, half], sems.at[26 + core * 3 + k]))
            stores[-1].start()
    for made in stores:
        made.wait()


def work(rows, cols, main, halo, probe, amps, split):
    vmem = pltpu.VMEM
    return pl.pallas_call(
        work_kernel,
        out_shape=[
            jax.ShapeDtypeStruct((3, 32, 16, TW), BF),
            jax.ShapeDtypeStruct((1, 32, 48, HALO), BF),
            jax.ShapeDtypeStruct((2, 32, 16, PX), BF),
        ],
        in_specs=[HBM] * 8,
        out_specs=[HBM] * 3,
        scratch_shapes=[
            vmem((3, 32, 16, TW), BF), vmem((1, 32, 48, HALO), BF), vmem((2, 32, 16, PX), BF),
            pltpu.SMEM((3,), jnp.int32), pltpu.SMEM((3,), jnp.int32),
            vmem((4, 32, 48, 256), BF), vmem((3, 32, 16, 256), BF), vmem((256, 256), BF),
            vmem((2, 2, SLABS, ROWS, 128), F32), vmem((2, 2, SLABS, ROWS, 128), F32),
            vmem((2, 2, 2, PX + 8, 128), F32), vmem((3, 4, PX + 8, 128), F32),
            vmem((8, PX, PX), BF),
            vmem((2, 2, 2, PX + 8, 128), F32), vmem((2, 2, 4, PX, 128), F32),
            vmem((2, 2, PX, 256), BF), vmem((2, 2, PX, 256), BF), vmem((2, PX, PX), BF),
            pltpu.SemaphoreType.DMA((32,)),
        ],
        compiler_params=pltpu.CompilerParams(vmem_limit_bytes=62 * MB),
        name="work",
    )(rows, cols, main, halo, probe, amps, jnp.asarray(tables()), split)


class Light:
    def __init__(self, spots, probe, lit, acc, spill_acc, first):
        self.spots, self.probe, self.lit, self.acc, self.spill_acc, self.first = spots, probe, lit, acc, spill_acc, first

    def prepare(self):
        for j in (0, 5):
            self.lit[j] = jnp.zeros((PX + 2 * OWN + 8, 128), F32)
        for j in range(4):
            self.lit[j + 1, 0:OWN] = jnp.zeros((OWN, 128), F32)
            self.lit[j + 1, PX + OWN:] = jnp.zeros((OWN + 8, 128), F32)

            @pl.loop(0, PX, step=64)
            def _(r):
                here = pl.ds(pl.multiple_of(r, 64), 64)
                cs = slice(j * 128, (j + 1) * 128)
                pr, pi = self.probe[0, here, cs], self.probe[1, here, cs]
                self.lit[j + 1, pl.ds(pl.multiple_of(r + OWN, 8), 64)] = pr * pr + pi * pi

        self.acc[...] = jnp.zeros_like(self.acc)
        self.spill_acc[...] = jnp.zeros_like(self.spill_acc)

    def add(self, begin, end):
        lane = lax.broadcasted_iota(jnp.int32, (8, 128), 1)

        @pl.loop(begin, end)
        def _(o):
            for k in range(3):
                for which, to, slabs, shift in ((0, self.acc, 8, 0), (1, self.spill_acc, 2, 8)):
                    row = self.spots[0, o, which * 2, k]
                    col = self.spots[0, o, which * 2 + 1, k]
                    start = jnp.clip(self.first - row + OWN, 0, PX + OWN)
                    b, m = col // 128, col % 128
                    last = [None] * 3
                    for j in range(-1, slabs):
                        slab = jnp.clip(j + shift - b + 1, 0, 5)
                        for t in range(3):
                            here = pltpu.roll(self.lit[slab, pl.ds(start + t, 8, stride=3), :], m, 1)
                            if j >= 0:
                                to[t, j] += jnp.where(lane >= m, here, last[t])
                            last[t] = here

    def result(self, y, out):
        for j in range(8):
            for t in range(3):
                value = self.acc[t, j]
                if j < 2:
                    value = value + jnp.where(y == 0, 0.0, self.spill_acc[t, j])
                out[j, pl.ds(t, 8, stride=3), :] = value


class Halving:
    def __init__(self, src, part, rotation, me, refs):
        (self.mine, self.came, self.acc0, self.acc1, self.s0, self.r0, self.s1, self.r1, self.s2, self.r2,
         self.fin, self.send, self.recv, self.local) = refs
        self.src, self.part = src, part
        self.y, self.pat = me
        self.own = self.pat % 2 * 16
        self.other = 16 - self.own
        self.dims = order(rotation)
        self.bits = [bits_of(self.pat)[d] for d in self.dims]
        self.made = {}

    def copy(self, name, src, dst, pat):
        slot = len(self.made)
        made = pltpu.make_async_remote_copy(
            src_ref=src, dst_ref=dst, send_sem=self.send.at[self.part, slot], recv_sem=self.recv.at[self.part, slot],
            device_id=(self.y, pat), device_id_type=MESH)
        made.start()
        self.made[name] = made

    def fetch(self):
        self.fetched = pltpu.make_async_copy(
            self.src.at[self.part, pl.ds(self.own, 16)], self.mine.at[self.part], self.local.at[self.part])
        self.fetched.start()

    def swap(self, half):
        at = (1 - self.bits[0]) * 8 if half == 0 else self.bits[0] * 8
        self.copy(("swap", half), self.src.at[self.part, pl.ds(self.other + at, 8)],
                  self.came.at[self.part, half], partner_of(self.pat, "core"))

    def zero(self, u):
        p, b0, b1 = self.part, self.bits[0], self.bits[1]
        if u == 0:
            self.fetched.wait()
            self.made["swap", 0].wait_recv()
        group = (1 - b1) * 4 if u == 0 else b1 * 4

        @pl.loop(0, 4)
        def _(j):
            at = group + j
            total = self.mine[p, (1 - b0) * 8 + at].astype(F32) + self.came[p, 0, at].astype(F32)
            self.s0[p, u, j] = total.astype(BF)

        self.copy(("zero", u), self.s0.at[p, u], self.r0.at[p, u], partner_of(self.pat, self.dims[0]))

    def zero_kept(self):
        p, b0 = self.part, self.bits[0]
        self.made["swap", 1].wait_recv()

        @pl.loop(0, 8)
        def _(j):
            self.acc0[p, j] = self.mine[p, b0 * 8 + j].astype(F32) + self.came[p, 1, j].astype(F32)

    def one(self):
        p, b1 = self.part, self.bits[1]
        self.made["zero", 0].wait_recv()

        @pl.loop(0, 4)
        def _(j):
            self.s1[p, j] = (self.acc0[p, (1 - b1) * 4 + j] + self.r0[p, 0, j].astype(F32)).astype(BF)

        self.copy("one", self.s1.at[p], self.r1.at[p], partner_of(self.pat, self.dims[1]))

    def one_kept(self):
        p, b1 = self.part, self.bits[1]
        self.made["zero", 1].wait_recv()

        @pl.loop(0, 4)
        def _(j):
            self.acc1[p, j] = self.acc0[p, b1 * 4 + j] + self.r0[p, 1, j].astype(F32)

    def two(self):
        p, b2, b3 = self.part, self.bits[2], self.bits[3]
        self.made["one"].wait_recv()

        def total(flip2, flip3):
            at = (1 - b2 if flip2 else b2) * 2 + (1 - b3 if flip3 else b3)
            return self.acc1[p, at] + self.r1[p, at].astype(F32)

        d2, d3 = self.dims[2], self.dims[3]
        for k, (flip2, flip3, pat) in enumerate((
            (True, True, corner_of(self.pat, d2, d3)),
            (True, False, partner_of(self.pat, d2)),
            (False, True, partner_of(self.pat, d3)),
        )):
            self.s2[p, k] = total(flip2, flip3).astype(BF)
            self.copy(("two", k), self.s2.at[p, k], self.r2.at[p, k], pat)
        self.fin[p] = total(False, False)

    def total(self):
        for k in range(3):
            self.made["two", k].wait_recv()
        return self.fin[self.part] + sum(self.r2[self.part, k].astype(F32) for k in range(3))

    def finish(self):
        for made in self.made.values():
            made.wait_send()


HALVING_REFS = 14


def halving_scratch(parts, rows, columns):
    block = (rows, columns)
    return [
        pltpu.VMEM((parts, 16, *block), BF), pltpu.VMEM((parts, 2, 8, *block), BF),
        pltpu.VMEM((parts, 8, *block), F32), pltpu.VMEM((parts, 4, *block), F32),
        pltpu.VMEM((parts, 2, 4, *block), BF), pltpu.VMEM((parts, 2, 4, *block), BF),
        pltpu.VMEM((parts, 4, *block), BF), pltpu.VMEM((parts, 4, *block), BF),
        pltpu.VMEM((parts, 3, *block), BF), pltpu.VMEM((parts, 3, *block), BF),
        pltpu.VMEM((parts, *block), F32),
        pltpu.SemaphoreType.DMA((parts, 8)), pltpu.SemaphoreType.DMA((parts, 8)), pltpu.SemaphoreType.DMA((parts,)),
    ]


class Rings:
    def __init__(self, src, me, mine, local, came, keep, s1, r1, s2, r2, fin, pbuf, sems):
        self.src, self.came, self.keep, self.pbuf = src, came, keep, pbuf
        self.mine, self.local = mine, local
        self.s1, self.r1, self.s2, self.r2, self.fin = s1, r1, s2, r2, fin
        self.y, self.pat = me
        self.core = self.pat % 2
        self.sibling = partner_of(self.pat, "core")
        self.sems, self.made, self.used = sems, {}, 0
        x, z = (self.pat // 2) % 4, self.pat // 8
        self.at = ((x, z), (z, x))
        self.axes = (("x", "z"), ("z", "x"))

    def send(self, name, src, dst, pat):
        send, recv = self.sems
        made = pltpu.make_async_remote_copy(
            src_ref=src, dst_ref=dst, send_sem=send.at[self.used], recv_sem=recv.at[self.used],
            device_id=(self.y, pat), device_id_type=MESH)
        made.start()
        self.made[name] = made
        self.used += 1

    def swap(self):
        for h in range(2):
            self.send(("swap", h), self.src.at[h, pl.ds((1 - self.core) * 16, 16)], self.came.at[h], self.sibling)

    def fetch(self):
        self.fetched = pltpu.make_async_copy(self.src.at[:, pl.ds(self.core * 16, 16)], self.mine, self.local.at[0])
        self.fetched.start()

    def ring_one(self):
        self.fetched.wait()
        for h in range(2):
            self.made["swap", h].wait_recv()
            f = self.at[h][0]

            @pl.loop(0, 4)
            def _(j):
                at = f * 4 + j
                self.keep[h, j] = self.mine[h, at].astype(F32) + self.came[h, at].astype(F32)

            for k in (2, 1, 3):
                to = (f + k) % 4

                @pl.loop(0, 4)
                def _(j):
                    at = to * 4 + j
                    total = self.mine[h, at].astype(F32) + self.came[h, at].astype(F32)
                    self.s1[h, k - 1, j] = total.astype(BF)

                self.send(("one", h, k), self.s1.at[h, k - 1], self.r1.at[h, k - 1],
                          along(self.pat, self.axes[h][0], k))

    def ring_two(self):
        for h in range(2):
            for k in range(1, 4):
                self.made["one", h, k].wait_recv()
            g = self.at[h][1]

            def total(j):
                return self.keep[h, j] + sum(self.r1[h, k, j].astype(F32) for k in range(3))

            for k in (2, 1, 3):
                self.s2[h, k - 1] = total((g + k) % 4).astype(BF)
                self.send(("two", h, k), self.s2.at[h, k - 1], self.r2.at[h, k - 1],
                          along(self.pat, self.axes[h][1], k))
            self.fin[h] = total(g)

    def total(self, h):
        for k in range(1, 4):
            self.made["two", h, k].wait_recv()
        return self.fin[h] + sum(self.r2[h, k].astype(F32) for k in range(3))

    def gather_one(self, values):
        for h in range(2):
            place = ring_place(self.pat, h)
            self.pbuf[h, pl.ds(place, 1)] = values[h].reshape(1, 16, PX)
            mine = self.pbuf.at[h, pl.ds(place, 1)]
            for k in (2, 1, 3):
                self.send(("three", h, k), mine, mine, along(self.pat, self.axes[h][1], k))

    def gather_two(self):
        for h in range(2):
            for k in range(1, 4):
                self.made["three", h, k].wait_recv()
            mine = self.pbuf.at[h, pl.ds(self.core * 16 + self.at[h][0] * 4, 4)]
            for k in (2, 1, 3):
                self.send(("four", h, k), mine, mine, along(self.pat, self.axes[h][0], k))
            self.send(("near", h, 0), mine, mine, self.sibling)

    def gather_three(self):
        for k in (1, 3, 2):
            for h in range(2):
                self.made["four", h, k].wait_recv()
                came = self.pbuf.at[h, pl.ds(self.core * 16 + (self.at[h][0] + 4 - k) % 4 * 4, 4)]
                self.send(("near", h, k), came, came, self.sibling)

    def finish(self):
        for name, made in self.made.items():
            if name[0] == "near":
                made.wait_recv()
        for made in self.made.values():
            made.wait_send()


RING_SENDS = 2 + 4 * 6 + 8


def reduce_kernel(spots_ref, main_ref, spill_ref, sum_ref, probe_ref, join_hbm, obj_out, probe_out, *refs):
    y, pat = lax.axis_index("obj"), lax.axis_index("pat")
    me = (y, pat)
    rows = lax.axis_size("obj")
    mains = [Halving(main_ref, p, p, me, refs[:HALVING_REFS]) for p in range(3)]
    spills = [Halving(spill_ref, 0, 3, me, refs[HALVING_REFS:2 * HALVING_REFS])]
    (summine, rlocal, spill, spilled, ypro, came, keep, s1, r1, s2, r2, fin, pbuf, lit, acc, spill_acc, lights,
     spots, probe, join_ref, ysend, yrecv, psend, precv, lsem) = refs[2 * HALVING_REFS:]
    rings = Rings(sum_ref, me, summine, rlocal, came, keep, s1, r1, s2, r2, fin, pbuf, (psend, precv))
    light = Light(spots, probe, lit, acc, spill_acc, pat * OWN)
    objs = spills + mains
    rings.fetch()
    for part in objs:
        part.fetch()
    loads = [pltpu.make_async_copy(src, dst, lsem.at[k]) for k, (src, dst) in enumerate(
        ((probe_ref, probe), (spots_ref, spots), (join_hbm, join_ref)))]
    for made in loads:
        made.start()
    others = [((y + k) % rows, pat) for k in (1, 2, 3)]
    near = [(y, along(pat, axis, k)) for axis in ("x", "z") for k in (1, 2, 3)]
    greet(others + near + [(y, partner_of(pat, "core"))] + [(y, corner_of(pat, *c)) for c in CORNERS])
    rings.swap()
    for half in range(2):
        for part in objs:
            part.swap(half)
    rings.ring_one()
    for part in objs:
        part.zero(0)
    for made in loads:
        made.wait()
    light.prepare()
    rings.ring_two()
    for part in objs:
        part.zero(1)
    for part in objs:
        part.zero_kept()
    for part in objs:
        part.one()
    for h in range(2):
        ypro[pl.ds(y, 1), :, h * PX:(h + 1) * PX] = rings.total(h).reshape(1, 16, PX)
    mine = ypro.at[pl.ds(y, 1)]
    across = []
    for k, other in enumerate(others):
        across.append(pltpu.make_async_remote_copy(
            src_ref=mine, dst_ref=mine, send_sem=ysend.at[k], recv_sem=yrecv.at[k],
            device_id=other, device_id_type=MESH))
        across[-1].start()
    light.add(0, 16)
    for made in across:
        made.wait_recv()
    total = (ypro[0] + ypro[1] + ypro[2] + ypro[3]).astype(BF)
    joined = [dot(total[:, c * 256:(c + 1) * 256], join_ref[...]).astype(BF) for c in range(4)]
    rings.gather_one([jnp.concatenate(joined[2 * h:2 * h + 2], axis=1) for h in range(2)])
    for part in objs:
        part.one_kept()
    for part in objs:
        part.two()
    light.add(16, 24)
    rings.gather_two()
    spill[...] = spills[0].total()
    over = pltpu.make_async_remote_copy(
        src_ref=spill, dst_ref=spilled, send_sem=ysend.at[3], recv_sem=yrecv.at[3],
        device_id=others[0], device_id_type=MESH)
    over.start()
    light.add(24, 32)
    rings.gather_three()
    light.result(y, lights)
    totals = [part.total() for part in mains]
    over.wait_recv()
    chunks = []
    for c in range(4):
        whole = jnp.concatenate([total[:, c * 256:(c + 1) * 256] for total in totals], axis=0)
        chunks.append(whole + jnp.where(y == 0, 0.0, spilled[...]) if c == 0 else whole)
    joined = moved(jnp.concatenate(chunks, axis=0), join_ref[...])
    for j in range(8):
        here = joined[j // 2 * 48:(j // 2 + 1) * 48, (j % 2) * 128:(j % 2 + 1) * 128]
        under = lights[j] + 1.0
        for layer in range(2):
            obj_out[layer * OWN:(layer + 1) * OWN, j * 128:(j + 1) * 128] = here[layer * OWN:(layer + 1) * OWN] / under
    rings.finish()
    store = pltpu.make_async_copy(pbuf, probe_out, lsem.at[3])
    store.start()
    for part in objs:
        part.finish()
    for made in across + [over]:
        made.wait_send()
    store.wait()


def reduce_all(spots, main, spill, sums, probe, join):
    dma = pltpu.SemaphoreType.DMA
    vmem = pltpu.VMEM
    return pl.pallas_call(
        reduce_kernel,
        out_shape=[jax.ShapeDtypeStruct((48, TW), F32), jax.ShapeDtypeStruct((2, 32, 16, PX), BF)],
        in_specs=[HBM] * 6,
        out_specs=[VMEM, HBM],
        scratch_shapes=[
            *halving_scratch(3, 16, TW), *halving_scratch(1, 48, HALO),
            vmem((2, 16, 16, PX), BF), dma((1,)),
            vmem((48, HALO), F32), vmem((48, HALO), F32), vmem((4, 16, TW), F32),
            vmem((2, 16, 16, PX), BF), vmem((2, 4, 16, PX), F32),
            vmem((2, 3, 4, 16, PX), BF), vmem((2, 3, 4, 16, PX), BF),
            vmem((2, 3, 16, PX), BF), vmem((2, 3, 16, PX), BF),
            vmem((2, 16, PX), F32), vmem((2, 32, 16, PX), BF),
            vmem((6, PX + 2 * OWN + 8, 128), F32), vmem((3, 8, 8, 128), F32), vmem((3, 2, 8, 128), F32),
            vmem((8, OWN, 128), F32),
            pltpu.SMEM((1, 32, 8, 128), jnp.int32), vmem((2, PX, PX), F32), vmem((256, 256), BF),
            dma((4,)), dma((4,)), dma((RING_SENDS,)), dma((RING_SENDS,)), dma((4,)),
        ],
        compiler_params=pltpu.CompilerParams(
            collective_id=1, has_side_effects=True, vmem_limit_bytes=62 * MB),
        cost_estimate=pl.CostEstimate(flops=0, bytes_accessed=60 * MB, transcendentals=0),
        name="reduce_all",
    )(spots, main, spill, sums, probe, join)


def finish_kernel(scale, own_ref, gathered_ref, obj_out, probe_out, own, gathered, probe, sems):
    loads = [pltpu.make_async_copy(gathered_ref.at[h], gathered.at[h], sems.at[h]) for h in range(2)]
    loads.append(pltpu.make_async_copy(own_ref, own, sems.at[2]))
    for made in loads:
        made.start()
    stores = []
    for h in range(2):
        loads[h].wait()
        for o in range(32):
            probe[h, o * 16:(o + 1) * 16] = gathered[h, ring_place(o, h)].astype(F32) * scale
            if o % 16 == 15:
                rows = pl.ds(o // 16 * 256, 256)
                stores.append(pltpu.make_async_copy(
                    probe.at[h, rows], probe_out.at[h, rows], sems.at[3 + 2 * h + o // 16]))
                stores[-1].start()
    loads[2].wait()
    stores.append(pltpu.make_async_copy(own, obj_out, sems.at[7]))
    stores[-1].start()
    for made in stores:
        made.wait()


def finish(scale, own, gathered):
    return pl.pallas_call(
        functools.partial(finish_kernel, scale),
        out_shape=[jax.ShapeDtypeStruct((48, TW), F32), jax.ShapeDtypeStruct((2, PX, PX), F32)],
        in_specs=[HBM] * 2,
        out_specs=[HBM] * 2,
        scratch_shapes=[
            pltpu.VMEM((48, TW), F32), pltpu.VMEM((2, 32, 16, PX), BF), pltpu.VMEM((2, PX, PX), F32),
            pltpu.SemaphoreType.DMA((8,)),
        ],
        compiler_params=pltpu.CompilerParams(vmem_limit_bytes=62 * MB),
        name="finish",
    )(own, gathered)


def local(obj, probe, amps, rows, cols):
    total = rows.shape[0] * lax.axis_size("obj") * lax.axis_size("pat")
    split = splitter()
    main, halo, spots = gather(obj, rows, cols, jnp.asarray(split))
    sums = work(rows, cols, main, halo, probe, amps, jnp.asarray(split))
    own, gathered = reduce_all(spots, *sums, probe, jnp.asarray(split.T))
    own, probe_grad = finish(1.0 / math.sqrt(total), own, gathered)
    obj_step = own.reshape(2, OWN, TW)
    return (obj_step, probe_grad)


def solution(mesh):
    placed = (
        P(None, "pat", "obj"),
        P(),
        P(("obj", "pat"), None, None),
        P(("obj", "pat")),
        P(("obj", "pat")),
    )
    return jax.shard_map(
        local, mesh=mesh, in_specs=placed, out_specs=(P(None, "pat", "obj"), P()), check_vma=False
    )
```
